256 devices in a mesh: fsdp: 32 (over z, y_hi, core), ctx: 8 (over y_lo, x).
Axes of the slice: x: 4, y: 4 (y_hi: 2, y_lo: 2; y = y_hi * 2 + y_lo), z: 8, core: 2. Of those that a mesh axis runs over, the one named last changes fastest.
Arguments:
- inputs: bfloat16 [32, 1024, 2560], P('fsdp', 'ctx'), may hold values from -6 to 6
- queries: bfloat16 [32, 1024, 4096], P('fsdp', 'ctx')
- keys: bfloat16 [32, 1024, 512], P('fsdp', 'ctx')
- values: bfloat16 [32, 1024, 512], P('fsdp', 'ctx'), may hold values from -6 to 6
- output_cotangent: bfloat16 [32, 1024, 4096], P('fsdp', 'ctx'), may hold values from -6 to 6
- key_value_weight: bfloat16 [2560, 1024], P('fsdp'), may hold values from -0.1875 to 0.1875
- doc_ids: int32 [32, 32], P('fsdp'), may hold values from 0 to 7, never falling along the last dimension, each value on 1 to 16 neighbouring positions
- block_order: int32 [32], replicated, may hold values from 0 to 31, each once
Outputs:
- input_grad: bfloat16 [32, 1024, 2560], P('fsdp', 'ctx')
- query_grad: bfloat16 [32, 1024, 4096], P('fsdp', 'ctx')
- kv_grad: bfloat16 [32, 1024, 1024], P('fsdp', 'ctx')
- weight_grad: float32 [2560, 1024], P(('fsdp', 'ctx'))
The draws below stay inside these ranges and needn't reach their ends.
Inputs may be any that keep to these rules, and one draw needn't show every extreme that they name: `doc_ids`: each slab's document numbers are 0 to 7 in sequence order, never falling; every document covers 1 to 16 blocks and one covers exactly 16. `block_order`: each sequence block is held by exactly one stored block.
All inputs are finite; a program needn't handle non-finite values.
Results may differ from the reference program's by a relative error of at most 0.015.
Values may be sent and summed in bfloat16 or wider, within the bound.
No kernel may reach another device: no remote copies, remote signals or barrier semaphores. Data moves between devices by JAX's collectives and lax.ppermute only.
A program may use at most 128 MiB of HBM per device.

```python
import math
import jax
import jax.numpy as jnp
import numpy as np
from jax import lax

INPUT_FEATURES = 2560
HQ = 32
KEY_VALUE_HEADS = 4
HEAD_WIDTH = 128
BLK = 32
QUERY_PER_KEY = 8
SLAB_ROWS = 1024
NB = 32
SLAB_COUNT = 32
DOCS = 8
DOC_MOST = 16


def lifted_keys(key, lift):
    array_dims = (SLAB_COUNT, SLAB_ROWS, KEY_VALUE_HEADS * HEAD_WIDTH)
    base = jnp.clip(jax.random.normal(key, array_dims, jnp.float32), -5.0, 5.0)
    raw = jax.random.bernoulli(jax.random.fold_in(key, 11), 1.0 / 32.0, (SLAB_COUNT, SLAB_ROWS))
    inner = jnp.arange(SLAB_ROWS) % BLK != 0
    chosen = raw & inner[None, :] & jnp.logical_not(jnp.roll(raw, -1, axis=1))
    following = jnp.roll(chosen, -1, axis=1)
    near = jnp.where(following[..., None], 0.99 * jnp.roll(base, -1, axis=1), base)
    key_result = jnp.where(lift > 0.0, near, base)
    strengths = jnp.array([10.0, 16.0, 22.0], jnp.float32)
    level = strengths[jax.random.randint(jax.random.fold_in(key, 12), (SLAB_COUNT, SLAB_ROWS), 0, 3)]
    return (key_result, chosen, level)


def draw_keys(key, part):
    lift = 0.0
    key_result, chosen, level = lifted_keys(key, lift)
    return key_result.astype(jnp.bfloat16)


def draw_queries(key, part):
    lift = 0.0
    key_result, chosen, level = lifted_keys(key, lift)
    key = jax.random.fold_in(key, 5)
    base = jnp.clip(jax.random.normal(key, (SLAB_COUNT, SLAB_ROWS, HQ * HEAD_WIDTH), jnp.float32), -5.0, 5.0)
    head_expand = jnp.broadcast_to(key_result.reshape(SLAB_COUNT, SLAB_ROWS, KEY_VALUE_HEADS, 1, HEAD_WIDTH), (SLAB_COUNT, SLAB_ROWS, KEY_VALUE_HEADS, QUERY_PER_KEY, HEAD_WIDTH))
    aligned = level[..., None] * head_expand.reshape(SLAB_COUNT, SLAB_ROWS, HQ * HEAD_WIDTH)
    picked = chosen & (lift > 0.0)
    return jnp.where(picked[..., None], aligned, base).astype(jnp.bfloat16)


def strengthened(values, own_key, source, target, blocks, factor):
    owner, partner = [(jnp.arange(values.shape[dim]) // (values.shape[dim] // blocks)).reshape([-1 if axis == dim else 1 for axis in range(values.ndim)]) for dim in (source, target)]
    chosen = jax.random.permutation(own_key, blocks)[partner]
    strong = (owner == chosen) | (owner == (partner + blocks // 2) % blocks)
    return jnp.where(strong, factor * values, values)


def shard_levels(own_key, shape, pieces, least, top_value):
    loudness, own = 1.0, jax.random.fold_in(own_key, 6)
    for axis_at, shards_of in pieces:
        steps = jnp.exp(jax.random.uniform(jax.random.fold_in(own, axis_at), (shards_of,), jnp.float32, least / len(pieces), top_value / len(pieces)))
        loudness = loudness * jnp.repeat(steps, shape[axis_at] // shards_of).reshape([-1 if axis == axis_at else 1 for axis in range(len(shape))])
    return loudness


def split_up(amount, total, bound, skew):
    portions = [(1 << 20) // math.isqrt(rank ** skew) + 1 for rank in range(2, amount + 1)]
    surplus, counts = total - bound - (amount - 1), [1] * (amount - 1)
    while surplus > 0:
        movable = [i for i in range(amount - 1) if counts[i] < bound]
        whole, remaining = sum([portions[i] for i in movable]), surplus
        for i in movable:
            more = min(bound - counts[i], max(1, remaining * portions[i] // whole), surplus)
            counts[i] = counts[i] + more
            surplus = surplus - more
    return np.array([bound] + counts)


def uneven_parts(own_key, amount, total, most, skew):
    if amount == 2:
        one = jax.random.randint(own_key, (), max(1, total - most), min(most, total - 1) + 1)
        return jnp.stack([one, total - one])
    lengths = jnp.asarray(split_up(amount, total, most, skew), jnp.int32)
    pairs = (amount - 1) // 2
    donor, taker = lengths[1:1 + 2 * pairs:2], lengths[2:2 + 2 * pairs:2]
    slack = jnp.minimum(donor - 1, most - taker)
    shifted = jax.random.randint(jax.random.fold_in(own_key, 1), (pairs,), 0, 1 << 20) % (slack + 1)
    lengths = lengths.at[1:1 + 2 * pairs:2].set(donor - shifted).at[2:2 + 2 * pairs:2].set(taker + shifted)
    return lengths[jax.random.permutation(jax.random.fold_in(own_key, 2), amount)]


def noise(rng, dims, scale, most, split=(), kind=jnp.bfloat16):
    drawn = scale * jax.random.normal(rng, dims, jnp.float32)
    if split:
        drawn = drawn * shard_levels(rng, dims, split, -0.22, 0.18)
    return jnp.clip(drawn, -most, most).astype(kind)


def noise_with(stream_key, shape, width, limit, shards, heavy, kind=jnp.bfloat16):
    result = width * jax.random.normal(stream_key, shape, jnp.float32)
    if shards:
        result = result * shard_levels(stream_key, shape, shards, -0.22, 0.18)
    return jnp.clip(strengthened(result, jax.random.fold_in(stream_key, 3), *heavy), -limit, limit).astype(kind)


def setup_inputs(seed: int = 0) -> dict:
    splits = jax.random.split(jax.random.key(seed), 9)
    inputs = noise_with(splits[0], (SLAB_COUNT, SLAB_ROWS, INPUT_FEATURES), 1.0, 6.0, ((0, 32), (1, 8)), (1, 2, 8, 2.0))
    queries = draw_queries(jax.random.fold_in(splits[8], 71), 0)
    keys = draw_keys(jax.random.fold_in(splits[8], 71), 0)
    values = noise(splits[3], (SLAB_COUNT, SLAB_ROWS, KEY_VALUE_HEADS * HEAD_WIDTH), 1.0, 6.0, ((0, 32), (1, 8)))
    output_cotangent = noise(splits[4], (SLAB_COUNT, SLAB_ROWS, HQ * HEAD_WIDTH), 1.0, 6.0, ((0, 32), (1, 8)))
    key_value_weight = noise(splits[5], (INPUT_FEATURES, 2 * KEY_VALUE_HEADS * HEAD_WIDTH), (2 * KEY_VALUE_HEADS * HEAD_WIDTH) ** -0.5, 0.1875, ((0, 32),))
    doc_ids = jax.vmap(lambda own: jnp.searchsorted(jnp.cumsum(uneven_parts(own, DOCS, NB, DOC_MOST, 2)), jnp.arange(NB), side="right"))(jax.random.split(splits[6], SLAB_COUNT)).reshape((SLAB_COUNT, NB)).astype(jnp.int32)
    block_order = jax.random.permutation(splits[7], NB).astype(jnp.int32)
    return {"inputs": inputs, "queries": queries, "keys": keys, "values": values, "output_cotangent": output_cotangent, "key_value_weight": key_value_weight, "doc_ids": doc_ids, "block_order": block_order}


def locate(order, docs):
    stored = jnp.arange(SLAB_ROWS, dtype=jnp.int32)
    seq_block = order[stored // BLK]
    position = seq_block * BLK + stored % BLK
    document = docs[seq_block]
    return (position, document)

def slab_grads(inputs, queries, keys, values, output_cotangent, key_value_weight, docs, order):
    position, document = locate(order, docs)
    visible = (position[None, :] <= position[:, None]) & (document[None, :] == document[:, None])
    score_scale = 1.0 / math.sqrt(HEAD_WIDTH)
    heads_of_query = queries.astype(jnp.float32).reshape(SLAB_ROWS, KEY_VALUE_HEADS, QUERY_PER_KEY, HEAD_WIDTH).transpose(1, 2, 0, 3)
    output_grad_heads = output_cotangent.astype(jnp.float32).reshape(SLAB_ROWS, KEY_VALUE_HEADS, QUERY_PER_KEY, HEAD_WIDTH).transpose(1, 2, 0, 3)
    heads_of_key = keys.astype(jnp.float32).reshape(SLAB_ROWS, KEY_VALUE_HEADS, HEAD_WIDTH).transpose(1, 0, 2)
    heads_of_value = values.astype(jnp.float32).reshape(SLAB_ROWS, KEY_VALUE_HEADS, HEAD_WIDTH).transpose(1, 0, 2)

    def per_head(head_items):
        query_h, dout_h, key_h, value_h = head_items
        scores = jnp.einsum('gtd,kd->gtk', query_h, key_h) * score_scale
        masked = jnp.where(visible[None], scores, -jnp.inf)
        row_max = lax.optimization_barrier(jnp.max(masked, axis=2, keepdims=True))
        summed = lax.optimization_barrier(jnp.sum(jnp.where(visible[None], jnp.exp(masked - row_max), 0.0), axis=2, keepdims=True))
        log_total = row_max + jnp.log(summed)
        probs = jnp.where(visible[None], jnp.exp(scores - log_total), 0.0)
        products = jnp.einsum('gtd,kd->gtk', dout_h, value_h)
        row_delta = lax.optimization_barrier(jnp.sum(probs * products, axis=2, keepdims=True))
        score_grad = lax.optimization_barrier((probs * (products - row_delta)).astype(jnp.bfloat16)).astype(jnp.float32)
        probs_low = lax.optimization_barrier(probs.astype(jnp.bfloat16)).astype(jnp.float32)
        query_part = jnp.einsum('gtk,kd->gtd', score_grad, key_h) * score_scale
        key_part = jnp.einsum('gtk,gtd->kd', score_grad, query_h) * score_scale
        value_part = jnp.einsum('gtk,gtd->kd', probs_low, dout_h)
        return (query_part, key_part, value_part)
    query_parts, key_pieces, value_pieces = lax.map(per_head, (heads_of_query, output_grad_heads, heads_of_key, heads_of_value))
    query_grad = query_parts.transpose(2, 0, 1, 3).reshape(SLAB_ROWS, HQ * HEAD_WIDTH).astype(jnp.bfloat16)
    key_row_block = key_pieces.transpose(1, 0, 2).reshape(SLAB_ROWS, KEY_VALUE_HEADS * HEAD_WIDTH)
    value_row_block = value_pieces.transpose(1, 0, 2).reshape(SLAB_ROWS, KEY_VALUE_HEADS * HEAD_WIDTH)
    kv_grad = jnp.concatenate([key_row_block, value_row_block], axis=1).astype(jnp.bfloat16)
    input_grad = jnp.dot(kv_grad, key_value_weight.T, preferred_element_type=jnp.float32).astype(jnp.bfloat16)
    weight_term = jnp.dot(inputs.T, kv_grad, preferred_element_type=jnp.float32)
    return (input_grad, query_grad, kv_grad, weight_term)

def reference(inputs, queries, keys, values, output_cotangent, key_value_weight, doc_ids, block_order):

    def per_slab(grad_total, slab_items):
        slab_in, slab_q, slab_k, slab_v, slab_d, slab_docs = slab_items
        input_grad, query_grad, kv_grad, weight_term = slab_grads(slab_in, slab_q, slab_k, slab_v, slab_d, key_value_weight, slab_docs, block_order)
        return (grad_total + weight_term, (input_grad, query_grad, kv_grad))
    initial_total = jnp.zeros((INPUT_FEATURES, 2 * KEY_VALUE_HEADS * HEAD_WIDTH), jnp.float32)
    grad_total, outputs = lax.scan(per_slab, initial_total, (inputs, queries, keys, values, output_cotangent, doc_ids))
    input_grad, query_grad, kv_grad = outputs
    return (input_grad, query_grad, kv_grad, grad_total)
```

```python
import functools
import math

import jax
import jax.numpy as jnp
from jax import lax
from jax.experimental import pallas as pl
from jax.experimental.pallas import tpu as pltpu
from jax.sharding import PartitionSpec as P

HQ = 32
KEY_VALUE_HEADS = 4
HEAD_WIDTH = 128
BLK = 32
QUERY_PER_KEY = 8

CTX = 8
FSDP = 32
ROWS = 128
SLAB = 1024
FEATURES = 2560
FEAT_TILE = FEATURES // CTX
Q_COLS = 512
PACK_COLS = 2 * Q_COLS + 2 * HEAD_WIDTH
HALF = 512
SCALE = 1.0 / math.sqrt(HEAD_WIDTH)
LOG2E = math.log2(math.e)
LOWEST = -1e30
NN = (((1,), (0,)), ((), ()))
NT = (((1,), (1,)), ((), ()))
VMEM = pl.BlockSpec(memory_space=pltpu.VMEM)
SMEM = pl.BlockSpec(memory_space=pltpu.SMEM)
VMEM_LIMIT = 48 * 1024 * 1024


def dot(a, b, dims):
    return lax.dot_general(a, b, dims, preferred_element_type=jnp.float32)


def shape(dims, kind=jnp.bfloat16):
    return jax.ShapeDtypeStruct(dims, kind)


def params():
    return pltpu.CompilerParams(vmem_limit_bytes=VMEM_LIMIT)


def cost(flops, moved):
    return pl.CostEstimate(flops=flops, bytes_accessed=moved, transcendentals=0)


def pack_kernel(c_ref, q_ref, d_ref, k_ref, v_ref, *outs):
    c = c_ref[0]
    for s in range(CTX):
        dest = lax.rem(c + s, CTX)
        cols = pl.ds(pl.multiple_of(dest * Q_COLS, Q_COLS), Q_COLS)
        head = pl.ds(pl.multiple_of((dest // 2) * HEAD_WIDTH, HEAD_WIDTH), HEAD_WIDTH)
        outs[s][:, 0:Q_COLS] = q_ref[:, cols]
        outs[s][:, Q_COLS : 2 * Q_COLS] = d_ref[:, cols]
        outs[s][:, 2 * Q_COLS : 2 * Q_COLS + HEAD_WIDTH] = k_ref[:, head]
        outs[s][:, 2 * Q_COLS + HEAD_WIDTH :] = v_ref[:, head]


def turn_kernel(c_ref, x_ref, *refs):
    outs, turned = refs[:CTX], refs[CTX]
    c = c_ref[0]
    for j in range(FEATURES // 128):
        turned[j * 128 : (j + 1) * 128, :] = x_ref[:, j * 128 : (j + 1) * 128].T
    for s in range(CTX):
        dest = lax.rem(c + s, CTX)
        outs[s][...] = turned[pl.ds(pl.multiple_of(dest * FEAT_TILE, FEAT_TILE), FEAT_TILE), :]


def attention_kernel(c_ref, docs_ref, order_ref, *refs):
    ins = refs[0:CTX]
    dq_outs = refs[CTX : 2 * CTX]
    keep_ref, send_ref = refs[2 * CTX : 2 * CTX + 2]
    q_s, d_s, k_s, v_s, kt_s, dq_s, dkv_s, place, begin = refs[2 * CTX + 2 :]
    c = c_ref[0]

    first = lax.fori_loop(
        0, 17, lambda i, a: jnp.where(docs_ref[i] == docs_ref[i + 15], i, a), jnp.int32(0)
    )

    def place_block(st, carry):
        b = order_ref[st]
        inside = (b >= first) & (b < first + 16)
        place[st] = jnp.where(inside, b - first, jnp.where(b < first, b + 16, b))
        return carry

    lax.fori_loop(0, 32, place_block, 0)

    def begin_block(t, carry):
        last_doc, last_begin = carry
        doc = docs_ref[jnp.where(t < first, t, t + 16)]
        now = jnp.where(doc == last_doc, last_begin, t)
        begin[t] = jnp.int32(0)
        begin[t + 16] = now * BLK
        return doc, now

    lax.fori_loop(0, 16, begin_block, (jnp.int32(-1), jnp.int32(0)))

    for s in range(CTX):
        src = lax.rem(c + CTX - s, CTX)
        for k in range(4):
            rows = pl.ds(pl.multiple_of(place[src * 4 + k] * BLK, BLK), BLK)
            block = slice(k * BLK, (k + 1) * BLK)
            q_s[rows, :] = ins[s][block, 0:Q_COLS]
            d_s[rows, :] = ins[s][block, Q_COLS : 2 * Q_COLS]
            k_s[rows, :] = ins[s][block, 2 * Q_COLS : 2 * Q_COLS + HEAD_WIDTH]
            v_s[rows, :] = ins[s][block, 2 * Q_COLS + HEAD_WIDTH :]
    for j in range(SLAB // 128):
        kt_s[:, j * 128 : (j + 1) * 128] = k_s[j * 128 : (j + 1) * 128, :].T
    dkv_s[...] = jnp.zeros_like(dkv_s)

    def half(hf, carry):
        base = pl.multiple_of(hf * HALF, HALF)
        for i in range(HALF // 128):
            n = (i + 1) * 128
            rows = pl.ds(pl.multiple_of(base + i * 128, 128), 128)
            keys = pl.ds(base, n)
            key_n = k_s[keys, :]
            value_n = v_s[keys, :]
            lane = lax.broadcasted_iota(jnp.int32, (n, 128), 1)
            row = lax.broadcasted_iota(jnp.int32, (n, 128), 0)
            low = jnp.zeros((n, 128), jnp.int32)
            for kk in range(4):
                low = jnp.where(lane // BLK == kk, begin[hf * 16 + i * 4 + kk], low)
            seen = (row >= low) & (row <= lane + i * 128)
            bias = jnp.where(seen, 0.0, LOWEST)
            bias = jnp.concatenate([bias, bias], axis=1)
            for g in range(2):
                cols = [slice((2 * g + e) * 128, (2 * g + e + 1) * 128) for e in range(2)]
                qs = jnp.concatenate([q_s[rows, e] for e in cols], axis=0)
                ds = jnp.concatenate([d_s[rows, e] for e in cols], axis=0)
                scores = dot(key_n, qs, NT) * (SCALE * LOG2E) + bias
                top = jnp.max(scores, axis=0, keepdims=True)
                probs = jnp.exp2(scores - top)
                total = jnp.sum(probs, axis=0, keepdims=True)
                probs = probs * (1.0 / total)
                products = dot(value_n, ds, NT)
                delta = jnp.sum(probs * products, axis=0, keepdims=True)
                score_grad = (probs * (products - delta)).astype(jnp.bfloat16)
                probs_low = probs.astype(jnp.bfloat16)
                dkv_s[keys, 0:128] += dot(score_grad, qs, NN)
                dkv_s[keys, 128:256] += dot(probs_low, ds, NN)
                dqt = dot(kt_s[:, keys], score_grad, NN) * SCALE
                for e in range(2):
                    dq_s[rows, cols[e]] = dqt[:, e * 128 : (e + 1) * 128].T.astype(jnp.bfloat16)
        return carry

    lax.fori_loop(0, 2, half, 0)

    odd = lax.rem(c, 2)
    own = pl.ds(pl.multiple_of(odd * 128, 128), 128)
    other = pl.ds(pl.multiple_of((1 - odd) * 128, 128), 128)
    own_scale = jnp.where(odd == 0, SCALE, 1.0)
    other_scale = jnp.where(odd == 0, 1.0, SCALE)
    for st in range(32):
        rows = pl.ds(pl.multiple_of(place[st] * BLK, BLK), BLK)
        block = slice(st * BLK, (st + 1) * BLK)
        keep_ref[block, :] = dkv_s[rows, own] * own_scale
        send_ref[block, :] = (dkv_s[rows, other] * other_scale).astype(jnp.bfloat16)
    for s in range(CTX):
        dest = lax.rem(c + s, CTX)
        for k in range(4):
            rows = pl.ds(pl.multiple_of(place[dest * 4 + k] * BLK, BLK), BLK)
            dq_outs[s][k * BLK : (k + 1) * BLK, :] = dq_s[rows, :]


def weight_kernel(at_ref, *refs):
    pieces, xs = refs[0:CTX], refs[CTX : 2 * CTX]
    kv_ref, keep_ref, send_ref, x_s = refs[2 * CTX :]
    c, core = at_ref[0], at_ref[1]
    for s in range(CTX):
        src = lax.rem(c + CTX - s, CTX)
        block = src // 2 + KEY_VALUE_HEADS * lax.rem(src, 2)
        kv_ref[:, pl.ds(pl.multiple_of(block * 128, 128), 128)] = pieces[s][...]
        x_s[:, pl.ds(pl.multiple_of(src * 128, 128), 128)] = xs[s][...]
    part = FEAT_TILE // 2
    other = pl.ds(pl.multiple_of((1 - core) * part, part), part)
    own = pl.ds(pl.multiple_of(core * part, part), part)
    for j in range(4):
        cols = slice(j * 256, (j + 1) * 256)
        send_ref[:, cols] = dot(x_s[other, :], kv_ref[:, cols], NN).astype(jnp.bfloat16)
        keep_ref[:, cols] = dot(x_s[own, :], kv_ref[:, cols], NN)


def input_kernel(c_ref, kv_ref, w_ref, kv_rows_ref, *refs):
    outs, tile = refs[:CTX], refs[CTX]
    c = c_ref[0]
    for j in range(4):
        rows = slice(j * 256, (j + 1) * 256)
        tile[:, rows] = dot(w_ref[...], kv_ref[rows, :], NT).astype(jnp.bfloat16)
    for s in range(CTX):
        dest = lax.rem(c + s, CTX)
        outs[s][...] = tile[:, pl.ds(pl.multiple_of(dest * 128, 128), 128)]
    kv_rows_ref[...] = kv_ref[pl.ds(pl.multiple_of(c * ROWS, ROWS), ROWS), :]


def input_out_kernel(c_ref, *refs):
    pieces, out_ref, tile = refs[:CTX], refs[CTX], refs[CTX + 1]
    c = c_ref[0]
    for s in range(CTX):
        src = lax.rem(c + CTX - s, CTX)
        tile[pl.ds(pl.multiple_of(src * FEAT_TILE, FEAT_TILE), FEAT_TILE), :] = pieces[s][...]
    for j in range(FEATURES // 128):
        out_ref[:, j * 128 : (j + 1) * 128] = tile[j * 128 : (j + 1) * 128, :].T


def chunk_kernel(z_ref, keep_ref, got_ref, *refs):
    outs, parts = refs[:CTX], refs[CTX]
    total = keep_ref[...] + got_ref[...].astype(jnp.float32)
    for j in range(8):
        parts[j] = total[j * 10 : (j + 1) * 10, :]
    for s in range(8):
        outs[s][...] = parts[lax.rem(z_ref[0] + s, 8)].astype(jnp.bfloat16)


def to_shift(value, s):
    if s == 0:
        return value
    return lax.ppermute(value, "ctx", [(i, (i + s) % CTX) for i in range(CTX)])


def body(inputs, queries, keys, values, output_cotangent, key_value_weight, doc_ids, block_order):
    c = lax.axis_index("ctx").astype(jnp.int32)
    f = lax.axis_index("fsdp").astype(jnp.int32)
    z, y_hi, core = f // 4, (f // 2) % 2, f % 2
    c_at = c.reshape(1)

    packed = pl.pallas_call(
        pack_kernel,
        in_specs=[SMEM] + [VMEM] * 4,
        out_specs=[VMEM] * CTX,
        out_shape=[shape((ROWS, PACK_COLS))] * CTX,
        compiler_params=params(),
        cost_estimate=cost(0, 5_000_000),
    )(c_at, queries[0], output_cotangent[0], keys[0], values[0])
    got = [to_shift(packed[s], s) for s in range(CTX)]

    own_rows = lax.dynamic_slice_in_dim(key_value_weight, c * 10, 10, 0)
    perm = [(f1 * CTX + c1, ((f1 * CTX + c1) % FSDP) * CTX + (f1 * CTX + c1) // FSDP)
            for f1 in range(FSDP) for c1 in range(CTX)]
    own_rows = lax.ppermute(own_rows, ("fsdp", "ctx"), perm)
    weight_tile = lax.all_gather(own_rows.reshape(80, 128), "fsdp", axis=0, tiled=True)
    weight_tile = weight_tile.reshape(FEAT_TILE, 1024)

    turned = pl.pallas_call(
        turn_kernel,
        in_specs=[SMEM, VMEM],
        out_specs=[VMEM] * CTX,
        out_shape=[shape((FEAT_TILE, ROWS))] * CTX,
        scratch_shapes=[pltpu.VMEM((FEATURES, ROWS), jnp.bfloat16)],
        compiler_params=params(),
        cost_estimate=cost(0, 1_300_000),
    )(c_at, inputs[0])
    got_x = [to_shift(turned[s], s) for s in range(CTX)]

    results = pl.pallas_call(
        attention_kernel,
        in_specs=[SMEM] * 3 + [VMEM] * CTX,
        out_specs=[VMEM] * (CTX + 2),
        out_shape=[shape((ROWS, Q_COLS))] * CTX
        + [shape((SLAB, HEAD_WIDTH), jnp.float32), shape((SLAB, HEAD_WIDTH))],
        scratch_shapes=[
            pltpu.VMEM((SLAB, Q_COLS), jnp.bfloat16),
            pltpu.VMEM((SLAB, Q_COLS), jnp.bfloat16),
            pltpu.VMEM((SLAB, HEAD_WIDTH), jnp.bfloat16),
            pltpu.VMEM((SLAB, HEAD_WIDTH), jnp.bfloat16),
            pltpu.VMEM((HEAD_WIDTH, SLAB), jnp.bfloat16),
            pltpu.VMEM((SLAB, Q_COLS), jnp.bfloat16),
            pltpu.VMEM((SLAB, 2 * HEAD_WIDTH), jnp.float32),
            pltpu.SMEM((32,), jnp.int32),
            pltpu.SMEM((32,), jnp.int32),
        ],
        compiler_params=params(),
        cost_estimate=cost(2_000_000_000, 5_000_000),
    )(c_at, doc_ids[0], block_order, *got)
    dq_parts, keep, send = results[:CTX], results[CTX], results[CTX + 1]

    taken = lax.ppermute(send, "ctx", [(i, i ^ 1) for i in range(CTX)])
    own_cols = (keep + taken.astype(jnp.float32)).astype(jnp.bfloat16)
    pieces = [to_shift(own_cols, s) for s in range(CTX)]

    kv_all, wg_keep, wg_send = pl.pallas_call(
        weight_kernel,
        in_specs=[SMEM] + [VMEM] * (2 * CTX),
        out_specs=[VMEM] * 3,
        out_shape=[
            shape((SLAB, 1024)),
            shape((FEAT_TILE // 2, 1024), jnp.float32),
            shape((FEAT_TILE // 2, 1024)),
        ],
        scratch_shapes=[pltpu.VMEM((FEAT_TILE, SLAB), jnp.bfloat16)],
        compiler_params=params(),
        cost_estimate=cost(700_000_000, 5_000_000),
    )(jnp.stack([c, core]), *pieces, *got_x)

    wg_got = lax.ppermute(wg_send, "fsdp", [(i, i ^ 1) for i in range(FSDP)])

    ig_results = pl.pallas_call(
        input_kernel,
        in_specs=[SMEM] + [VMEM] * 2,
        out_specs=[VMEM] * (CTX + 1),
        out_shape=[shape((ROWS, 1024))] + [shape((FEAT_TILE, ROWS))] * CTX,
        scratch_shapes=[pltpu.VMEM((FEAT_TILE, SLAB), jnp.bfloat16)],
        compiler_params=params(),
        cost_estimate=cost(700_000_000, 4_000_000),
    )(c_at, kv_all, weight_tile)
    kv_rows, ig_parts = ig_results[0], ig_results[1:]
    ig_got = [to_shift(ig_parts[s], s) for s in range(CTX)]

    half_sum = wg_keep + wg_got.astype(jnp.float32)
    part = FEAT_TILE // 4
    second_send = lax.dynamic_slice_in_dim(half_sum, (1 - y_hi) * part, part, 0)
    second_keep = lax.dynamic_slice_in_dim(half_sum, y_hi * part, part, 0)
    second_got = lax.ppermute(
        second_send.astype(jnp.bfloat16), "fsdp", [(i, i ^ 2) for i in range(FSDP)]
    )
    chunks = pl.pallas_call(
        chunk_kernel,
        in_specs=[SMEM] + [VMEM] * 2,
        out_specs=[VMEM] * 8,
        out_shape=[shape((10, 1024))] * 8,
        scratch_shapes=[pltpu.VMEM((8, 10, 1024), jnp.float32)],
        compiler_params=params(),
        cost_estimate=cost(0, 700_000),
    )(z.reshape(1), second_keep, second_got)
    weight_grad = None
    for s in range(8):
        perm = []
        for f1 in range(FSDP):
            for c1 in range(CTX):
                z1, y1, core1 = f1 // 4, (f1 // 2) % 2, f1 % 2
                perm.append((f1 * CTX + c1, (c1 * 4 + core1 * 2 + y1) * CTX + (z1 + s) % 8))
        arrived = lax.ppermute(chunks[s], ("fsdp", "ctx"), perm).astype(jnp.float32)
        weight_grad = arrived if weight_grad is None else weight_grad + arrived

    dq_got = [to_shift(dq_parts[s], s) for s in range(CTX)]
    query_grad = pl.pallas_call(
        query_out_kernel,
        in_specs=[SMEM] + [VMEM] * CTX,
        out_specs=VMEM,
        out_shape=shape((ROWS, HQ * HEAD_WIDTH)),
        compiler_params=params(),
        cost_estimate=cost(0, 2_000_000),
    )(c_at, *dq_got)
    input_grad = pl.pallas_call(
        input_out_kernel,
        in_specs=[SMEM] + [VMEM] * CTX,
        out_specs=VMEM,
        out_shape=shape((ROWS, FEATURES)),
        scratch_shapes=[pltpu.VMEM((FEATURES, ROWS), jnp.bfloat16)],
        compiler_params=params(),
        cost_estimate=cost(0, 1_300_000),
    )(c_at, *ig_got)
    return (input_grad[None], query_grad[None], kv_rows[None], weight_grad)


def query_out_kernel(c_ref, *refs):
    pieces, out_ref = refs[:CTX], refs[CTX]
    c = c_ref[0]
    for s in range(CTX):
        src = lax.rem(c + CTX - s, CTX)
        out_ref[:, pl.ds(pl.multiple_of(src * Q_COLS, Q_COLS), Q_COLS)] = pieces[s][...]


def solution(mesh):
    placed = (
        P("fsdp", "ctx", None),
        P("fsdp", "ctx", None),
        P("fsdp", "ctx", None),
        P("fsdp", "ctx", None),
        P("fsdp", "ctx", None),
        P("fsdp", None),
        P("fsdp", None),
        P(),
    )
    return jax.shard_map(
        body,
        mesh=mesh,
        in_specs=placed,
        out_specs=(
            P("fsdp", "ctx", None),
            P("fsdp", "ctx", None),
            P("fsdp", "ctx", None),
            P(("fsdp", "ctx"), None),
        ),
        check_vma=False,
    )
```

```python
import functools
import math

import jax
import jax.numpy as jnp
from jax import lax
from jax.experimental import pallas as pl
from jax.experimental.pallas import tpu as pltpu
from jax.sharding import PartitionSpec as P

HQ = 32
KEY_VALUE_HEADS = 4
HEAD_WIDTH = 128
BLK = 32
QUERY_PER_KEY = 8

CTX = 8
FSDP = 32
ROWS = 128
SLAB = 1024
FEATURES = 2560
FEAT_TILE = FEATURES // CTX
Q_COLS = 512
PACK_COLS = 2 * Q_COLS + 2 * HEAD_WIDTH
HALF = 512
SCALE = 1.0 / math.sqrt(HEAD_WIDTH)
LOG2E = math.log2(math.e)
LOWEST = -1e30
NN = (((1,), (0,)), ((), ()))
NT = (((1,), (1,)), ((), ()))
VMEM = pl.BlockSpec(memory_space=pltpu.VMEM)
SMEM = pl.BlockSpec(memory_space=pltpu.SMEM)
VMEM_LIMIT = 48 * 1024 * 1024


def dot(a, b, dims):
    return lax.dot_general(a, b, dims, preferred_element_type=jnp.float32)


def shape(dims, kind=jnp.bfloat16):
    return jax.ShapeDtypeStruct(dims, kind)


def params():
    return pltpu.CompilerParams(vmem_limit_bytes=VMEM_LIMIT)


def cost(flops, moved):
    return pl.CostEstimate(flops=flops, bytes_accessed=moved, transcendentals=0)


def pack_kernel(q_ref, d_ref, k_ref, v_ref, out_ref):
    for dest in range(CTX):
        cols = slice(dest * Q_COLS, (dest + 1) * Q_COLS)
        head = slice((dest // 2) * HEAD_WIDTH, (dest // 2 + 1) * HEAD_WIDTH)
        out_ref[dest, :, 0:Q_COLS] = q_ref[:, cols]
        out_ref[dest, :, Q_COLS : 2 * Q_COLS] = d_ref[:, cols]
        out_ref[dest, :, 2 * Q_COLS : 2 * Q_COLS + HEAD_WIDTH] = k_ref[:, head]
        out_ref[dest, :, 2 * Q_COLS + HEAD_WIDTH :] = v_ref[:, head]


def turn_kernel(x_ref, out_ref, turned):
    turned[FEATURES:, :] = jnp.zeros((16, ROWS), jnp.float32)
    for j in range(FEATURES // 128):
        block = x_ref[:, j * 128 : (j + 1) * 128].T
        turned[j * 128 : (j + 1) * 128, :] = block.astype(jnp.float32)
    for dest in range(CTX):
        for shard in range(FSDP):
            at = shard * 80 + dest * 10
            window = turned[at : at + 16, :]
            out_ref[dest, shard * 16 : (shard + 1) * 16, :] = window.astype(jnp.bfloat16)


def attention_kernel(c_ref, docs_ref, order_ref, *refs):
    in_ref, dq_ref, keep_ref, send_ref = refs[:4]
    q_s, d_s, k_s, v_s, kt_s, dq_s, dkv_s, place, begin = refs[4:]
    c = c_ref[0]

    first = lax.fori_loop(
        0, 17, lambda i, a: jnp.where(docs_ref[i] == docs_ref[i + 15], i, a), jnp.int32(0)
    )

    def place_block(st, carry):
        b = order_ref[st]
        inside = (b >= first) & (b < first + 16)
        place[st] = jnp.where(inside, b - first, jnp.where(b < first, b + 16, b))
        return carry

    lax.fori_loop(0, 32, place_block, 0)

    def begin_block(t, carry):
        last_doc, last_begin = carry
        doc = docs_ref[jnp.where(t < first, t, t + 16)]
        now = jnp.where(doc == last_doc, last_begin, t)
        begin[t] = jnp.int32(0)
        begin[t + 16] = now * BLK
        return doc, now

    lax.fori_loop(0, 16, begin_block, (jnp.int32(-1), jnp.int32(0)))

    for st in range(32):
        rows = pl.ds(pl.multiple_of(place[st] * BLK, BLK), BLK)
        src, block = st // 4, slice((st % 4) * BLK, (st % 4 + 1) * BLK)
        q_s[rows, :] = in_ref[src, block, 0:Q_COLS]
        d_s[rows, :] = in_ref[src, block, Q_COLS : 2 * Q_COLS]
        k_s[rows, :] = in_ref[src, block, 2 * Q_COLS : 2 * Q_COLS + HEAD_WIDTH]
        v_s[rows, :] = in_ref[src, block, 2 * Q_COLS + HEAD_WIDTH :]
    for j in range(SLAB // 128):
        kt_s[:, j * 128 : (j + 1) * 128] = k_s[j * 128 : (j + 1) * 128, :].T
    dkv_s[...] = jnp.zeros_like(dkv_s)

    def half(hf, carry):
        base = pl.multiple_of(hf * HALF, HALF)
        for i in range(HALF // 128):
            n = (i + 1) * 128
            rows = pl.ds(pl.multiple_of(base + i * 128, 128), 128)
            keys = pl.ds(base, n)
            key_n = k_s[keys, :]
            value_n = v_s[keys, :]
            lane = lax.broadcasted_iota(jnp.int32, (n, 128), 1)
            row = lax.broadcasted_iota(jnp.int32, (n, 128), 0)
            low = jnp.zeros((n, 128), jnp.int32)
            for kk in range(4):
                low = jnp.where(lane // BLK == kk, begin[hf * 16 + i * 4 + kk], low)
            seen = (row >= low) & (row <= lane + i * 128)
            bias = jnp.where(seen, 0.0, LOWEST)
            bias = jnp.concatenate([bias, bias], axis=1)
            for g in range(2):
                cols = [slice((2 * g + e) * 128, (2 * g + e + 1) * 128) for e in range(2)]
                qs = jnp.concatenate([q_s[rows, e] for e in cols], axis=0)
                ds = jnp.concatenate([d_s[rows, e] for e in cols], axis=0)
                scores = dot(key_n, qs, NT) * (SCALE * LOG2E) + bias
                top = jnp.max(scores, axis=0, keepdims=True)
                probs = jnp.exp2(scores - top)
                total = jnp.sum(probs, axis=0, keepdims=True)
                probs = probs * (1.0 / total)
                products = dot(value_n, ds, NT)
                delta = jnp.sum(probs * products, axis=0, keepdims=True)
                score_grad = (probs * (products - delta)).astype(jnp.bfloat16)
                probs_low = probs.astype(jnp.bfloat16)
                dkv_s[keys, 0:128] += dot(score_grad, qs, NN)
                dkv_s[keys, 128:256] += dot(probs_low, ds, NN)
                dqt = dot(kt_s[:, keys], score_grad, NN) * SCALE
                for e in range(2):
                    dq_s[rows, cols[e]] = dqt[:, e * 128 : (e + 1) * 128].T.astype(jnp.bfloat16)
        return carry

    lax.fori_loop(0, 2, half, 0)

    odd = lax.rem(c, 2)
    own = pl.ds(pl.multiple_of(odd * 128, 128), 128)
    other = pl.ds(pl.multiple_of((1 - odd) * 128, 128), 128)
    own_scale = jnp.where(odd == 0, SCALE, 1.0)
    other_scale = jnp.where(odd == 0, 1.0, SCALE)
    for st in range(32):
        rows = pl.ds(pl.multiple_of(place[st] * BLK, BLK), BLK)
        block = slice(st * BLK, (st + 1) * BLK)
        keep_ref[block, :] = dkv_s[rows, own] * own_scale
        send_ref[block, :] = (dkv_s[rows, other] * other_scale).astype(jnp.bfloat16)
        dq_ref[st // 4, (st % 4) * BLK : (st % 4 + 1) * BLK, :] = dq_s[rows, :]


def pair_kernel(keep_ref, taken_ref, out_ref):
    total = (keep_ref[...] + taken_ref[...].astype(jnp.float32)).astype(jnp.bfloat16)
    for dest in range(CTX):
        out_ref[dest] = total


def weight_kernel(pieces_ref, x_ref, kv_ref, out_ref, x_s):
    for src in range(CTX):
        block = src // 2 + KEY_VALUE_HEADS * (src % 2)
        kv_ref[:, block * 128 : (block + 1) * 128] = pieces_ref[src]
        x_s[:, src * 128 : (src + 1) * 128] = x_ref[src]
    for j in range(4):
        cols = slice(j * 256, (j + 1) * 256)
        tile = dot(x_s[...], kv_ref[:, cols], NN).astype(jnp.bfloat16)
        for k in range(FSDP):
            out_ref[k, :, cols] = tile[k * 16 : (k + 1) * 16, :]


def input_kernel(c_ref, kv_ref, w_ref, kv_rows_ref, out_ref):
    c = c_ref[0]
    for j in range(4):
        rows = slice(j * 256, (j + 1) * 256)
        tile = dot(w_ref[...], kv_ref[rows, :], NT).astype(jnp.bfloat16)
        out_ref[2 * j] = tile[:, 0:128]
        out_ref[2 * j + 1] = tile[:, 128:256]
    kv_rows_ref[...] = kv_ref[pl.ds(pl.multiple_of(c * ROWS, ROWS), ROWS), :]


def out_kernel(ig_ref, dq_ref, input_ref, query_ref):
    for src in range(CTX):
        query_ref[:, src * Q_COLS : (src + 1) * Q_COLS] = dq_ref[src]
    for j in range(FEATURES // 128):
        input_ref[:, j * 128 : (j + 1) * 128] = ig_ref[j * 128 : (j + 1) * 128, :].T


def sum_kernel(parts_ref, out_ref):
    total = parts_ref[0].astype(jnp.float32)
    for k in range(1, FSDP):
        total = total + parts_ref[k].astype(jnp.float32)
    out_ref[...] = total[0:10, :]


def exchange(value, axis):
    return lax.all_to_all(value, axis, 0, 0, tiled=True)


def body(inputs, queries, keys, values, output_cotangent, key_value_weight, doc_ids, block_order):
    c = lax.axis_index("ctx").astype(jnp.int32)
    c_at = c.reshape(1)

    packed = pl.pallas_call(
        pack_kernel,
        in_specs=[VMEM] * 4,
        out_specs=VMEM,
        out_shape=shape((CTX, ROWS, PACK_COLS)),
        compiler_params=params(),
        cost_estimate=cost(0, 5_000_000),
    )(queries[0], output_cotangent[0], keys[0], values[0])
    got = exchange(packed, "ctx")

    own_rows = lax.dynamic_slice_in_dim(key_value_weight, c * 10, 10, 0)
    perm = [(f1 * CTX + c1, ((f1 * CTX + c1) % FSDP) * CTX + (f1 * CTX + c1) // FSDP)
            for f1 in range(FSDP) for c1 in range(CTX)]
    own_rows = lax.ppermute(own_rows, ("fsdp", "ctx"), perm)
    weight_tile = exchange(jnp.broadcast_to(own_rows[None], (FSDP, 10, 1024)), "fsdp")
    weight_tile = weight_tile.reshape(FEAT_TILE, 1024)

    turned = pl.pallas_call(
        turn_kernel,
        in_specs=[VMEM],
        out_specs=VMEM,
        out_shape=shape((CTX, FSDP * 16, ROWS)),
        scratch_shapes=[pltpu.VMEM((FEATURES + 16, ROWS), jnp.float32)],
        compiler_params=params(),
        cost_estimate=cost(0, 1_300_000),
    )(inputs[0])
    got_x = exchange(turned, "ctx")

    dq_parts, keep, send = pl.pallas_call(
        attention_kernel,
        in_specs=[SMEM] * 3 + [VMEM],
        out_specs=[VMEM] * 3,
        out_shape=[
            shape((CTX, ROWS, Q_COLS)),
            shape((SLAB, HEAD_WIDTH), jnp.float32),
            shape((SLAB, HEAD_WIDTH)),
        ],
        scratch_shapes=[
            pltpu.VMEM((SLAB, Q_COLS), jnp.bfloat16),
            pltpu.VMEM((SLAB, Q_COLS), jnp.bfloat16),
            pltpu.VMEM((SLAB, HEAD_WIDTH), jnp.bfloat16),
            pltpu.VMEM((SLAB, HEAD_WIDTH), jnp.bfloat16),
            pltpu.VMEM((HEAD_WIDTH, SLAB), jnp.bfloat16),
            pltpu.VMEM((SLAB, Q_COLS), jnp.bfloat16),
            pltpu.VMEM((SLAB, 2 * HEAD_WIDTH), jnp.float32),
            pltpu.SMEM((32,), jnp.int32),
            pltpu.SMEM((32,), jnp.int32),
        ],
        compiler_params=params(),
        cost_estimate=cost(2_000_000_000, 5_000_000),
    )(c_at, doc_ids[0], block_order, got)

    taken = lax.ppermute(send, "ctx", [(i, i ^ 1) for i in range(CTX)])
    own_cols = pl.pallas_call(
        pair_kernel,
        in_specs=[VMEM] * 2,
        out_specs=VMEM,
        out_shape=shape((CTX, SLAB, HEAD_WIDTH)),
        compiler_params=params(),
        cost_estimate=cost(0, 3_000_000),
    )(keep, taken)
    pieces = exchange(own_cols, "ctx")

    kv_all, wg_parts = pl.pallas_call(
        weight_kernel,
        in_specs=[VMEM] * 2,
        out_specs=[VMEM] * 2,
        out_shape=[shape((SLAB, 1024)), shape((FSDP, 16, 1024))],
        scratch_shapes=[pltpu.VMEM((FSDP * 16, SLAB), jnp.bfloat16)],
        compiler_params=params(),
        cost_estimate=cost(1_100_000_000, 5_000_000),
    )(pieces, got_x)
    wg_got = exchange(wg_parts, "fsdp")

    kv_rows, ig_parts = pl.pallas_call(
        input_kernel,
        in_specs=[SMEM] + [VMEM] * 2,
        out_specs=[VMEM] * 2,
        out_shape=[shape((ROWS, 1024)), shape((CTX, FEAT_TILE, ROWS))],
        compiler_params=params(),
        cost_estimate=cost(700_000_000, 4_000_000),
    )(c_at, kv_all, weight_tile)
    ig_got = exchange(ig_parts, "ctx").reshape(FEATURES, ROWS)
    dq_got = exchange(dq_parts, "ctx")

    input_grad, query_grad = pl.pallas_call(
        out_kernel,
        in_specs=[VMEM] * 2,
        out_specs=[VMEM] * 2,
        out_shape=[shape((ROWS, FEATURES)), shape((ROWS, HQ * HEAD_WIDTH))],
        compiler_params=params(),
        cost_estimate=cost(0, 3_300_000),
    )(ig_got, dq_got)
    weight_grad = pl.pallas_call(
        sum_kernel,
        in_specs=[VMEM],
        out_specs=VMEM,
        out_shape=shape((10, 1024), jnp.float32),
        compiler_params=params(),
        cost_estimate=cost(0, 1_000_000),
    )(wg_got)
    return (input_grad[None], query_grad[None], kv_rows[None], weight_grad)


def solution(mesh):
    placed = (
        P("fsdp", "ctx", None),
        P("fsdp", "ctx", None),
        P("fsdp", "ctx", None),
        P("fsdp", "ctx", None),
        P("fsdp", "ctx", None),
        P("fsdp", None),
        P("fsdp", None),
        P(),
    )
    return jax.shard_map(
        body,
        mesh=mesh,
        in_specs=placed,
        out_specs=(
            P("fsdp", "ctx", None),
            P("fsdp", "ctx", None),
            P("fsdp", "ctx", None),
            P(("fsdp", "ctx"), None),
        ),
        check_vma=False,
    )
```

```python
import functools
import math

import jax
import jax.numpy as jnp
from jax import lax
from jax.experimental import pallas as pl
from jax.experimental.pallas import tpu as pltpu
from jax.sharding import PartitionSpec as P

HQ = 32
KEY_VALUE_HEADS = 4
HEAD_WIDTH = 128
BLK = 32
QUERY_PER_KEY = 8

CTX = 8
FSDP = 32
ROWS = 128
SLAB = 1024
FEATURES = 2560
FEAT_TILE = FEATURES // 4
Q_COLS = 512
PACK_COLS = 2 * Q_COLS + 2 * HEAD_WIDTH
HALF = 512
SCALE = 1.0 / math.sqrt(HEAD_WIDTH)
LOG2E = math.log2(math.e)
LOWEST = -1e30
NN = (((1,), (0,)), ((), ()))
NT = (((1,), (1,)), ((), ()))
VMEM = pl.BlockSpec(memory_space=pltpu.VMEM)
SMEM = pl.BlockSpec(memory_space=pltpu.SMEM)
VMEM_LIMIT = 48 * 1024 * 1024


def dot(a, b, dims):
    return lax.dot_general(a, b, dims, preferred_element_type=jnp.float32)


def shape(dims, kind=jnp.bfloat16):
    return jax.ShapeDtypeStruct(dims, kind)


def params():
    return pltpu.CompilerParams(vmem_limit_bytes=VMEM_LIMIT)


def cost(flops, moved):
    return pl.CostEstimate(flops=flops, bytes_accessed=moved, transcendentals=0)


def q_block(device):
    return (device % 4) * 2 + device // 4


def pack_kernel(q_ref, d_ref, k_ref, v_ref, out_ref):
    for dest in range(CTX):
        at = q_block(dest)
        cols = slice(at * Q_COLS, (at + 1) * Q_COLS)
        head = slice((dest % 4) * HEAD_WIDTH, (dest % 4 + 1) * HEAD_WIDTH)
        out_ref[dest, :, 0:Q_COLS] = q_ref[:, cols]
        out_ref[dest, :, Q_COLS : 2 * Q_COLS] = d_ref[:, cols]
        out_ref[dest, :, 2 * Q_COLS : 2 * Q_COLS + HEAD_WIDTH] = k_ref[:, head]
        out_ref[dest, :, 2 * Q_COLS + HEAD_WIDTH :] = v_ref[:, head]


def turn_kernel(x_ref, out_ref, turned, tile):
    for j in range(FEATURES // 128):
        block = x_ref[:, j * 128 : (j + 1) * 128].T
        turned[j * 128 : (j + 1) * 128, :] = block.astype(jnp.float32)
    for x in range(4):
        for low in range(4):
            for y in range(2):
                for z in range(8):
                    source = (z * 4 + low) * 80 + y * 40 + x * 10
                    at = (low * 2 + y) * 80 + z * 10
                    tile[at : at + 10, :] = turned[source : source + 10, :]
        piece = tile[...].astype(jnp.bfloat16)
        out_ref[x] = piece
        out_ref[x + 4] = piece


def attention_kernel(c_ref, docs_ref, order_ref, *refs):
    in_ref, dq_ref, keep_ref, send_ref = refs[:4]
    q_s, d_s, k_s, v_s, kt_s, dq_s, dkv_s, place, begin = refs[4:]
    c = c_ref[0]

    first = lax.fori_loop(
        0, 17, lambda i, a: jnp.where(docs_ref[i] == docs_ref[i + 15], i, a), jnp.int32(0)
    )

    def place_block(st, carry):
        b = order_ref[st]
        inside = (b >= first) & (b < first + 16)
        place[st] = jnp.where(inside, b - first, jnp.where(b < first, b + 16, b))
        return carry

    lax.fori_loop(0, 32, place_block, 0)

    def begin_block(t, carry):
        last_doc, last_begin = carry
        doc = docs_ref[jnp.where(t < first, t, t + 16)]
        now = jnp.where(doc == last_doc, last_begin, t)
        begin[t] = jnp.int32(0)
        begin[t + 16] = now * BLK
        return doc, now

    lax.fori_loop(0, 16, begin_block, (jnp.int32(-1), jnp.int32(0)))

    for st in range(32):
        rows = pl.ds(pl.multiple_of(place[st] * BLK, BLK), BLK)
        src, block = st // 4, slice((st % 4) * BLK, (st % 4 + 1) * BLK)
        q_s[rows, :] = in_ref[src, block, 0:Q_COLS]
        d_s[rows, :] = in_ref[src, block, Q_COLS : 2 * Q_COLS]
        k_s[rows, :] = in_ref[src, block, 2 * Q_COLS : 2 * Q_COLS + HEAD_WIDTH]
        v_s[rows, :] = in_ref[src, block, 2 * Q_COLS + HEAD_WIDTH :]
    for j in range(SLAB // 128):
        kt_s[:, j * 128 : (j + 1) * 128] = k_s[j * 128 : (j + 1) * 128, :].T
    dkv_s[...] = jnp.zeros_like(dkv_s)

    def half(hf, carry):
        base = pl.multiple_of(hf * HALF, HALF)
        for i in range(HALF // 128):
            n = (i + 1) * 128
            rows = pl.ds(pl.multiple_of(base + i * 128, 128), 128)
            keys = pl.ds(base, n)
            key_n = k_s[keys, :]
            value_n = v_s[keys, :]
            lane = lax.broadcasted_iota(jnp.int32, (n, 128), 1)
            row = lax.broadcasted_iota(jnp.int32, (n, 128), 0)
            low = jnp.zeros((n, 128), jnp.int32)
            for kk in range(4):
                low = jnp.where(lane // BLK == kk, begin[hf * 16 + i * 4 + kk], low)
            seen = (row >= low) & (row <= lane + i * 128)
            bias = jnp.where(seen, 0.0, LOWEST)
            bias = jnp.concatenate([bias, bias], axis=1)
            for g in range(2):
                cols = [slice((2 * g + e) * 128, (2 * g + e + 1) * 128) for e in range(2)]
                qs = jnp.concatenate([q_s[rows, e] for e in cols], axis=0)
                ds = jnp.concatenate([d_s[rows, e] for e in cols], axis=0)
                scores = dot(key_n, qs, NT) * (SCALE * LOG2E) + bias
                top = jnp.max(scores, axis=0, keepdims=True)
                probs = jnp.exp2(scores - top)
                total = jnp.sum(probs, axis=0, keepdims=True)
                probs = probs * (1.0 / total)
                products = dot(value_n, ds, NT)
                delta = jnp.sum(probs * products, axis=0, keepdims=True)
                score_grad = (probs * (products - delta)).astype(jnp.bfloat16)
                probs_low = probs.astype(jnp.bfloat16)
                dkv_s[keys, 0:128] += dot(score_grad, qs, NN)
                dkv_s[keys, 128:256] += dot(probs_low, ds, NN)
                dqt = dot(kt_s[:, keys], score_grad, NN) * SCALE
                for e in range(2):
                    dq_s[rows, cols[e]] = dqt[:, e * 128 : (e + 1) * 128].T.astype(jnp.bfloat16)
        return carry

    lax.fori_loop(0, 2, half, 0)

    odd = c // 4
    own = pl.ds(pl.multiple_of(odd * 128, 128), 128)
    other = pl.ds(pl.multiple_of((1 - odd) * 128, 128), 128)
    own_scale = jnp.where(odd == 0, SCALE, 1.0)
    other_scale = jnp.where(odd == 0, 1.0, SCALE)
    for st in range(32):
        rows = pl.ds(pl.multiple_of(place[st] * BLK, BLK), BLK)
        block = slice(st * BLK, (st + 1) * BLK)
        keep_ref[block, :] = dkv_s[rows, own] * own_scale
        send_ref[block, :] = (dkv_s[rows, other] * other_scale).astype(jnp.bfloat16)
        dq_ref[st // 4, (st % 4) * BLK : (st % 4 + 1) * BLK, :] = dq_s[rows, :]


def pair_kernel(keep_ref, taken_ref, out_ref):
    total = (keep_ref[...] + taken_ref[...].astype(jnp.float32)).astype(jnp.bfloat16)
    for dest in range(4):
        out_ref[dest] = total


def weight_kernel(pieces_ref, x_ref, kv_ref, out_ref, x_s):
    for src in range(4):
        kv_ref[:, src * 128 : (src + 1) * 128] = pieces_ref[src]
    for src in range(CTX):
        x_s[:, src * 128 : (src + 1) * 128] = x_ref[src]
    for j in range(2):
        cols = slice(j * 256, (j + 1) * 256)
        tile = dot(x_s[...], kv_ref[:, cols], NN).astype(jnp.bfloat16)
        for k in range(8):
            out_ref[k, :, cols] = tile[k * 80 : (k + 1) * 80, :]


def input_kernel(kv_ref, w_ref, own_ref, out_ref):
    for j in range(4):
        rows = slice(j * 256, (j + 1) * 256)
        tile = dot(w_ref[...], kv_ref[rows, :], NT).astype(jnp.bfloat16)
        out_ref[2 * j, 0:FEAT_TILE, :] = tile[:, 0:128]
        out_ref[2 * j + 1, 0:FEAT_TILE, :] = tile[:, 128:256]
    for dest in range(CTX):
        out_ref[dest, FEAT_TILE:, :] = own_ref[0, dest * ROWS : (dest + 1) * ROWS, :]


def input_out_kernel(parts_ref, input_ref, kv_rows_ref):
    for x in range(4):
        for j in range(FEAT_TILE // 128):
            rows = slice(j * 128, (j + 1) * 128)
            total = parts_ref[x, rows, :].astype(jnp.float32) + parts_ref[x + 4, rows, :].astype(jnp.float32)
            at = x * FEAT_TILE + j * 128
            input_ref[:, at : at + 128] = total.T.astype(jnp.bfloat16)
    for src in range(CTX):
        kv_rows_ref[:, src * 128 : (src + 1) * 128] = parts_ref[src, FEAT_TILE:, :]


def query_out_kernel(dq_ref, query_ref):
    for src in range(CTX):
        at = q_block(src)
        query_ref[:, at * Q_COLS : (at + 1) * Q_COLS] = dq_ref[src]


def first_sum_kernel(parts_ref, out_ref):
    for y in range(2):
        total = parts_ref[y].astype(jnp.float32)
        for low in range(1, 4):
            total = total + parts_ref[low * 2 + y].astype(jnp.float32)
        for z in range(8):
            out_ref[z, :, y * 512 : (y + 1) * 512] = total[z * 10 : (z + 1) * 10, :].astype(jnp.bfloat16)


def second_sum_kernel(parts_ref, out_ref):
    total = parts_ref[0].astype(jnp.float32)
    for k in range(1, 8):
        total = total + parts_ref[k].astype(jnp.float32)
    out_ref[...] = total


def exchange(value, axis):
    return lax.all_to_all(value, axis, 0, 0, tiled=True)


def body(inputs, queries, keys, values, output_cotangent, key_value_weight, doc_ids, block_order):
    c = lax.axis_index(("y", "x")).astype(jnp.int32)
    c_at = c.reshape(1)

    packed = pl.pallas_call(
        pack_kernel,
        in_specs=[VMEM] * 4,
        out_specs=VMEM,
        out_shape=shape((CTX, ROWS, PACK_COLS)),
        compiler_params=params(),
        cost_estimate=cost(0, 5_000_000),
    )(queries[0], output_cotangent[0], keys[0], values[0])
    got = exchange(packed, ("y", "x"))

    turned = pl.pallas_call(
        turn_kernel,
        in_specs=[VMEM],
        out_specs=VMEM,
        out_shape=shape((CTX, FEAT_TILE, ROWS)),
        scratch_shapes=[
            pltpu.VMEM((FEATURES, ROWS), jnp.float32),
            pltpu.VMEM((FEAT_TILE, ROWS), jnp.float32),
        ],
        compiler_params=params(),
        cost_estimate=cost(0, 1_300_000),
    )(inputs[0])
    own_rows = lax.dynamic_slice(
        key_value_weight, (lax.rem(c, 4) * 20, (c // 4) * 512), (20, 512)
    )
    perm = []
    for f1 in range(FSDP):
        for c1 in range(CTX):
            y1, x1 = c1 // 4, c1 % 4
            perm.append((f1 * CTX + c1, ((f1 % 8) * 4 + x1) * CTX + y1 * 4 + f1 // 8))
    own_rows = lax.ppermute(own_rows, ("z", "yh", "core", "y", "x"), perm)
    weight_tile = exchange(
        jnp.broadcast_to(own_rows[None], (FSDP, 20, 512)), ("z", "yh", "core")
    ).reshape(FEAT_TILE, 512)

    got, turned, weight_tile = lax.optimization_barrier((got, turned, weight_tile))
    got_x = exchange(turned, ("y", "x"))

    dq_parts, keep, send = pl.pallas_call(
        attention_kernel,
        in_specs=[SMEM] * 3 + [VMEM],
        out_specs=[VMEM] * 3,
        out_shape=[
            shape((CTX, ROWS, Q_COLS)),
            shape((SLAB, HEAD_WIDTH), jnp.float32),
            shape((SLAB, HEAD_WIDTH)),
        ],
        scratch_shapes=[
            pltpu.VMEM((SLAB, Q_COLS), jnp.bfloat16),
            pltpu.VMEM((SLAB, Q_COLS), jnp.bfloat16),
            pltpu.VMEM((SLAB, HEAD_WIDTH), jnp.bfloat16),
            pltpu.VMEM((SLAB, HEAD_WIDTH), jnp.bfloat16),
            pltpu.VMEM((HEAD_WIDTH, SLAB), jnp.bfloat16),
            pltpu.VMEM((SLAB, Q_COLS), jnp.bfloat16),
            pltpu.VMEM((SLAB, 2 * HEAD_WIDTH), jnp.float32),
            pltpu.SMEM((32,), jnp.int32),
            pltpu.SMEM((32,), jnp.int32),
        ],
        compiler_params=params(),
        cost_estimate=cost(2_000_000_000, 5_000_000),
    )(c_at, doc_ids[0], block_order, got)

    taken = lax.ppermute(send, "y", [(0, 1), (1, 0)])
    own_cols = pl.pallas_call(
        pair_kernel,
        in_specs=[VMEM] * 2,
        out_specs=VMEM,
        out_shape=shape((4, SLAB, HEAD_WIDTH)),
        compiler_params=params(),
        cost_estimate=cost(0, 3_000_000),
    )(keep, taken)
    pieces = exchange(own_cols, "x")
    dq_got = exchange(dq_parts, ("y", "x"))

    kv_half, wg_parts = pl.pallas_call(
        weight_kernel,
        in_specs=[VMEM] * 2,
        out_specs=[VMEM] * 2,
        out_shape=[shape((SLAB, 512)), shape((8, 80, 512))],
        scratch_shapes=[pltpu.VMEM((FEAT_TILE, SLAB), jnp.bfloat16)],
        compiler_params=params(),
        cost_estimate=cost(700_000_000, 5_000_000),
    )(pieces, got_x)
    wg_got = exchange(wg_parts, ("yh", "core", "y"))

    ig_parts = pl.pallas_call(
        input_kernel,
        in_specs=[VMEM] * 3,
        out_specs=VMEM,
        out_shape=shape((CTX, FEAT_TILE + ROWS, ROWS)),
        compiler_params=params(),
        cost_estimate=cost(700_000_000, 4_000_000),
    )(kv_half, weight_tile, own_cols)
    ig_got = exchange(ig_parts, ("y", "x"))

    wg_second = pl.pallas_call(
        first_sum_kernel,
        in_specs=[VMEM],
        out_specs=VMEM,
        out_shape=shape((8, 10, 1024)),
        compiler_params=params(),
        cost_estimate=cost(0, 1_000_000),
    )(wg_got)
    wg_last = exchange(wg_second, "z")

    query_grad = pl.pallas_call(
        query_out_kernel,
        in_specs=[VMEM],
        out_specs=VMEM,
        out_shape=shape((ROWS, HQ * HEAD_WIDTH)),
        compiler_params=params(),
        cost_estimate=cost(0, 2_000_000),
    )(dq_got)
    input_grad, kv_rows = pl.pallas_call(
        input_out_kernel,
        in_specs=[VMEM],
        out_specs=[VMEM] * 2,
        out_shape=[shape((ROWS, FEATURES)), shape((ROWS, 1024))],
        compiler_params=params(),
        cost_estimate=cost(0, 2_000_000),
    )(ig_got)
    weight_grad = pl.pallas_call(
        second_sum_kernel,
        in_specs=[VMEM],
        out_specs=VMEM,
        out_shape=shape((10, 1024), jnp.float32),
        compiler_params=params(),
        cost_estimate=cost(0, 200_000),
    )(wg_last)
    return (input_grad[None], query_grad[None], kv_rows[None], weight_grad)


def solution(mesh):
    axes = ("z", "yh", "core", "y", "x")
    named = jax.sharding.Mesh(mesh.devices.reshape(8, 2, 2, 2, 4), axes)
    fsdp, ctx = axes[:3], axes[3:]
    return jax.shard_map(
        body,
        mesh=named,
        in_specs=(P(fsdp, ctx, None),) * 5 + (P(fsdp, None), P(fsdp, None), P()),
        out_specs=(P(fsdp, ctx, None),) * 3 + (P(axes, None),),
        check_vma=False,
    )
```

```python
import functools
import math

import jax
import jax.numpy as jnp
from jax import lax
from jax.experimental import pallas as pl
from jax.experimental.pallas import tpu as pltpu
from jax.sharding import PartitionSpec as P

HQ = 32
KEY_VALUE_HEADS = 4
HEAD_WIDTH = 128
BLK = 32
QUERY_PER_KEY = 8

CTX = 8
FSDP = 32
ROWS = 128
SLAB = 1024
FEATURES = 2560
FEAT_TILE = FEATURES // 4
Q_COLS = 512
PACK_COLS = 2 * Q_COLS + 2 * HEAD_WIDTH
HALF = 512
SCALE = 1.0 / math.sqrt(HEAD_WIDTH)
LOG2E = math.log2(math.e)
LOWEST = -1e30
NN = (((1,), (0,)), ((), ()))
NT = (((1,), (1,)), ((), ()))
VMEM = pl.BlockSpec(memory_space=pltpu.VMEM)
SMEM = pl.BlockSpec(memory_space=pltpu.SMEM)
VMEM_LIMIT = 48 * 1024 * 1024


def dot(a, b, dims):
    return lax.dot_general(a, b, dims, preferred_element_type=jnp.float32)


def shape(dims, kind=jnp.bfloat16):
    return jax.ShapeDtypeStruct(dims, kind)


def params():
    return pltpu.CompilerParams(vmem_limit_bytes=VMEM_LIMIT)


def cost(flops, moved):
    return pl.CostEstimate(flops=flops, bytes_accessed=moved, transcendentals=0)


def q_block(device):
    return (device % 4) * 2 + device // 4


def pack_kernel(q_ref, d_ref, k_ref, v_ref, out_ref):
    for dest in range(CTX):
        at = q_block(dest)
        cols = slice(at * Q_COLS, (at + 1) * Q_COLS)
        head = slice((dest % 4) * HEAD_WIDTH, (dest % 4 + 1) * HEAD_WIDTH)
        out_ref[dest, :, 0:Q_COLS] = q_ref[:, cols]
        out_ref[dest, :, Q_COLS : 2 * Q_COLS] = d_ref[:, cols]
        out_ref[dest, :, 2 * Q_COLS : 2 * Q_COLS + HEAD_WIDTH] = k_ref[:, head]
        out_ref[dest, :, 2 * Q_COLS + HEAD_WIDTH :] = v_ref[:, head]


def tile_row(z, low, y):
    row = (low % 2) * 320 + (low // 2) * 160
    return row + (z % 2) * 80 + (z // 2 % 2) * 40 + (z // 4) * 20 + y * 10


def turn_kernel(x_ref, out_ref, turned, tile):
    for j in range(FEATURES // 128):
        block = x_ref[:, j * 128 : (j + 1) * 128].T
        turned[j * 128 : (j + 1) * 128, :] = block.astype(jnp.float32)
    for x in range(4):
        for low in range(4):
            for y in range(2):
                for z in range(8):
                    source = (z * 4 + low) * 80 + y * 40 + x * 10
                    at = tile_row(z, low, y)
                    tile[at : at + 10, :] = turned[source : source + 10, :]
        piece = tile[...].astype(jnp.bfloat16)
        out_ref[x] = piece
        out_ref[x + 4] = piece


def attention_kernel(c_ref, docs_ref, order_ref, *refs):
    in_ref, dq_ref, keep_ref, send_ref = refs[:4]
    q_s, d_s, k_s, v_s, kt_s, dq_s, dkv_s, place, begin = refs[4:]
    c = c_ref[0]

    first = lax.fori_loop(
        0, 17, lambda i, a: jnp.where(docs_ref[i] == docs_ref[i + 15], i, a), jnp.int32(0)
    )

    def place_block(st, carry):
        b = order_ref[st]
        inside = (b >= first) & (b < first + 16)
        place[st] = jnp.where(inside, b - first, jnp.where(b < first, b + 16, b))
        return carry

    lax.fori_loop(0, 32, place_block, 0)

    def begin_block(t, carry):
        last_doc, last_begin = carry
        doc = docs_ref[jnp.where(t < first, t, t + 16)]
        now = jnp.where(doc == last_doc, last_begin, t)
        begin[t] = jnp.int32(0)
        begin[t + 16] = now * BLK
        return doc, now

    lax.fori_loop(0, 16, begin_block, (jnp.int32(-1), jnp.int32(0)))

    for st in range(32):
        rows = pl.ds(pl.multiple_of(place[st] * BLK, BLK), BLK)
        src, block = st // 4, slice((st % 4) * BLK, (st % 4 + 1) * BLK)
        q_s[rows, :] = in_ref[src, block, 0:Q_COLS]
        d_s[rows, :] = in_ref[src, block, Q_COLS : 2 * Q_COLS]
        k_s[rows, :] = in_ref[src, block, 2 * Q_COLS : 2 * Q_COLS + HEAD_WIDTH]
        v_s[rows, :] = in_ref[src, block, 2 * Q_COLS + HEAD_WIDTH :]
    for j in range(SLAB // 128):
        kt_s[:, j * 128 : (j + 1) * 128] = k_s[j * 128 : (j + 1) * 128, :].T
    dkv_s[...] = jnp.zeros_like(dkv_s)

    def half(hf, carry):
        base = pl.multiple_of(hf * HALF, HALF)
        for i in range(HALF // 128):
            n = (i + 1) * 128
            rows = pl.ds(pl.multiple_of(base + i * 128, 128), 128)
            keys = pl.ds(base, n)
            key_n = k_s[keys, :]
            value_n = v_s[keys, :]
            lane = lax.broadcasted_iota(jnp.int32, (n, 128), 1)
            row = lax.broadcasted_iota(jnp.int32, (n, 128), 0)
            low = jnp.zeros((n, 128), jnp.int32)
            for kk in range(4):
                low = jnp.where(lane // BLK == kk, begin[hf * 16 + i * 4 + kk], low)
            seen = (row >= low) & (row <= lane + i * 128)
            bias = jnp.where(seen, 0.0, LOWEST)
            bias = jnp.concatenate([bias, bias], axis=1)
            for g in range(2):
                cols = [slice((2 * g + e) * 128, (2 * g + e + 1) * 128) for e in range(2)]
                qs = jnp.concatenate([q_s[rows, e] for e in cols], axis=0)
                ds = jnp.concatenate([d_s[rows, e] for e in cols], axis=0)
                scores = dot(key_n, qs, NT) * (SCALE * LOG2E) + bias
                top = jnp.max(scores, axis=0, keepdims=True)
                probs = jnp.exp2(scores - top)
                total = jnp.sum(probs, axis=0, keepdims=True)
                probs = probs * (1.0 / total)
                products = dot(value_n, ds, NT)
                delta = jnp.sum(probs * products, axis=0, keepdims=True)
                score_grad = (probs * (products - delta)).astype(jnp.bfloat16)
                probs_low = probs.astype(jnp.bfloat16)
                dkv_s[keys, 0:128] += dot(score_grad, qs, NN)
                dkv_s[keys, 128:256] += dot(probs_low, ds, NN)
                dqt = dot(kt_s[:, keys], score_grad, NN) * SCALE
                for e in range(2):
                    dq_s[rows, cols[e]] = dqt[:, e * 128 : (e + 1) * 128].T.astype(jnp.bfloat16)
        return carry

    lax.fori_loop(0, 2, half, 0)

    odd = c // 4
    own = pl.ds(pl.multiple_of(odd * 128, 128), 128)
    other = pl.ds(pl.multiple_of((1 - odd) * 128, 128), 128)
    own_scale = jnp.where(odd == 0, SCALE, 1.0)
    other_scale = jnp.where(odd == 0, 1.0, SCALE)
    for st in range(32):
        rows = pl.ds(pl.multiple_of(place[st] * BLK, BLK), BLK)
        block = slice(st * BLK, (st + 1) * BLK)
        keep_ref[block, :] = dkv_s[rows, own] * own_scale
        send_ref[block, :] = (dkv_s[rows, other] * other_scale).astype(jnp.bfloat16)
        for g in range(4):
            at = g * 128 + (st % 4) * BLK
            dq_ref[st // 4, at : at + BLK, :] = dq_s[rows, g * 128 : (g + 1) * 128]


def pair_kernel(keep_ref, taken_ref, out_ref):
    total = (keep_ref[...] + taken_ref[...].astype(jnp.float32)).astype(jnp.bfloat16)
    for dest in range(4):
        out_ref[dest] = total


def weight_kernel(core_ref, pieces_ref, x_ref, kv_ref, send_ref, keep_ref, x_s):
    for src in range(4):
        kv_ref[:, src * 128 : (src + 1) * 128] = pieces_ref[src]
    for src in range(CTX):
        x_s[:, src * 128 : (src + 1) * 128] = x_ref[src]
    core, part = core_ref[0], FEAT_TILE // 2
    other = pl.ds(pl.multiple_of((1 - core) * part, part), part)
    own = pl.ds(pl.multiple_of(core * part, part), part)
    for j in range(2):
        cols = slice(j * 256, (j + 1) * 256)
        send_ref[:, cols] = dot(x_s[other, :], kv_ref[:, cols], NN).astype(jnp.bfloat16)
        keep_ref[:, cols] = dot(x_s[own, :], kv_ref[:, cols], NN)


def halve_kernel(bit_ref, keep_ref, got_ref, send_ref, kept_ref):
    part = kept_ref.shape[0]
    total = keep_ref[...] + got_ref[...].astype(jnp.float32)
    low, high, upper = total[:part, :], total[part:, :], bit_ref[0] == 1
    send_ref[...] = jnp.where(upper, low, high).astype(send_ref.dtype)
    kept_ref[...] = jnp.where(upper, high, low)


def join_kernel(y_ref, own_ref, got_ref, out_ref):
    upper = y_ref[0] == 1
    out_ref[:, 0:512] = jnp.where(upper, got_ref[...], own_ref[...])
    out_ref[:, 512:1024] = jnp.where(upper, own_ref[...], got_ref[...])


def input_kernel(f_ref, kv_ref, w_ref, own_ref, dq_ref, out_ref, w_s):
    for at in range(FSDP):
        mask = sum(((at >> i) & 1) << bit for i, bit in enumerate(GATHER_BITS))
        source = f_ref[0] ^ mask
        rows = pl.ds(pl.multiple_of((source // 4) * 80, 80), 80)
        cols = pl.ds(pl.multiple_of(lax.rem(source, 4) * 128, 128), 128)
        w_s[rows, cols] = w_ref[at]
    for j in range(4):
        rows = slice(j * 256, (j + 1) * 256)
        tile = dot(w_s[...], kv_ref[rows, :], NT).astype(jnp.bfloat16)
        out_ref[2 * j, 0:FEAT_TILE, :] = tile[:, 0:128]
        out_ref[2 * j + 1, 0:FEAT_TILE, :] = tile[:, 128:256]
    for dest in range(CTX):
        out_ref[dest, FEAT_TILE : FEAT_TILE + ROWS, :] = own_ref[0, dest * ROWS : (dest + 1) * ROWS, :]
        out_ref[dest, FEAT_TILE + ROWS :, :] = dq_ref[dest]


def out_kernel(parts_ref, input_ref, query_ref, kv_rows_ref):
    for x in range(4):
        for j in range(FEAT_TILE // 128):
            rows = slice(j * 128, (j + 1) * 128)
            total = parts_ref[x, rows, :].astype(jnp.float32) + parts_ref[x + 4, rows, :].astype(jnp.float32)
            at = x * FEAT_TILE + j * 128
            input_ref[:, at : at + 128] = total.T.astype(jnp.bfloat16)
    for src in range(CTX):
        kv_rows_ref[:, src * 128 : (src + 1) * 128] = parts_ref[src, FEAT_TILE : FEAT_TILE + ROWS, :]
        for g in range(4):
            at = q_block(src) * Q_COLS + g * 128
            rows = slice(FEAT_TILE + ROWS + g * 128, FEAT_TILE + ROWS + (g + 1) * 128)
            query_ref[:, at : at + 128] = parts_ref[src, rows, :]


GATHER_BITS = (4, 3, 2, 1, 0)
BIT_AXES = (("core", 1), ("yh", 1), ("z", 1), ("z", 2), ("z", 4))


def swap(value, bit):
    axis, mask = BIT_AXES[bit]
    return lax.ppermute(value, axis, [(i, i ^ mask) for i in range(8 if axis == "z" else 2)])


def exchange(value, axis):
    return lax.all_to_all(value, axis, 0, 0, tiled=True)


def body(inputs, queries, keys, values, output_cotangent, key_value_weight, doc_ids, block_order):
    c = lax.axis_index(("y", "x")).astype(jnp.int32)
    c_at = c.reshape(1)

    packed = pl.pallas_call(
        pack_kernel,
        in_specs=[VMEM] * 4,
        out_specs=VMEM,
        out_shape=shape((CTX, ROWS, PACK_COLS)),
        compiler_params=params(),
        cost_estimate=cost(0, 5_000_000),
    )(queries[0], output_cotangent[0], keys[0], values[0])
    got = exchange(packed, ("y", "x"))

    turned = pl.pallas_call(
        turn_kernel,
        in_specs=[VMEM],
        out_specs=VMEM,
        out_shape=shape((CTX, FEAT_TILE, ROWS)),
        scratch_shapes=[
            pltpu.VMEM((FEATURES, ROWS), jnp.float32),
            pltpu.VMEM((FEAT_TILE, ROWS), jnp.float32),
        ],
        compiler_params=params(),
        cost_estimate=cost(0, 1_300_000),
    )(inputs[0])
    f = lax.axis_index(("z", "yh", "core")).astype(jnp.int32)
    tile = lax.dynamic_slice(key_value_weight, (0, c * 128), (80, 128))
    perm = []
    for f1 in range(FSDP):
        for c1 in range(CTX):
            y1, x1 = c1 // 4, c1 % 4
            perm.append((f1 * CTX + c1, ((f1 % 8) * 4 + x1) * CTX + y1 * 4 + f1 // 8))
    tile = lax.ppermute(tile, ("z", "yh", "core", "y", "x"), perm)[None]
    for bit in GATHER_BITS:
        tile = jnp.concatenate([tile, swap(tile, bit)], axis=0)

    got, turned, weight_tile = lax.optimization_barrier((got, turned, tile))
    got_x = exchange(turned, ("y", "x"))

    dq_parts, keep, send = pl.pallas_call(
        attention_kernel,
        in_specs=[SMEM] * 3 + [VMEM],
        out_specs=[VMEM] * 3,
        out_shape=[
            shape((CTX, Q_COLS, ROWS)),
            shape((SLAB, HEAD_WIDTH), jnp.float32),
            shape((SLAB, HEAD_WIDTH)),
        ],
        scratch_shapes=[
            pltpu.VMEM((SLAB, Q_COLS), jnp.bfloat16),
            pltpu.VMEM((SLAB, Q_COLS), jnp.bfloat16),
            pltpu.VMEM((SLAB, HEAD_WIDTH), jnp.bfloat16),
            pltpu.VMEM((SLAB, HEAD_WIDTH), jnp.bfloat16),
            pltpu.VMEM((HEAD_WIDTH, SLAB), jnp.bfloat16),
            pltpu.VMEM((SLAB, Q_COLS), jnp.bfloat16),
            pltpu.VMEM((SLAB, 2 * HEAD_WIDTH), jnp.float32),
            pltpu.SMEM((32,), jnp.int32),
            pltpu.SMEM((32,), jnp.int32),
        ],
        compiler_params=params(),
        cost_estimate=cost(10_000_000_000, 5_000_000),
    )(c_at, doc_ids[0], block_order, got)

    taken = lax.ppermute(send, "y", [(0, 1), (1, 0)])
    taken, got_x = lax.optimization_barrier((taken, got_x))
    own_cols = pl.pallas_call(
        pair_kernel,
        in_specs=[VMEM] * 2,
        out_specs=VMEM,
        out_shape=shape((4, SLAB, HEAD_WIDTH)),
        compiler_params=params(),
        cost_estimate=cost(0, 3_000_000),
    )(keep, taken)
    pieces = exchange(own_cols, "x")

    core, y = lax.rem(f, 2), c // 4
    kv_half, wg_send, wg_keep = pl.pallas_call(
        weight_kernel,
        in_specs=[SMEM] + [VMEM] * 2,
        out_specs=[VMEM] * 3,
        out_shape=[shape((SLAB, 512)), shape((320, 512)), shape((320, 512), jnp.float32)],
        scratch_shapes=[pltpu.VMEM((FEAT_TILE, SLAB), jnp.bfloat16)],
        compiler_params=params(),
        cost_estimate=cost(700_000_000, 5_000_000),
    )(core.reshape(1), pieces, got_x)

    wg_got = swap(wg_send, 0)
    parts = pl.pallas_call(
        input_kernel,
        in_specs=[SMEM] + [VMEM] * 4,
        out_specs=VMEM,
        out_shape=shape((CTX, FEAT_TILE + ROWS + Q_COLS, ROWS)),
        scratch_shapes=[pltpu.VMEM((FEAT_TILE, 512), jnp.bfloat16)],
        compiler_params=params(),
        cost_estimate=cost(700_000_000, 4_000_000),
    )(f.reshape(1), kv_half, weight_tile, own_cols, dq_parts)
    parts_got = exchange(parts, ("y", "x"))

    def halve(bit, keep, got, kind):
        rows = keep.shape[0] // 2
        return pl.pallas_call(
            halve_kernel,
            in_specs=[SMEM] + [VMEM] * 2,
            out_specs=[VMEM] * 2,
            out_shape=[shape((rows, 512), kind), shape((rows, 512), jnp.float32)],
            compiler_params=params(),
            cost_estimate=cost(0, rows * 512 * 16),
        )(bit.reshape(1), keep, got)

    for bit, kind in ((1, jnp.bfloat16), (2, jnp.bfloat16), (3, jnp.float32), (4, jnp.float32)):
        wg_send, wg_keep = halve((f >> bit) & 1, wg_keep, wg_got, kind)
        wg_got = swap(wg_send, bit)
    wg_send, wg_keep = halve(y, wg_keep, wg_got, jnp.float32)
    wg_got = lax.ppermute(wg_send, "y", [(0, 1), (1, 0)])
    weight_grad = pl.pallas_call(
        join_kernel,
        in_specs=[SMEM] + [VMEM] * 2,
        out_specs=VMEM,
        out_shape=shape((10, 1024), jnp.float32),
        compiler_params=params(),
        cost_estimate=cost(0, 100_000),
    )(y.reshape(1), wg_keep, wg_got)

    input_grad, query_grad, kv_rows = pl.pallas_call(
        out_kernel,
        in_specs=[VMEM],
        out_specs=[VMEM] * 3,
        out_shape=[shape((ROWS, FEATURES)), shape((ROWS, HQ * HEAD_WIDTH)), shape((ROWS, 1024))],
        compiler_params=params(),
        cost_estimate=cost(0, 5_000_000),
    )(parts_got)
    return (input_grad[None], query_grad[None], kv_rows[None], weight_grad)


def solution(mesh):
    axes = ("z", "yh", "core", "y", "x")
    named = jax.sharding.Mesh(mesh.devices.reshape(8, 2, 2, 2, 4), axes)
    fsdp, ctx = axes[:3], axes[3:]
    return jax.shard_map(
        body,
        mesh=named,
        in_specs=(P(fsdp, ctx, None),) * 5 + (P(fsdp, None), P(fsdp, None), P()),
        out_specs=(P(fsdp, ctx, None),) * 3 + (P(axes, None),),
        check_vma=False,
    )
```

```python
import functools
import math

import jax
import jax.numpy as jnp
from jax import lax
from jax.experimental import pallas as pl
from jax.experimental.pallas import tpu as pltpu
from jax.sharding import PartitionSpec as P

HQ = 32
KEY_VALUE_HEADS = 4
HEAD_WIDTH = 128
BLK = 32
QUERY_PER_KEY = 8

CTX = 8
FSDP = 32
ROWS = 128
SLAB = 1024
FEATURES = 2560
FEAT_TILE = FEATURES // 4
Q_COLS = 512
PACK_COLS = 2 * Q_COLS + 2 * HEAD_WIDTH
HALF = 512
SCALE = 1.0 / math.sqrt(HEAD_WIDTH)
LOG2E = math.log2(math.e)
LOWEST = -1e30
NN = (((1,), (0,)), ((), ()))
NT = (((1,), (1,)), ((), ()))
VMEM = pl.BlockSpec(memory_space=pltpu.VMEM)
HBM = pl.BlockSpec(memory_space=pltpu.HBM)
SMEM = pl.BlockSpec(memory_space=pltpu.SMEM)


def dot(a, b, dims):
    return lax.dot_general(a, b, dims, preferred_element_type=jnp.float32)


def shape(dims, kind=jnp.bfloat16):
    return jax.ShapeDtypeStruct(dims, kind)


def params(mib):
    return pltpu.CompilerParams(vmem_limit_bytes=mib * 1024 * 1024)


def cost(flops, moved):
    return pl.CostEstimate(flops=flops, bytes_accessed=moved, transcendentals=0)


def q_block(device):
    return (device % 4) * 2 + device // 4


def pack_kernel(q_ref, d_ref, k_ref, v_ref, out_ref, sems):
    copies = []
    for dest in range(CTX):
        at = q_block(dest) * Q_COLS
        head = (dest % 4) * HEAD_WIDTH
        place = 0
        for ref, first, width in (
            (q_ref, at, Q_COLS),
            (d_ref, at, Q_COLS),
            (k_ref, head, HEAD_WIDTH),
            (v_ref, head, HEAD_WIDTH),
        ):
            copy = pltpu.make_async_copy(
                ref.at[:, first : first + width],
                out_ref.at[dest, :, place : place + width],
                sems.at[len(copies)],
            )
            copy.start()
            copies.append(copy)
            place += width
    for copy in copies:
        copy.wait()


def tile_row(z, low, y):
    row = (low % 2) * 320 + (z % 2) * 160 + (z // 2 % 2) * 80 + (z // 4) * 40
    return row + (low // 2) * 20 + y * 10


def turn_kernel(x_ref, out_ref, turned, tile):
    for j in range(FEATURES // 128):
        block = x_ref[:, j * 128 : (j + 1) * 128].T
        turned[j * 128 : (j + 1) * 128, :] = block.astype(jnp.float32)
    for x in range(4):
        for low in range(4):
            for y in range(2):
                for z in range(8):
                    source = (z * 4 + low) * 80 + y * 40 + x * 10
                    at = tile_row(z, low, y)
                    tile[at : at + 10, :] = turned[source : source + 10, :]
        out_ref[x] = tile[...].astype(jnp.bfloat16)


def attention_kernel(c_ref, docs_ref, order_ref, *refs):
    in_ref, dq_ref, keep_ref, send_ref = refs[:4]
    q_s, d_s, k_s, v_s, kt_s, dq_s, dkv_s, place, begin = refs[4:]
    c = c_ref[0]

    first = lax.fori_loop(
        0, 17, lambda i, a: jnp.where(docs_ref[i] == docs_ref[i + 15], i, a), jnp.int32(0)
    )

    def place_block(st, carry):
        b = order_ref[st]
        inside = (b >= first) & (b < first + 16)
        place[st] = jnp.where(inside, b - first, jnp.where(b < first, b + 16, b))
        return carry

    lax.fori_loop(0, 32, place_block, 0)

    def begin_block(t, carry):
        last_doc, last_begin = carry
        doc = docs_ref[jnp.where(t < first, t, t + 16)]
        now = jnp.where(doc == last_doc, last_begin, t)
        begin[t] = jnp.int32(0)
        begin[t + 16] = now * BLK
        return doc, now

    lax.fori_loop(0, 16, begin_block, (jnp.int32(-1), jnp.int32(0)))

    for st in range(32):
        rows = pl.ds(pl.multiple_of(place[st] * BLK, BLK), BLK)
        src, block = st // 4, slice((st % 4) * BLK, (st % 4 + 1) * BLK)
        q_s[rows, :] = in_ref[src, block, 0:Q_COLS]
        d_s[rows, :] = in_ref[src, block, Q_COLS : 2 * Q_COLS]
        k_s[rows, :] = in_ref[src, block, 2 * Q_COLS : 2 * Q_COLS + HEAD_WIDTH]
        v_s[rows, :] = in_ref[src, block, 2 * Q_COLS + HEAD_WIDTH :]
    for j in range(SLAB // 128):
        kt_s[:, j * 128 : (j + 1) * 128] = k_s[j * 128 : (j + 1) * 128, :].T
    dkv_s[...] = jnp.zeros_like(dkv_s)

    def half(hf, carry):
        base = pl.multiple_of(hf * HALF, HALF)
        for i in range(HALF // 128):
            n = (i + 1) * 128
            rows = pl.ds(pl.multiple_of(base + i * 128, 128), 128)
            keys = pl.ds(base, n)
            key_n = k_s[keys, :]
            value_n = v_s[keys, :]
            lane = lax.broadcasted_iota(jnp.int32, (n, 128), 1)
            row = lax.broadcasted_iota(jnp.int32, (n, 128), 0)
            low = jnp.zeros((n, 128), jnp.int32)
            for kk in range(4):
                low = jnp.where(lane // BLK == kk, begin[hf * 16 + i * 4 + kk], low)
            seen = (row >= low) & (row <= lane + i * 128)
            bias = jnp.where(seen, 0.0, LOWEST)
            bias = jnp.concatenate([bias, bias], axis=1)
            for g in range(2):
                cols = [slice((2 * g + e) * 128, (2 * g + e + 1) * 128) for e in range(2)]
                qs = jnp.concatenate([q_s[rows, e] for e in cols], axis=0)
                ds = jnp.concatenate([d_s[rows, e] for e in cols], axis=0)
                scores = dot(key_n, qs, NT) * (SCALE * LOG2E) + bias
                top = jnp.max(scores, axis=0, keepdims=True)
                probs = jnp.exp2(scores - top)
                total = jnp.sum(probs, axis=0, keepdims=True)
                probs = probs * (1.0 / total)
                products = dot(value_n, ds, NT)
                delta = jnp.sum(probs * products, axis=0, keepdims=True)
                score_grad = (probs * (products - delta)).astype(jnp.bfloat16)
                probs_low = probs.astype(jnp.bfloat16)
                dkv_s[keys, 0:128] += dot(score_grad, qs, NN)
                dkv_s[keys, 128:256] += dot(probs_low, ds, NN)
                dqt = dot(kt_s[:, keys], score_grad, NN) * SCALE
                for e in range(2):
                    dq_s[rows, cols[e]] = dqt[:, e * 128 : (e + 1) * 128].T.astype(jnp.bfloat16)
        return carry

    lax.fori_loop(0, 2, half, 0)

    y = c // 4
    for t in range(16):
        block = slice(t * BLK, (t + 1) * BLK)
        for half_y, ref in ((y, keep_ref), (1 - y, send_ref)):
            rows = pl.ds(pl.multiple_of(place[half_y * 16 + t] * BLK, BLK), BLK)
            ref[block, 0:128] = (dkv_s[rows, 0:128] * SCALE).astype(ref.dtype)
            ref[block, 128:256] = dkv_s[rows, 128:256].astype(ref.dtype)
    for st in range(32):
        rows = pl.ds(pl.multiple_of(place[st] * BLK, BLK), BLK)
        dq_ref[st // 4, (st % 4) * BLK : (st % 4 + 1) * BLK, :] = dq_s[rows, :]


def pair_kernel(keep_ref, taken_ref, out_ref):
    total = (keep_ref[...] + taken_ref[...].astype(jnp.float32)).astype(jnp.bfloat16)
    for dest in range(4):
        out_ref[dest] = total


def weight_kernel(at_ref, pieces_ref, x_ref, kv_ref, kv_rows_ref, send_ref, keep_ref, x_s):
    core, x = at_ref[0], at_ref[1]
    for src in range(4):
        kv_ref[:, src * 128 : (src + 1) * 128] = pieces_ref[src, :, 0:128]
        kv_ref[:, 512 + src * 128 : 512 + (src + 1) * 128] = pieces_ref[src, :, 128:256]
        x_s[:, src * 128 : (src + 1) * 128] = x_ref[src]
    part = FEAT_TILE // 2
    other = pl.ds(pl.multiple_of((1 - core) * part, part), part)
    own = pl.ds(pl.multiple_of(core * part, part), part)
    for j in range(4):
        cols = slice(j * 256, (j + 1) * 256)
        send_ref[:, cols] = dot(x_s[other, :], kv_ref[:, cols], NN).astype(jnp.bfloat16)
        keep_ref[:, cols] = dot(x_s[own, :], kv_ref[:, cols], NN)
    kv_rows_ref[...] = kv_ref[pl.ds(pl.multiple_of(x * ROWS, ROWS), ROWS), :]


def halve_kernel(bit_ref, keep_ref, got_ref, send_ref, kept_ref):
    part = kept_ref.shape[0]
    total = keep_ref[...] + got_ref[...].astype(jnp.float32)
    low, high, upper = total[:part, :], total[part:, :], bit_ref[0] == 1
    send_ref[...] = jnp.where(upper, low, high).astype(send_ref.dtype)
    kept_ref[...] = jnp.where(upper, high, low)


def input_kernel(f_ref, kv_ref, w_ref, out_ref, w_s):
    for at in range(FSDP):
        mask = sum(((at >> i) & 1) << bit for i, bit in enumerate(GATHER_BITS))
        source = f_ref[0] ^ mask
        rows = pl.ds(pl.multiple_of((source // 4) * 80, 80), 80)
        cols = pl.ds(pl.multiple_of(lax.rem(source, 4) * 256, 256), 256)
        w_s[rows, cols] = w_ref[at]
    for j in range(2):
        rows = slice(j * 256, (j + 1) * 256)
        tile = dot(w_s[...], kv_ref[rows, :], NT).astype(jnp.bfloat16)
        out_ref[2 * j] = tile[:, 0:128]
        out_ref[2 * j + 1] = tile[:, 128:256]


def input_out_kernel(parts_ref, out_ref):
    for x in range(4):
        for j in range(FEAT_TILE // 128):
            at = x * FEAT_TILE + j * 128
            out_ref[:, at : at + 128] = parts_ref[x, j * 128 : (j + 1) * 128, :].T


def query_out_kernel(dq_ref, out_ref):
    for src in range(CTX):
        at = q_block(src) * Q_COLS
        out_ref[:, at : at + Q_COLS] = dq_ref[src]


GATHER_BITS = (1, 4, 3, 2, 0)
BIT_AXES = (("core", 1), ("yh", 1), ("z", 1), ("z", 2), ("z", 4))


def swap(value, bit):
    axis, mask = BIT_AXES[bit]
    return lax.ppermute(value, axis, [(i, i ^ mask) for i in range(8 if axis == "z" else 2)])


def exchange(value, axis):
    return lax.all_to_all(value, axis, 0, 0, tiled=True)


def body(inputs, queries, keys, values, output_cotangent, key_value_weight, doc_ids, block_order):
    f = lax.axis_index(("z", "yh", "core")).astype(jnp.int32)
    y, x = lax.axis_index("y").astype(jnp.int32), lax.axis_index("x").astype(jnp.int32)
    c_at = (y * 4 + x).reshape(1)

    tile = lax.dynamic_slice(key_value_weight, (0, x * 256), (80, 256))
    perm = []
    for f1 in range(FSDP):
        for c1 in range(CTX):
            y1, x1 = c1 // 4, c1 % 4
            perm.append((f1 * CTX + c1, ((f1 % 8) * 4 + x1) * CTX + y1 * 4 + f1 // 8))
    tile = lax.ppermute(tile, ("z", "yh", "core", "y", "x"), perm)[None]

    def widen(tile, bit):
        return jnp.concatenate([tile, swap(tile, bit)], axis=0)

    tile = widen(tile, GATHER_BITS[0])

    packed = pl.pallas_call(
        pack_kernel,
        in_specs=[HBM] * 4,
        out_specs=HBM,
        out_shape=shape((CTX, ROWS, PACK_COLS)),
        scratch_shapes=[pltpu.SemaphoreType.DMA((4 * CTX,))],
        cost_estimate=cost(0, 5_000_000),
    )(queries[0], output_cotangent[0], keys[0], values[0])
    packed, tile = lax.optimization_barrier((packed, tile))
    got = exchange(packed, ("y", "x"))
    tile = widen(widen(tile, GATHER_BITS[1]), GATHER_BITS[2])

    turned = pl.pallas_call(
        turn_kernel,
        in_specs=[VMEM],
        out_specs=VMEM,
        out_shape=shape((4, FEAT_TILE, ROWS)),
        scratch_shapes=[
            pltpu.VMEM((FEATURES, ROWS), jnp.float32),
            pltpu.VMEM((FEAT_TILE, ROWS), jnp.float32),
        ],
        compiler_params=params(8),
        cost_estimate=cost(0, 1_300_000),
    )(inputs[0])

    got, turned, tile = lax.optimization_barrier((got, turned, tile))
    got_x = exchange(turned, "x")
    weight_tile = widen(widen(tile, GATHER_BITS[3]), GATHER_BITS[4])

    dq_parts, keep, send = pl.pallas_call(
        attention_kernel,
        in_specs=[SMEM] * 3 + [VMEM],
        out_specs=[VMEM] * 3,
        out_shape=[
            shape((CTX, ROWS, Q_COLS)),
            shape((SLAB // 2, 2 * HEAD_WIDTH), jnp.float32),
            shape((SLAB // 2, 2 * HEAD_WIDTH)),
        ],
        scratch_shapes=[
            pltpu.VMEM((SLAB, Q_COLS), jnp.bfloat16),
            pltpu.VMEM((SLAB, Q_COLS), jnp.bfloat16),
            pltpu.VMEM((SLAB, HEAD_WIDTH), jnp.bfloat16),
            pltpu.VMEM((SLAB, HEAD_WIDTH), jnp.bfloat16),
            pltpu.VMEM((HEAD_WIDTH, SLAB), jnp.bfloat16),
            pltpu.VMEM((SLAB, Q_COLS), jnp.bfloat16),
            pltpu.VMEM((SLAB, 2 * HEAD_WIDTH), jnp.float32),
            pltpu.SMEM((32,), jnp.int32),
            pltpu.SMEM((32,), jnp.int32),
        ],
        compiler_params=params(24),
        cost_estimate=cost(10_000_000_000, 5_000_000),
    )(c_at, doc_ids[0], block_order, got)

    taken = lax.ppermute(send, "y", [(0, 1), (1, 0)])
    taken, got_x, weight_tile = lax.optimization_barrier((taken, got_x, weight_tile))
    own_cols = pl.pallas_call(
        pair_kernel,
        in_specs=[VMEM] * 2,
        out_specs=VMEM,
        out_shape=shape((4, SLAB // 2, 2 * HEAD_WIDTH)),
        compiler_params=params(6),
        cost_estimate=cost(0, 2_000_000),
    )(keep, taken)
    pieces = exchange(own_cols, "x")
    pieces, dq_parts = lax.optimization_barrier((pieces, dq_parts))
    dq_got = exchange(dq_parts, ("y", "x"))

    kv_half, kv_rows, wg_send, wg_keep = pl.pallas_call(
        weight_kernel,
        in_specs=[SMEM] + [VMEM] * 2,
        out_specs=[VMEM] * 4,
        out_shape=[
            shape((SLAB // 2, 1024)),
            shape((ROWS, 1024)),
            shape((FEAT_TILE // 2, 1024)),
            shape((FEAT_TILE // 2, 1024), jnp.float32),
        ],
        scratch_shapes=[pltpu.VMEM((FEAT_TILE, SLAB // 2), jnp.bfloat16)],
        compiler_params=params(12),
        cost_estimate=cost(700_000_000, 6_000_000),
    )(jnp.stack([lax.rem(f, 2), x]), pieces, got_x)

    wg_got = swap(wg_send, 0)
    parts = pl.pallas_call(
        input_kernel,
        in_specs=[SMEM] + [VMEM] * 2,
        out_specs=VMEM,
        out_shape=shape((4, FEAT_TILE, ROWS)),
        scratch_shapes=[pltpu.VMEM((FEAT_TILE, 1024), jnp.bfloat16)],
        compiler_params=params(12),
        cost_estimate=cost(700_000_000, 4_000_000),
    )(f.reshape(1), kv_half, weight_tile)
    ig_got = exchange(parts, "x")

    def halve(bit, keep, got, kind):
        rows = keep.shape[0] // 2
        return pl.pallas_call(
            halve_kernel,
            in_specs=[SMEM] + [VMEM] * 2,
            out_specs=[VMEM] * 2,
            out_shape=[shape((rows, 1024), kind), shape((rows, 1024), jnp.float32)],
            compiler_params=params(6),
            cost_estimate=cost(0, rows * 1024 * 16),
        )(bit.reshape(1), keep, got)

    for bit, kind in ((2, jnp.bfloat16), (3, jnp.bfloat16), (4, jnp.bfloat16), (1, jnp.float32)):
        wg_send, wg_keep = halve((f >> bit) & 1, wg_keep, wg_got, kind)
        wg_got = swap(wg_send, bit)
    wg_send, wg_keep = halve(y, wg_keep, wg_got, jnp.float32)
    weight_grad = wg_keep + lax.ppermute(wg_send, "y", [(0, 1), (1, 0)])

    query_grad = pl.pallas_call(
        query_out_kernel,
        in_specs=[VMEM],
        out_specs=VMEM,
        out_shape=shape((ROWS, HQ * HEAD_WIDTH)),
        compiler_params=params(6),
        cost_estimate=cost(0, 2_000_000),
    )(dq_got)
    input_grad = pl.pallas_call(
        input_out_kernel,
        in_specs=[VMEM],
        out_specs=VMEM,
        out_shape=shape((ROWS, FEATURES)),
        compiler_params=params(6),
        cost_estimate=cost(0, 1_300_000),
    )(ig_got)
    return (input_grad[None], query_grad[None], kv_rows[None], weight_grad)


def solution(mesh):
    axes = ("z", "yh", "core", "y", "x")
    named = jax.sharding.Mesh(mesh.devices.reshape(8, 2, 2, 2, 4), axes)
    fsdp, ctx = axes[:3], axes[3:]
    return jax.shard_map(
        body,
        mesh=named,
        in_specs=(P(fsdp, ctx, None),) * 5 + (P(fsdp, None), P(fsdp, None), P()),
        out_specs=(P(fsdp, ctx, None),) * 3 + (P(axes, None),),
        check_vma=False,
    )
```

```python
import functools
import math

import jax
import jax.numpy as jnp
from jax import lax
from jax.experimental import pallas as pl
from jax.experimental.pallas import tpu as pltpu
from jax.sharding import PartitionSpec as P

HQ = 32
KEY_VALUE_HEADS = 4
HEAD_WIDTH = 128
BLK = 32
QUERY_PER_KEY = 8

CTX = 8
FSDP = 32
ROWS = 128
SLAB = 1024
FEATURES = 2560
FEAT_TILE = FEATURES // 4
Q_COLS = 512
PACK_COLS = 2 * Q_COLS + 2 * HEAD_WIDTH
HALF = 512
SCALE = 1.0 / math.sqrt(HEAD_WIDTH)
LOG2E = math.log2(math.e)
LOWEST = -1e30
NN = (((1,), (0,)), ((), ()))
NT = (((1,), (1,)), ((), ()))
VMEM = pl.BlockSpec(memory_space=pltpu.VMEM)
HBM = pl.BlockSpec(memory_space=pltpu.HBM)
SMEM = pl.BlockSpec(memory_space=pltpu.SMEM)


def dot(a, b, dims):
    return lax.dot_general(a, b, dims, preferred_element_type=jnp.float32)


def shape(dims, kind=jnp.bfloat16):
    return jax.ShapeDtypeStruct(dims, kind)


def params(mib):
    return pltpu.CompilerParams(vmem_limit_bytes=mib * 1024 * 1024)


def cost(flops, moved):
    return pl.CostEstimate(flops=flops, bytes_accessed=moved, transcendentals=0)


def q_block(device):
    return (device % 4) * 2 + device // 4


def pack_kernel(q_ref, d_ref, k_ref, v_ref, out_ref, sems):
    copies = []
    for dest in range(CTX):
        at = q_block(dest) * Q_COLS
        head = (dest % 4) * HEAD_WIDTH
        place = 0
        for ref, first, width in (
            (q_ref, at, Q_COLS),
            (d_ref, at, Q_COLS),
            (k_ref, head, HEAD_WIDTH),
            (v_ref, head, HEAD_WIDTH),
        ):
            copy = pltpu.make_async_copy(
                ref.at[:, first : first + width],
                out_ref.at[dest, :, place : place + width],
                sems.at[len(copies)],
            )
            copy.start()
            copies.append(copy)
            place += width
    for copy in copies:
        copy.wait()


def tile_row(z, low, y):
    row = (low % 2) * 320 + (z % 2) * 160 + (z // 2 % 2) * 80 + (z // 4) * 40
    return row + (low // 2) * 20 + y * 10


def turn_kernel(x_ref, in_ref, *refs):
    outs, turned, tile = refs[:4], refs[4], refs[5]
    for j in range(FEATURES // 128):
        block = in_ref[:, j * 128 : (j + 1) * 128].T
        turned[j * 128 : (j + 1) * 128, :] = block.astype(jnp.float32)
    for x in range(4):
        for low in range(4):
            for y in range(2):
                for z in range(8):
                    source = (z * 4 + low) * 80 + y * 40 + x * 10
                    at = tile_row(z, low, y)
                    tile[x, at : at + 10, :] = turned[source : source + 10, :]
    for s in range(4):
        outs[s][...] = tile[lax.rem(x_ref[0] + s, 4)].astype(jnp.bfloat16)


def attention_kernel(c_ref, docs_ref, order_ref, *refs):
    in_ref, dq_ref, keep_ref, send_ref = refs[:4]
    q_s, d_s, k_s, v_s, kt_s, dq_s, dkv_s, place, begin = refs[4:]
    c = c_ref[0]

    first = lax.fori_loop(
        0, 17, lambda i, a: jnp.where(docs_ref[i] == docs_ref[i + 15], i, a), jnp.int32(0)
    )

    def place_block(st, carry):
        b = order_ref[st]
        inside = (b >= first) & (b < first + 16)
        place[st] = jnp.where(inside, b - first, jnp.where(b < first, b + 16, b))
        return carry

    lax.fori_loop(0, 32, place_block, 0)

    def begin_block(t, carry):
        last_doc, last_begin = carry
        doc = docs_ref[jnp.where(t < first, t, t + 16)]
        now = jnp.where(doc == last_doc, last_begin, t)
        begin[t] = jnp.int32(0)
        begin[t + 16] = now * BLK
        return doc, now

    lax.fori_loop(0, 16, begin_block, (jnp.int32(-1), jnp.int32(0)))

    for st in range(32):
        rows = pl.ds(pl.multiple_of(place[st] * BLK, BLK), BLK)
        src, block = st // 4, slice((st % 4) * BLK, (st % 4 + 1) * BLK)
        q_s[rows, :] = in_ref[src, block, 0:Q_COLS]
        d_s[rows, :] = in_ref[src, block, Q_COLS : 2 * Q_COLS]
        k_s[rows, :] = in_ref[src, block, 2 * Q_COLS : 2 * Q_COLS + HEAD_WIDTH]
        v_s[rows, :] = in_ref[src, block, 2 * Q_COLS + HEAD_WIDTH :]
    for j in range(SLAB // 128):
        kt_s[:, j * 128 : (j + 1) * 128] = k_s[j * 128 : (j + 1) * 128, :].T
    dkv_s[...] = jnp.zeros_like(dkv_s)

    def half(hf, carry):
        base = pl.multiple_of(hf * HALF, HALF)
        for i in range(HALF // 128):
            n = (i + 1) * 128
            rows = pl.ds(pl.multiple_of(base + i * 128, 128), 128)
            keys = pl.ds(base, n)
            key_n = k_s[keys, :]
            value_n = v_s[keys, :]
            lane = lax.broadcasted_iota(jnp.int32, (n, 128), 1)
            row = lax.broadcasted_iota(jnp.int32, (n, 128), 0)
            low = jnp.zeros((n, 128), jnp.int32)
            for kk in range(4):
                low = jnp.where(lane // BLK == kk, begin[hf * 16 + i * 4 + kk], low)
            seen = (row >= low) & (row <= lane + i * 128)
            bias = jnp.where(seen, 0.0, LOWEST)
            bias = jnp.concatenate([bias, bias], axis=1)
            for g in range(2):
                cols = [slice((2 * g + e) * 128, (2 * g + e + 1) * 128) for e in range(2)]
                qs = jnp.concatenate([q_s[rows, e] for e in cols], axis=0)
                ds = jnp.concatenate([d_s[rows, e] for e in cols], axis=0)
                scores = dot(key_n, qs, NT) * (SCALE * LOG2E) + bias
                top = jnp.max(scores, axis=0, keepdims=True)
                probs = jnp.exp2(scores - top)
                total = jnp.sum(probs, axis=0, keepdims=True)
                probs = probs * (1.0 / total)
                products = dot(value_n, ds, NT)
                delta = jnp.sum(probs * products, axis=0, keepdims=True)
                score_grad = (probs * (products - delta)).astype(jnp.bfloat16)
                probs_low = probs.astype(jnp.bfloat16)
                dkv_s[keys, 0:128] += dot(score_grad, qs, NN)
                dkv_s[keys, 128:256] += dot(probs_low, ds, NN)
                dqt = dot(kt_s[:, keys], score_grad, NN) * SCALE
                for e in range(2):
                    dq_s[rows, cols[e]] = dqt[:, e * 128 : (e + 1) * 128].T.astype(jnp.bfloat16)
        return carry

    lax.fori_loop(0, 2, half, 0)

    y = c // 4
    for t in range(16):
        block = slice(t * BLK, (t + 1) * BLK)
        for half_y, ref in ((y, keep_ref), (1 - y, send_ref)):
            rows = pl.ds(pl.multiple_of(place[half_y * 16 + t] * BLK, BLK), BLK)
            ref[block, 0:128] = (dkv_s[rows, 0:128] * SCALE).astype(ref.dtype)
            ref[block, 128:256] = dkv_s[rows, 128:256].astype(ref.dtype)
    for st in range(32):
        rows = pl.ds(pl.multiple_of(place[st] * BLK, BLK), BLK)
        dq_ref[st // 4, (st % 4) * BLK : (st % 4 + 1) * BLK, :] = dq_s[rows, :]


def pair_kernel(keep_ref, taken_ref, out_ref):
    out_ref[...] = (keep_ref[...] + taken_ref[...].astype(jnp.float32)).astype(jnp.bfloat16)


def weight_kernel(at_ref, *refs):
    pieces, ins = refs[:4], refs[4:8]
    kv_ref, kv_rows_ref, send_ref, keep_ref, x_s = refs[8:]
    core, x = at_ref[0], at_ref[1]
    for s in range(4):
        at = pl.multiple_of(lax.rem(x + 4 - s, 4) * 128, 128)
        kv_ref[:, pl.ds(at, 128)] = pieces[s][:, 0:128]
        kv_ref[:, pl.ds(pl.multiple_of(512 + at, 128), 128)] = pieces[s][:, 128:256]
        x_s[:, pl.ds(at, 128)] = ins[s][...]
    part = FEAT_TILE // 2
    other = pl.ds(pl.multiple_of((1 - core) * part, part), part)
    own = pl.ds(pl.multiple_of(core * part, part), part)
    for j in range(4):
        cols = slice(j * 256, (j + 1) * 256)
        send_ref[:, cols] = dot(x_s[other, :], kv_ref[:, cols], NN).astype(jnp.bfloat16)
        keep_ref[:, cols] = dot(x_s[own, :], kv_ref[:, cols], NN)
    kv_rows_ref[...] = kv_ref[pl.ds(pl.multiple_of(x * ROWS, ROWS), ROWS), :]


def halve_kernel(bit_ref, keep_ref, got_ref, send_ref, kept_ref):
    part = kept_ref.shape[0]
    total = keep_ref[...] + got_ref[...].astype(jnp.float32)
    low, high, upper = total[:part, :], total[part:, :], bit_ref[0] == 1
    send_ref[...] = jnp.where(upper, low, high).astype(send_ref.dtype)
    kept_ref[...] = jnp.where(upper, high, low)


def input_kernel(f_ref, kv_ref, w_ref, far_ref, out_ref, w_s):
    for at in range(FSDP):
        mask = sum(((at >> i) & 1) << bit for i, bit in enumerate(GATHER_BITS))
        source = f_ref[0] ^ mask
        rows = pl.ds(pl.multiple_of((source // 4) * 80, 80), 80)
        cols = pl.ds(pl.multiple_of(lax.rem(source, 4) * 256, 256), 256)
        w_s[rows, cols] = w_ref[at] if at < FSDP // 2 else far_ref[at - FSDP // 2]
    for j in range(2):
        rows = slice(j * 256, (j + 1) * 256)
        tile = dot(w_s[...], kv_ref[rows, :], NT).astype(jnp.bfloat16)
        out_ref[2 * j] = tile[:, 0:128]
        out_ref[2 * j + 1] = tile[:, 128:256]


def input_out_kernel(parts_ref, out_ref):
    for x in range(4):
        for j in range(FEAT_TILE // 128):
            at = x * FEAT_TILE + j * 128
            out_ref[:, at : at + 128] = parts_ref[x, j * 128 : (j + 1) * 128, :].T


def query_out_kernel(dq_ref, out_ref):
    for src in range(CTX):
        at = q_block(src) * Q_COLS
        out_ref[:, at : at + Q_COLS] = dq_ref[src]


GATHER_BITS = (4, 3, 2, 0, 1)
BIT_AXES = (("core", 1), ("yh", 1), ("z", 1), ("z", 2), ("z", 4))


def swap(value, bit):
    axis, mask = BIT_AXES[bit]
    return lax.ppermute(value, axis, [(i, i ^ mask) for i in range(8 if axis == "z" else 2)])


def to_shift(value, s):
    return lax.ppermute(value, "x", [(i, (i + s) % 4) for i in range(4)]) if s else value


def exchange(value, axis):
    return lax.all_to_all(value, axis, 0, 0, tiled=True)


def body(inputs, queries, keys, values, output_cotangent, key_value_weight, doc_ids, block_order):
    f = lax.axis_index(("z", "yh", "core")).astype(jnp.int32)
    y, x = lax.axis_index("y").astype(jnp.int32), lax.axis_index("x").astype(jnp.int32)
    c_at = (y * 4 + x).reshape(1)

    tile = lax.dynamic_slice(key_value_weight, (0, x * 256), (80, 256))
    perm = []
    for f1 in range(FSDP):
        for c1 in range(CTX):
            y1, x1 = c1 // 4, c1 % 4
            perm.append((f1 * CTX + c1, ((f1 % 8) * 4 + x1) * CTX + y1 * 4 + f1 // 8))
    tile = lax.ppermute(tile, ("z", "yh", "core", "y", "x"), perm)[None]

    def widen(tile, bit):
        return jnp.concatenate([tile, swap(tile, bit)], axis=0)

    packed = pl.pallas_call(
        pack_kernel,
        in_specs=[HBM] * 4,
        out_specs=VMEM,
        out_shape=shape((CTX, ROWS, PACK_COLS)),
        scratch_shapes=[pltpu.SemaphoreType.DMA((4 * CTX,))],
        compiler_params=params(6),
        cost_estimate=cost(0, 5_000_000),
    )(queries[0], output_cotangent[0], keys[0], values[0])
    packed, tile = lax.optimization_barrier((packed, tile))
    got = exchange(packed, ("y", "x"))
    for bit in GATHER_BITS[:4]:
        tile = widen(tile, bit)

    turned = pl.pallas_call(
        turn_kernel,
        in_specs=[SMEM, VMEM],
        out_specs=[VMEM] * 4,
        out_shape=[shape((FEAT_TILE, ROWS))] * 4,
        scratch_shapes=[
            pltpu.VMEM((FEATURES, ROWS), jnp.float32),
            pltpu.VMEM((4, FEAT_TILE, ROWS), jnp.float32),
        ],
        compiler_params=params(8),
        cost_estimate=cost(0, 1_300_000),
    )(x.reshape(1), inputs[0])

    got, turned, tile = lax.optimization_barrier((got, turned, tile))
    got_x = [to_shift(turned[s], s) for s in range(4)]

    dq_parts, keep, send = pl.pallas_call(
        attention_kernel,
        in_specs=[SMEM] * 3 + [VMEM],
        out_specs=[VMEM] * 3,
        out_shape=[
            shape((CTX, ROWS, Q_COLS)),
            shape((SLAB // 2, 2 * HEAD_WIDTH), jnp.float32),
            shape((SLAB // 2, 2 * HEAD_WIDTH)),
        ],
        scratch_shapes=[
            pltpu.VMEM((SLAB, Q_COLS), jnp.bfloat16),
            pltpu.VMEM((SLAB, Q_COLS), jnp.bfloat16),
            pltpu.VMEM((SLAB, HEAD_WIDTH), jnp.bfloat16),
            pltpu.VMEM((SLAB, HEAD_WIDTH), jnp.bfloat16),
            pltpu.VMEM((HEAD_WIDTH, SLAB), jnp.bfloat16),
            pltpu.VMEM((SLAB, Q_COLS), jnp.bfloat16),
            pltpu.VMEM((SLAB, 2 * HEAD_WIDTH), jnp.float32),
            pltpu.SMEM((32,), jnp.int32),
            pltpu.SMEM((32,), jnp.int32),
        ],
        compiler_params=params(24),
        cost_estimate=cost(10_000_000_000, 5_000_000),
    )(c_at, doc_ids[0], block_order, got)

    taken = lax.ppermute(send, "y", [(0, 1), (1, 0)])
    taken, got_x, tile = lax.optimization_barrier((taken, got_x, tile))
    far_tile = swap(tile, GATHER_BITS[4])
    own_cols = pl.pallas_call(
        pair_kernel,
        in_specs=[VMEM] * 2,
        out_specs=VMEM,
        out_shape=shape((SLAB // 2, 2 * HEAD_WIDTH)),
        compiler_params=params(6),
        cost_estimate=cost(0, 2_000_000),
    )(keep, taken)
    pieces = [to_shift(own_cols, s) for s in range(4)]
    pieces, far_tile = lax.optimization_barrier((pieces, far_tile))

    kv_half, kv_rows, wg_send, wg_keep = pl.pallas_call(
        weight_kernel,
        in_specs=[SMEM] + [VMEM] * 8,
        out_specs=[VMEM] * 4,
        out_shape=[
            shape((SLAB // 2, 1024)),
            shape((ROWS, 1024)),
            shape((FEAT_TILE // 2, 1024)),
            shape((FEAT_TILE // 2, 1024), jnp.float32),
        ],
        scratch_shapes=[pltpu.VMEM((FEAT_TILE, SLAB // 2), jnp.bfloat16)],
        compiler_params=params(12),
        cost_estimate=cost(700_000_000, 6_000_000),
    )(jnp.stack([lax.rem(f, 2), x]), *pieces, *got_x)

    wg_got = swap(wg_send, 0)
    parts = pl.pallas_call(
        input_kernel,
        in_specs=[SMEM] + [VMEM] * 3,
        out_specs=VMEM,
        out_shape=shape((4, FEAT_TILE, ROWS)),
        scratch_shapes=[pltpu.VMEM((FEAT_TILE, 1024), jnp.bfloat16)],
        compiler_params=params(12),
        cost_estimate=cost(700_000_000, 4_000_000),
    )(f.reshape(1), kv_half, tile, far_tile)
    parts, dq_parts = lax.optimization_barrier((parts, dq_parts))
    dq_got = exchange(dq_parts, ("y", "x"))

    def halve(bit, keep, got, kind):
        rows = keep.shape[0] // 2
        return pl.pallas_call(
            halve_kernel,
            in_specs=[SMEM] + [VMEM] * 2,
            out_specs=[VMEM] * 2,
            out_shape=[shape((rows, 1024), kind), shape((rows, 1024), jnp.float32)],
            compiler_params=params(6),
            cost_estimate=cost(0, rows * 1024 * 16),
        )(bit.reshape(1), keep, got)

    for bit, kind in ((2, jnp.bfloat16), (3, jnp.bfloat16), (4, jnp.bfloat16), (1, jnp.float32)):
        wg_send, wg_keep = halve((f >> bit) & 1, wg_keep, wg_got, kind)
        wg_got = swap(wg_send, bit)
        if bit == 3:
            wg_got, parts = lax.optimization_barrier((wg_got, parts))
            ig_got = exchange(parts, "x")
    wg_send, wg_keep = halve(y, wg_keep, wg_got, jnp.float32)
    weight_grad = wg_keep + lax.ppermute(wg_send, "y", [(0, 1), (1, 0)])

    query_grad = pl.pallas_call(
        query_out_kernel,
        in_specs=[VMEM],
        out_specs=VMEM,
        out_shape=shape((ROWS, HQ * HEAD_WIDTH)),
        compiler_params=params(6),
        cost_estimate=cost(0, 2_000_000),
    )(dq_got)
    input_grad = pl.pallas_call(
        input_out_kernel,
        in_specs=[VMEM],
        out_specs=VMEM,
        out_shape=shape((ROWS, FEATURES)),
        compiler_params=params(6),
        cost_estimate=cost(0, 1_300_000),
    )(ig_got)
    return (input_grad[None], query_grad[None], kv_rows[None], weight_grad)


def solution(mesh):
    axes = ("z", "yh", "core", "y", "x")
    named = jax.sharding.Mesh(mesh.devices.reshape(8, 2, 2, 2, 4), axes)
    fsdp, ctx = axes[:3], axes[3:]
    return jax.shard_map(
        body,
        mesh=named,
        in_specs=(P(fsdp, ctx, None),) * 5 + (P(fsdp, None), P(fsdp, None), P()),
        out_specs=(P(fsdp, ctx, None),) * 3 + (P(axes, None),),
        check_vma=False,
    )
```

```python
import functools
import math

import jax
import jax.numpy as jnp
from jax import lax
from jax.experimental import pallas as pl
from jax.experimental.pallas import tpu as pltpu
from jax.sharding import PartitionSpec as P

HQ = 32
KEY_VALUE_HEADS = 4
HEAD_WIDTH = 128
BLK = 32
QUERY_PER_KEY = 8

CTX = 8
FSDP = 32
ROWS = 128
SLAB = 1024
FEATURES = 2560
FEAT_TILE = FEATURES // 4
Q_COLS = 512
PACK_COLS = 2 * Q_COLS + 2 * HEAD_WIDTH
HALF = 512
SCALE = 1.0 / math.sqrt(HEAD_WIDTH)
LOG2E = math.log2(math.e)
LOWEST = -1e30
NN = (((1,), (0,)), ((), ()))
NT = (((1,), (1,)), ((), ()))
VMEM = pl.BlockSpec(memory_space=pltpu.VMEM)
HBM = pl.BlockSpec(memory_space=pltpu.HBM)
SMEM = pl.BlockSpec(memory_space=pltpu.SMEM)


def dot(a, b, dims):
    return lax.dot_general(a, b, dims, preferred_element_type=jnp.float32)


def shape(dims, kind=jnp.bfloat16):
    return jax.ShapeDtypeStruct(dims, kind)


def params(mib):
    return pltpu.CompilerParams(vmem_limit_bytes=mib * 1024 * 1024)


def cost(flops, moved):
    return pl.CostEstimate(flops=flops, bytes_accessed=moved, transcendentals=0)


def q_block(device):
    return (device % 4) * 2 + device // 4


def pack_kernel(q_ref, d_ref, k_ref, v_ref, out_ref, sems):
    copies = []
    for dest in range(CTX):
        at = q_block(dest) * Q_COLS
        head = (dest % 4) * HEAD_WIDTH
        place = 0
        for ref, first, width in (
            (q_ref, at, Q_COLS),
            (d_ref, at, Q_COLS),
            (k_ref, head, HEAD_WIDTH),
            (v_ref, head, HEAD_WIDTH),
        ):
            copy = pltpu.make_async_copy(
                ref.at[:, first : first + width],
                out_ref.at[dest, :, place : place + width],
                sems.at[len(copies)],
            )
            copy.start()
            copies.append(copy)
            place += width
    for copy in copies:
        copy.wait()


def tile_row(z, low, y):
    row = (low % 2) * 320 + y * 160 + (low // 2) * 80
    return row + (z % 2) * 40 + (z // 2 % 2) * 20 + (z // 4) * 10


def turn_kernel(in_ref, *refs):
    outs, turned, tile = refs[:4], refs[4], refs[5]
    for j in range(FEATURES // 128):
        block = in_ref[:, j * 128 : (j + 1) * 128].T
        turned[j * 128 : (j + 1) * 128, :] = block.astype(jnp.float32)
    for x in range(4):
        for low in range(4):
            for y in range(2):
                for z in range(8):
                    source = (z * 4 + low) * 80 + y * 40 + x * 10
                    at = tile_row(z, low, y)
                    tile[x, at : at + 10, :] = turned[source : source + 10, :]
    for s in range(4):
        outs[s][...] = tile[lax.rem(lax.axis_index("x") + s, 4)].astype(jnp.bfloat16)


def attention_kernel(docs_ref, order_ref, *refs):
    in_ref, dq_ref, keep_ref, send_ref = refs[:4]
    q_s, d_s, k_s, v_s, kt_s, dq_s, dkv_s, place, begin = refs[4:]

    first = lax.fori_loop(
        0, 17, lambda i, a: jnp.where(docs_ref[i] == docs_ref[i + 15], i, a), jnp.int32(0)
    )

    def place_block(st, carry):
        b = order_ref[st]
        inside = (b >= first) & (b < first + 16)
        place[st] = jnp.where(inside, b - first, jnp.where(b < first, b + 16, b))
        return carry

    lax.fori_loop(0, 32, place_block, 0)

    def begin_block(t, carry):
        last_doc, last_begin = carry
        doc = docs_ref[jnp.where(t < first, t, t + 16)]
        now = jnp.where(doc == last_doc, last_begin, t)
        begin[t] = jnp.int32(0)
        begin[t + 16] = now * BLK
        return doc, now

    lax.fori_loop(0, 16, begin_block, (jnp.int32(-1), jnp.int32(0)))

    for st in range(32):
        rows = pl.ds(pl.multiple_of(place[st] * BLK, BLK), BLK)
        src, block = st // 4, slice((st % 4) * BLK, (st % 4 + 1) * BLK)
        q_s[rows, :] = in_ref[src, block, 0:Q_COLS]
        d_s[rows, :] = in_ref[src, block, Q_COLS : 2 * Q_COLS]
        k_s[rows, :] = in_ref[src, block, 2 * Q_COLS : 2 * Q_COLS + HEAD_WIDTH]
        v_s[rows, :] = in_ref[src, block, 2 * Q_COLS + HEAD_WIDTH :]
    for j in range(SLAB // 128):
        kt_s[:, j * 128 : (j + 1) * 128] = k_s[j * 128 : (j + 1) * 128, :].T
    dkv_s[...] = jnp.zeros_like(dkv_s)

    def half(hf, carry):
        base = pl.multiple_of(hf * HALF, HALF)
        for i in range(HALF // 128):
            n = (i + 1) * 128
            rows = pl.ds(pl.multiple_of(base + i * 128, 128), 128)
            keys = pl.ds(base, n)
            key_n = k_s[keys, :]
            value_n = v_s[keys, :]
            lane = lax.broadcasted_iota(jnp.int32, (n, 128), 1)
            row = lax.broadcasted_iota(jnp.int32, (n, 128), 0)
            low = jnp.zeros((n, 128), jnp.int32)
            for kk in range(4):
                low = jnp.where(lane // BLK == kk, begin[hf * 16 + i * 4 + kk], low)
            seen = (row >= low) & (row <= lane + i * 128)
            bias = jnp.where(seen, 0.0, LOWEST)
            bias = jnp.concatenate([bias, bias], axis=1)
            for g in range(2):
                cols = [slice((2 * g + e) * 128, (2 * g + e + 1) * 128) for e in range(2)]
                qs = jnp.concatenate([q_s[rows, e] for e in cols], axis=0)
                ds = jnp.concatenate([d_s[rows, e] for e in cols], axis=0)
                scores = dot(key_n, qs, NT) * (SCALE * LOG2E) + bias
                top = jnp.max(scores, axis=0, keepdims=True)
                probs = jnp.exp2(scores - top)
                total = jnp.sum(probs, axis=0, keepdims=True)
                probs = probs * (1.0 / total)
                products = dot(value_n, ds, NT)
                delta = jnp.sum(probs * products, axis=0, keepdims=True)
                score_grad = (probs * (products - delta)).astype(jnp.bfloat16)
                probs_low = probs.astype(jnp.bfloat16)
                dkv_s[keys, 0:128] += dot(score_grad, qs, NN)
                dkv_s[keys, 128:256] += dot(probs_low, ds, NN)
                dqt = dot(kt_s[:, keys], score_grad, NN) * SCALE
                for e in range(2):
                    dq_s[rows, cols[e]] = dqt[:, e * 128 : (e + 1) * 128].T.astype(jnp.bfloat16)
        return carry

    lax.fori_loop(0, 2, half, 0)

    y = lax.axis_index("y")
    for t in range(16):
        block = slice(t * BLK, (t + 1) * BLK)
        for half_y, ref in ((y, keep_ref), (1 - y, send_ref)):
            rows = pl.ds(pl.multiple_of(place[half_y * 16 + t] * BLK, BLK), BLK)
            ref[block, 0:128] = (dkv_s[rows, 0:128] * SCALE).astype(ref.dtype)
            ref[block, 128:256] = dkv_s[rows, 128:256].astype(ref.dtype)
    for st in range(32):
        rows = pl.ds(pl.multiple_of(place[st] * BLK, BLK), BLK)
        dq_ref[st // 4, (st % 4) * BLK : (st % 4 + 1) * BLK, :] = dq_s[rows, :]


def pair_kernel(keep_ref, taken_ref, out_ref):
    out_ref[...] = (keep_ref[...] + taken_ref[...].astype(jnp.float32)).astype(jnp.bfloat16)


def weight_kernel(*refs):
    pieces, ins = refs[:4], refs[4:8]
    kv_ref, kv_rows_ref, send_ref, keep_ref, x_s = refs[8:]
    core, x = lax.axis_index("core"), lax.axis_index("x")
    for s in range(4):
        at = pl.multiple_of(lax.rem(x + 4 - s, 4) * 128, 128)
        kv_ref[:, pl.ds(at, 128)] = pieces[s][:, 0:128]
        kv_ref[:, pl.ds(pl.multiple_of(512 + at, 128), 128)] = pieces[s][:, 128:256]
        x_s[:, pl.ds(at, 128)] = ins[s][...]
    part = FEAT_TILE // 2
    other = pl.ds(pl.multiple_of((1 - core) * part, part), part)
    own = pl.ds(pl.multiple_of(core * part, part), part)
    for j in range(4):
        cols = slice(j * 256, (j + 1) * 256)
        send_ref[:, cols] = dot(x_s[other, :], kv_ref[:, cols], NN).astype(jnp.bfloat16)
        keep_ref[:, cols] = dot(x_s[own, :], kv_ref[:, cols], NN)
    kv_rows_ref[...] = kv_ref[pl.ds(pl.multiple_of(x * ROWS, ROWS), ROWS), :]


def halve_kernel(axis, mask, keep_ref, got_ref, send_ref, kept_ref):
    part = kept_ref.shape[0]
    total = keep_ref[...] + got_ref[...].astype(jnp.float32)
    low, high = total[:part, :], total[part:, :]
    upper = (lax.axis_index(axis) & mask) != 0
    send_ref[...] = jnp.where(upper, low, high).astype(send_ref.dtype)
    kept_ref[...] = jnp.where(upper, high, low)


def add_kernel(keep_ref, got_ref, out_ref):
    out_ref[...] = keep_ref[...] + got_ref[...].astype(jnp.float32)


def slice_kernel(w_ref, out_ref):
    at = pl.multiple_of(lax.axis_index("x") * 256, 256)
    out_ref[0] = w_ref[:, pl.ds(at, 256)]


def join_kernel(near_ref, far_ref, out_ref):
    n = near_ref.shape[0]
    out_ref[0:n] = near_ref[...]
    out_ref[n:] = far_ref[...]


def input_kernel(kv_ref, w_ref, far_ref, out_ref, w_s):
    f = lax.axis_index("z") * 4 + lax.axis_index("yh") * 2 + lax.axis_index("core")
    for at in range(FSDP):
        mask = sum(((at >> i) & 1) << bit for i, bit in enumerate(GATHER_BITS))
        source = f ^ mask
        rows = pl.ds(pl.multiple_of((source // 4) * 80, 80), 80)
        cols = pl.ds(pl.multiple_of(lax.rem(source, 4) * 256, 256), 256)
        w_s[rows, cols] = w_ref[at] if at < FSDP // 2 else far_ref[at - FSDP // 2]
    for j in range(2):
        rows = slice(j * 256, (j + 1) * 256)
        tile = dot(w_s[...], kv_ref[rows, :], NT).astype(jnp.bfloat16)
        out_ref[2 * j] = tile[:, 0:128]
        out_ref[2 * j + 1] = tile[:, 128:256]


def input_out_kernel(parts_ref, out_ref):
    for x in range(4):
        for j in range(FEAT_TILE // 128):
            at = x * FEAT_TILE + j * 128
            out_ref[:, at : at + 128] = parts_ref[x, j * 128 : (j + 1) * 128, :].T


def query_out_kernel(dq_ref, out_ref):
    for src in range(CTX):
        at = q_block(src) * Q_COLS
        out_ref[:, at : at + Q_COLS] = dq_ref[src]


GATHER_BITS = (4, 3, 2, 1, 0)
BIT_AXES = (("core", 1), ("yh", 1), ("z", 1), ("z", 2), ("z", 4))


def swap(value, bit):
    axis, mask = BIT_AXES[bit]
    return lax.ppermute(value, axis, [(i, i ^ mask) for i in range(8 if axis == "z" else 2)])


def to_shift(value, s):
    return lax.ppermute(value, "x", [(i, (i + s) % 4) for i in range(4)]) if s else value


def exchange(value, axis):
    return lax.all_to_all(value, axis, 0, 0, tiled=True)


def body(inputs, queries, keys, values, output_cotangent, key_value_weight, doc_ids, block_order):
    tile = pl.pallas_call(
        slice_kernel,
        in_specs=[VMEM],
        out_specs=VMEM,
        out_shape=shape((1, 80, 256)),
        compiler_params=params(2),
        cost_estimate=cost(0, 200_000),
    )(key_value_weight)
    perm = []
    for f1 in range(FSDP):
        for c1 in range(CTX):
            y1, x1 = c1 // 4, c1 % 4
            perm.append((f1 * CTX + c1, ((f1 % 8) * 4 + x1) * CTX + y1 * 4 + f1 // 8))
    tile = lax.ppermute(tile, ("z", "yh", "core", "y", "x"), perm)

    def widen(tile, bit):
        n = 2 * tile.shape[0]
        return pl.pallas_call(
            join_kernel,
            in_specs=[VMEM] * 2,
            out_specs=VMEM,
            out_shape=shape((n, 80, 256)),
            compiler_params=params(3),
            cost_estimate=cost(0, n * 80_000),
        )(tile, swap(tile, bit))

    packed = pl.pallas_call(
        pack_kernel,
        in_specs=[HBM] * 4,
        out_specs=VMEM,
        out_shape=shape((CTX, ROWS, PACK_COLS)),
        scratch_shapes=[pltpu.SemaphoreType.DMA((4 * CTX,))],
        compiler_params=params(56),
        cost_estimate=cost(0, 5_000_000),
    )(queries[0], output_cotangent[0], keys[0], values[0])
    packed, tile = lax.optimization_barrier((packed, tile))
    got = exchange(packed, ("y", "x"))
    for bit in GATHER_BITS[:3]:
        tile = widen(tile, bit)

    turned = pl.pallas_call(
        turn_kernel,
        in_specs=[VMEM],
        out_specs=[VMEM] * 4,
        out_shape=[shape((FEAT_TILE, ROWS))] * 4,
        scratch_shapes=[
            pltpu.VMEM((FEATURES, ROWS), jnp.float32),
            pltpu.VMEM((4, FEAT_TILE, ROWS), jnp.float32),
        ],
        compiler_params=params(8),
        cost_estimate=cost(0, 1_300_000),
    )(inputs[0])

    got_x = [to_shift(turned[s], s) for s in range(4)]
    got, got_x, tile = lax.optimization_barrier((got, got_x, tile))
    tile = widen(tile, GATHER_BITS[3])

    dq_parts, keep, send = pl.pallas_call(
        attention_kernel,
        in_specs=[SMEM] * 2 + [VMEM],
        out_specs=[VMEM] * 3,
        out_shape=[
            shape((CTX, ROWS, Q_COLS)),
            shape((SLAB // 2, 2 * HEAD_WIDTH), jnp.float32),
            shape((SLAB // 2, 2 * HEAD_WIDTH)),
        ],
        scratch_shapes=[
            pltpu.VMEM((SLAB, Q_COLS), jnp.bfloat16),
            pltpu.VMEM((SLAB, Q_COLS), jnp.bfloat16),
            pltpu.VMEM((SLAB, HEAD_WIDTH), jnp.bfloat16),
            pltpu.VMEM((SLAB, HEAD_WIDTH), jnp.bfloat16),
            pltpu.VMEM((HEAD_WIDTH, SLAB), jnp.bfloat16),
            pltpu.VMEM((SLAB, Q_COLS), jnp.bfloat16),
            pltpu.VMEM((SLAB, 2 * HEAD_WIDTH), jnp.float32),
            pltpu.SMEM((32,), jnp.int32),
            pltpu.SMEM((32,), jnp.int32),
        ],
        compiler_params=params(24),
        cost_estimate=cost(10_000_000_000, 5_000_000),
    )(doc_ids[0], block_order, got)

    send, tile = lax.optimization_barrier((send, tile))
    taken = lax.ppermute(send, "y", [(0, 1), (1, 0)])
    far_tile = swap(tile, GATHER_BITS[4])
    own_cols = pl.pallas_call(
        pair_kernel,
        in_specs=[VMEM] * 2,
        out_specs=VMEM,
        out_shape=shape((SLAB // 2, 2 * HEAD_WIDTH)),
        compiler_params=params(6),
        cost_estimate=cost(0, 2_000_000),
    )(keep, taken)
    pieces = [to_shift(own_cols, s) for s in range(4)]
    pieces, far_tile = lax.optimization_barrier((pieces, far_tile))

    kv_half, kv_rows, wg_send, wg_keep = pl.pallas_call(
        weight_kernel,
        in_specs=[VMEM] * 8,
        out_specs=[VMEM] * 4,
        out_shape=[
            shape((SLAB // 2, 1024)),
            shape((ROWS, 1024)),
            shape((FEAT_TILE // 2, 1024)),
            shape((FEAT_TILE // 2, 1024), jnp.float32),
        ],
        scratch_shapes=[pltpu.VMEM((FEAT_TILE, SLAB // 2), jnp.bfloat16)],
        compiler_params=params(12),
        cost_estimate=cost(700_000_000, 6_000_000),
    )(*pieces, *got_x)

    wg_got = swap(wg_send, 0)
    parts = pl.pallas_call(
        input_kernel,
        in_specs=[VMEM] * 3,
        out_specs=VMEM,
        out_shape=shape((4, FEAT_TILE, ROWS)),
        scratch_shapes=[pltpu.VMEM((FEAT_TILE, 1024), jnp.bfloat16)],
        compiler_params=params(12),
        cost_estimate=cost(700_000_000, 4_000_000),
    )(kv_half, tile, far_tile)
    ig_got = exchange(parts, "x")

    def halve(axis, mask, keep, got):
        rows = keep.shape[0] // 2
        return pl.pallas_call(
            functools.partial(halve_kernel, axis, mask),
            in_specs=[VMEM] * 2,
            out_specs=[VMEM] * 2,
            out_shape=[shape((rows, 1024)), shape((rows, 1024), jnp.float32)],
            compiler_params=params(6),
            cost_estimate=cost(0, rows * 1024 * 16),
        )(keep, got)

    wg_send, wg_keep = halve("y", 1, wg_keep, wg_got)
    wg_got = lax.ppermute(wg_send, "y", [(0, 1), (1, 0)])
    for bit in (1, 2, 3, 4):
        wg_send, wg_keep = halve(*BIT_AXES[bit], wg_keep, wg_got)
        wg_got = swap(wg_send, bit)
        if bit == 1:
            wg_got, dq_parts = lax.optimization_barrier((wg_got, dq_parts))
            dq_got = exchange(dq_parts, ("y", "x"))
    weight_grad = pl.pallas_call(
        add_kernel,
        in_specs=[VMEM] * 2,
        out_specs=VMEM,
        out_shape=shape((10, 1024), jnp.float32),
        compiler_params=params(2),
        cost_estimate=cost(0, 100_000),
    )(wg_keep, wg_got)

    query_grad = pl.pallas_call(
        query_out_kernel,
        in_specs=[VMEM],
        out_specs=VMEM,
        out_shape=shape((ROWS, HQ * HEAD_WIDTH)),
        compiler_params=params(6),
        cost_estimate=cost(0, 2_000_000),
    )(dq_got)
    input_grad = pl.pallas_call(
        input_out_kernel,
        in_specs=[VMEM],
        out_specs=VMEM,
        out_shape=shape((ROWS, FEATURES)),
        compiler_params=params(6),
        cost_estimate=cost(0, 1_300_000),
    )(ig_got)
    return (input_grad[None], query_grad[None], kv_rows[None], weight_grad)


def solution(mesh):
    axes = ("z", "yh", "core", "y", "x")
    named = jax.sharding.Mesh(mesh.devices.reshape(8, 2, 2, 2, 4), axes)
    fsdp, ctx = axes[:3], axes[3:]
    return jax.shard_map(
        body,
        mesh=named,
        in_specs=(P(fsdp, ctx, None),) * 5 + (P(fsdp, None), P(fsdp, None), P()),
        out_specs=(P(fsdp, ctx, None),) * 3 + (P(axes, None),),
        check_vma=False,
    )
```

```python
import functools
import math

import jax
import jax.numpy as jnp
from jax import lax
from jax.experimental import pallas as pl
from jax.experimental.pallas import tpu as pltpu
from jax.sharding import PartitionSpec as P

HQ = 32
KEY_VALUE_HEADS = 4
HEAD_WIDTH = 128
BLK = 32
QUERY_PER_KEY = 8

CTX = 8
FSDP = 32
ROWS = 128
SLAB = 1024
FEATURES = 2560
FEAT_TILE = FEATURES // 4
Q_COLS = 512
PACK_COLS = 2 * Q_COLS + 2 * HEAD_WIDTH
HALF = 512
SCALE = 1.0 / math.sqrt(HEAD_WIDTH)
LOG2E = math.log2(math.e)
LOWEST = -1e30
NN = (((1,), (0,)), ((), ()))
NT = (((1,), (1,)), ((), ()))
VMEM = pl.BlockSpec(memory_space=pltpu.VMEM)
HBM = pl.BlockSpec(memory_space=pltpu.HBM)
SMEM = pl.BlockSpec(memory_space=pltpu.SMEM)


def dot(a, b, dims):
    return lax.dot_general(a, b, dims, preferred_element_type=jnp.float32)


def shape(dims, kind=jnp.bfloat16):
    return jax.ShapeDtypeStruct(dims, kind)


def params(mib):
    return pltpu.CompilerParams(vmem_limit_bytes=mib * 1024 * 1024)


def cost(flops, moved):
    return pl.CostEstimate(flops=flops, bytes_accessed=moved, transcendentals=0)


def q_block(device):
    return (device % 4) * 2 + device // 4


def pack_kernel(q_ref, d_ref, k_ref, v_ref, out_ref, packed, load_sems, store_sems):
    loads, stores = [], []
    for dest in range(CTX):
        at = q_block(dest) * Q_COLS
        head = (dest % 4) * HEAD_WIDTH
        place = 0
        for ref, first, width in (
            (q_ref, at, Q_COLS),
            (d_ref, at, Q_COLS),
            (k_ref, head, HEAD_WIDTH),
            (v_ref, head, HEAD_WIDTH),
        ):
            load = pltpu.make_async_copy(
                ref.at[:, first : first + width],
                packed.at[dest, :, place : place + width],
                load_sems.at[len(loads)],
            )
            load.start()
            loads.append(load)
            place += width
    for dest in range(CTX):
        for load in loads[4 * dest : 4 * dest + 4]:
            load.wait()
        store = pltpu.make_async_copy(packed.at[dest], out_ref.at[dest], store_sems.at[dest])
        store.start()
        stores.append(store)
    for store in stores:
        store.wait()


def tile_row(z, low, y):
    row = (low % 2) * 320 + y * 160 + (low // 2) * 80
    return row + (z % 2) * 40 + (z // 2 % 2) * 20 + (z // 4) * 10


def turn_kernel(in_ref, *refs):
    outs, turned, tile = refs[:4], refs[4], refs[5]
    for j in range(FEATURES // 128):
        block = in_ref[:, j * 128 : (j + 1) * 128].T
        turned[j * 128 : (j + 1) * 128, :] = block.astype(jnp.float32)
    for x in range(4):
        for low in range(4):
            for y in range(2):
                for z in range(8):
                    source = (z * 4 + low) * 80 + y * 40 + x * 10
                    at = tile_row(z, low, y)
                    tile[x, at : at + 10, :] = turned[source : source + 10, :]
    for s in range(4):
        outs[s][...] = tile[lax.rem(lax.axis_index("x") + s, 4)].astype(jnp.bfloat16)


def attention_kernel(docs_ref, order_ref, *refs):
    in_ref, dq_ref, dq_far_ref, keep_ref, send_ref = refs[:5]
    q_s, d_s, k_s, v_s, kt_s, dq_s, dkv_s, place, begin = refs[5:]

    first = lax.fori_loop(
        0, 17, lambda i, a: jnp.where(docs_ref[i] == docs_ref[i + 15], i, a), jnp.int32(0)
    )

    def place_block(st, carry):
        b = order_ref[st]
        inside = (b >= first) & (b < first + 16)
        place[st] = jnp.where(inside, b - first, jnp.where(b < first, b + 16, b))
        return carry

    lax.fori_loop(0, 32, place_block, 0)

    def begin_block(t, carry):
        last_doc, last_begin = carry
        doc = docs_ref[jnp.where(t < first, t, t + 16)]
        now = jnp.where(doc == last_doc, last_begin, t)
        begin[t] = jnp.int32(0)
        begin[t + 16] = now * BLK
        return doc, now

    lax.fori_loop(0, 16, begin_block, (jnp.int32(-1), jnp.int32(0)))

    for st in range(32):
        rows = pl.ds(pl.multiple_of(place[st] * BLK, BLK), BLK)
        src, block = st // 4, slice((st % 4) * BLK, (st % 4 + 1) * BLK)
        q_s[rows, :] = in_ref[src, block, 0:Q_COLS]
        d_s[rows, :] = in_ref[src, block, Q_COLS : 2 * Q_COLS]
        k_s[rows, :] = in_ref[src, block, 2 * Q_COLS : 2 * Q_COLS + HEAD_WIDTH]
        v_s[rows, :] = in_ref[src, block, 2 * Q_COLS + HEAD_WIDTH :]
    for j in range(SLAB // 128):
        kt_s[:, j * 128 : (j + 1) * 128] = k_s[j * 128 : (j + 1) * 128, :].T
    dkv_s[...] = jnp.zeros_like(dkv_s)

    def half(hf, carry):
        base = pl.multiple_of(hf * HALF, HALF)
        for i in range(HALF // 128):
            n = (i + 1) * 128
            rows = pl.ds(pl.multiple_of(base + i * 128, 128), 128)
            keys = pl.ds(base, n)
            key_n = k_s[keys, :]
            value_n = v_s[keys, :]
            lane = lax.broadcasted_iota(jnp.int32, (n, 128), 1)
            row = lax.broadcasted_iota(jnp.int32, (n, 128), 0)
            low = jnp.zeros((n, 128), jnp.int32)
            for kk in range(4):
                low = jnp.where(lane // BLK == kk, begin[hf * 16 + i * 4 + kk], low)
            seen = (row >= low) & (row <= lane + i * 128)
            bias = jnp.where(seen, 0.0, LOWEST)
            bias = jnp.concatenate([bias, bias], axis=1)
            for g in range(2):
                cols = [slice((2 * g + e) * 128, (2 * g + e + 1) * 128) for e in range(2)]
                qs = jnp.concatenate([q_s[rows, e] for e in cols], axis=0)
                ds = jnp.concatenate([d_s[rows, e] for e in cols], axis=0)
                scores = dot(key_n, qs, NT) * (SCALE * LOG2E) + bias
                top = jnp.max(scores, axis=0, keepdims=True)
                probs = jnp.exp2(scores - top)
                total = jnp.sum(probs, axis=0, keepdims=True)
                probs = probs * (1.0 / total)
                products = dot(value_n, ds, NT)
                delta = jnp.sum(probs * products, axis=0, keepdims=True)
                score_grad = (probs * (products - delta)).astype(jnp.bfloat16)
                probs_low = probs.astype(jnp.bfloat16)
                dkv_s[keys, 0:128] += dot(score_grad, qs, NN)
                dkv_s[keys, 128:256] += dot(probs_low, ds, NN)
                dqt = dot(kt_s[:, keys], score_grad, NN) * SCALE
                for e in range(2):
                    dq_s[rows, cols[e]] = dqt[:, e * 128 : (e + 1) * 128].T.astype(jnp.bfloat16)
        return carry

    lax.fori_loop(0, 2, half, 0)

    y = lax.axis_index("y")
    for t in range(16):
        block = slice(t * BLK, (t + 1) * BLK)
        for half_y, ref in ((y, keep_ref), (1 - y, send_ref)):
            rows = pl.ds(pl.multiple_of(place[half_y * 16 + t] * BLK, BLK), BLK)
            ref[block, 0:128] = (dkv_s[rows, 0:128] * SCALE).astype(ref.dtype)
            ref[block, 128:256] = dkv_s[rows, 128:256].astype(ref.dtype)
    for t in range(16):
        for half_y, ref in ((y, dq_ref), (1 - y, dq_far_ref)):
            rows = pl.ds(pl.multiple_of(place[half_y * 16 + t] * BLK, BLK), BLK)
            for g in range(4):
                at = g * 128 + (t % 4) * BLK
                ref[t // 4, at : at + BLK, :] = dq_s[rows, g * 128 : (g + 1) * 128]


def pair_kernel(keep_ref, taken_ref, out_ref):
    out_ref[...] = (keep_ref[...] + taken_ref[...].astype(jnp.float32)).astype(jnp.bfloat16)


def weight_kernel(*refs):
    pieces, ins = refs[:4], refs[4:8]
    kv_ref, kv_rows_ref, send_ref, keep_ref, x_s = refs[8:]
    core, x = lax.axis_index("core"), lax.axis_index("x")
    for s in range(4):
        at = pl.multiple_of(lax.rem(x + 4 - s, 4) * 128, 128)
        kv_ref[:, pl.ds(at, 128)] = pieces[s][:, 0:128]
        kv_ref[:, pl.ds(pl.multiple_of(512 + at, 128), 128)] = pieces[s][:, 128:256]
        x_s[:, pl.ds(at, 128)] = ins[s][...]
    part = FEAT_TILE // 2
    other = pl.ds(pl.multiple_of((1 - core) * part, part), part)
    own = pl.ds(pl.multiple_of(core * part, part), part)
    for j in range(4):
        cols = slice(j * 256, (j + 1) * 256)
        send_ref[:, cols] = dot(x_s[other, :], kv_ref[:, cols], NN).astype(jnp.bfloat16)
        keep_ref[:, cols] = dot(x_s[own, :], kv_ref[:, cols], NN)
    kv_rows_ref[...] = kv_ref[pl.ds(pl.multiple_of(x * ROWS, ROWS), ROWS), :]


def halve_kernel(axis, mask, keep_ref, got_ref, send_ref, kept_ref):
    part = kept_ref.shape[0]
    total = keep_ref[...] + got_ref[...].astype(jnp.float32)
    low, high = total[:part, :], total[part:, :]
    upper = (lax.axis_index(axis) & mask) != 0
    send_ref[...] = jnp.where(upper, low, high).astype(send_ref.dtype)
    kept_ref[...] = jnp.where(upper, high, low)


def add_kernel(keep_ref, got_ref, out_ref):
    out_ref[...] = keep_ref[...] + got_ref[...].astype(jnp.float32)


def holds(z, x, step):
    return z // 2 == x if step == 0 else z // 2 % 2 == x % 2


def take_kernel(step, own_ref, got_ref, out_ref):
    own = holds(lax.axis_index("z"), lax.axis_index("x"), step)
    out_ref[...] = jnp.where(own, own_ref[...], got_ref[...])


def join_kernel(near_ref, far_ref, out_ref):
    n = near_ref.shape[0]
    out_ref[0:n] = near_ref[...]
    out_ref[n:] = far_ref[...]


def input_kernel(kv_ref, w_ref, far_ref, dq_ref, dq_got_ref, *refs):
    outs, w_s, tile = refs[:4], refs[4], refs[5]
    z, yh, core = lax.axis_index("z"), lax.axis_index("yh"), lax.axis_index("core")
    x, y = lax.axis_index("x"), lax.axis_index("y")
    for at in range(8):
        shard = ((z & 1) ^ (at & 1)) * 4 + (yh ^ (at // 2 % 2)) * 2 + (core ^ (at // 4))
        rows = pl.ds(pl.multiple_of(shard * 80, 80), 80)
        w_s[rows, :] = w_ref[at] if at < 4 else far_ref[at - 4]
    for j in range(2):
        rows = slice(j * 256, (j + 1) * 256)
        block = dot(w_s[...], kv_ref[rows, :], NT).astype(jnp.bfloat16)
        tile[2 * j] = block[:, 0:128]
        tile[2 * j + 1] = block[:, 128:256]
    near = pl.multiple_of(FEAT_TILE + y * Q_COLS, 128)
    far = pl.multiple_of(FEAT_TILE + (1 - y) * Q_COLS, 128)
    for s in range(4):
        dest = lax.rem(x + s, 4)
        outs[s][0:FEAT_TILE, :] = tile[dest]
        outs[s][pl.ds(near, Q_COLS), :] = dq_ref[dest]
        outs[s][pl.ds(far, Q_COLS), :] = dq_got_ref[dest]


def out_kernel(*refs):
    parts, input_ref, query_ref = refs[:4], refs[4], refs[5]
    x = lax.axis_index("x")
    for s in range(4):
        src = lax.rem(x + 4 - s, 4)
        for j in range(FEAT_TILE // 128):
            cols = pl.ds(pl.multiple_of(src * FEAT_TILE + j * 128, 128), 128)
            input_ref[:, cols] = parts[s][j * 128 : (j + 1) * 128, :].T
        for g in range(8):
            cols = pl.ds(pl.multiple_of(src * 2 * Q_COLS + g * 128, 128), 128)
            at = FEAT_TILE + g * 128
            query_ref[:, cols] = parts[s][at : at + 128, :]


BIT_AXES = (("core", 1), ("yh", 1), ("z", 1), ("z", 2), ("z", 4))


def swap(value, bit):
    axis, mask = BIT_AXES[bit]
    return lax.ppermute(value, axis, [(i, i ^ mask) for i in range(8 if axis == "z" else 2)])


def to_shift(value, s):
    return lax.ppermute(value, "x", [(i, (i + s) % 4) for i in range(4)]) if s else value


def exchange(value, axis):
    return lax.all_to_all(value, axis, 0, 0, tiled=True)


def body(inputs, queries, keys, values, output_cotangent, key_value_weight, doc_ids, block_order):
    packed = pl.pallas_call(
        pack_kernel,
        in_specs=[HBM] * 4,
        out_specs=HBM,
        out_shape=shape((CTX, ROWS, PACK_COLS)),
        scratch_shapes=[
            pltpu.VMEM((CTX, ROWS, PACK_COLS), jnp.bfloat16),
            pltpu.SemaphoreType.DMA((4 * CTX,)),
            pltpu.SemaphoreType.DMA((CTX,)),
        ],
        compiler_params=params(56),
        cost_estimate=cost(0, 5_000_000),
    )(queries[0], output_cotangent[0], keys[0], values[0])
    got = exchange(packed, ("y", "x"))

    _, tile = lax.optimization_barrier((packed, key_value_weight))
    for step in range(2):
        mask = (4, 2)[step]
        pairs = [(z * 4 + x, (z ^ mask) * 4 + x) for z in range(8) for x in range(4) if holds(z, x, step)]
        tile = pl.pallas_call(
            functools.partial(take_kernel, step),
            in_specs=[VMEM] * 2,
            out_specs=VMEM,
            out_shape=shape((80, 1024)),
            compiler_params=params(3),
            cost_estimate=cost(0, 500_000),
        )(tile, lax.ppermute(tile, ("z", "x"), pairs))

    def widen(tile, tile_got):
        n = 2 * tile.shape[0]
        return pl.pallas_call(
            join_kernel,
            in_specs=[VMEM] * 2,
            out_specs=VMEM,
            out_shape=shape((n, 80, 1024)),
            compiler_params=params(4),
            cost_estimate=cost(0, n * 330_000),
        )(tile, tile_got)

    tile = widen(tile[None], swap(tile[None], 2))
    got, tile, inputs = lax.optimization_barrier((got, tile, inputs))

    turned = pl.pallas_call(
        turn_kernel,
        in_specs=[VMEM],
        out_specs=[VMEM] * 4,
        out_shape=[shape((FEAT_TILE, ROWS))] * 4,
        scratch_shapes=[
            pltpu.VMEM((FEATURES, ROWS), jnp.float32),
            pltpu.VMEM((4, FEAT_TILE, ROWS), jnp.float32),
        ],
        compiler_params=params(8),
        cost_estimate=cost(0, 1_300_000),
    )(inputs[0])
    got_x = [to_shift(turned[s], s) for s in range(4)]

    dq_near, dq_far, keep, send = pl.pallas_call(
        attention_kernel,
        in_specs=[SMEM] * 2 + [VMEM],
        out_specs=[VMEM] * 4,
        out_shape=[
            shape((4, Q_COLS, ROWS)),
            shape((4, Q_COLS, ROWS)),
            shape((SLAB // 2, 2 * HEAD_WIDTH), jnp.float32),
            shape((SLAB // 2, 2 * HEAD_WIDTH)),
        ],
        scratch_shapes=[
            pltpu.VMEM((SLAB, Q_COLS), jnp.bfloat16),
            pltpu.VMEM((SLAB, Q_COLS), jnp.bfloat16),
            pltpu.VMEM((SLAB, HEAD_WIDTH), jnp.bfloat16),
            pltpu.VMEM((SLAB, HEAD_WIDTH), jnp.bfloat16),
            pltpu.VMEM((HEAD_WIDTH, SLAB), jnp.bfloat16),
            pltpu.VMEM((SLAB, Q_COLS), jnp.bfloat16),
            pltpu.VMEM((SLAB, 2 * HEAD_WIDTH), jnp.float32),
            pltpu.SMEM((32,), jnp.int32),
            pltpu.SMEM((32,), jnp.int32),
        ],
        compiler_params=params(24),
        cost_estimate=cost(10_000_000_000, 5_000_000),
    )(doc_ids[0], block_order, got)

    send, got_x = lax.optimization_barrier((send, got_x))
    taken = lax.ppermute(send, "y", [(0, 1), (1, 0)])
    taken, tile, dq_far = lax.optimization_barrier((taken, tile, dq_far))
    dq_got = lax.ppermute(dq_far, "y", [(0, 1), (1, 0)])
    tile_got = swap(tile, 1)
    own_cols = pl.pallas_call(
        pair_kernel,
        in_specs=[VMEM] * 2,
        out_specs=VMEM,
        out_shape=shape((SLAB // 2, 2 * HEAD_WIDTH)),
        compiler_params=params(6),
        cost_estimate=cost(0, 2_000_000),
    )(keep, taken)
    pieces = [to_shift(own_cols, s) for s in range(4)]
    pieces, dq_got, tile_got = lax.optimization_barrier((pieces, dq_got, tile_got))

    kv_half, kv_rows, wg_send, wg_keep = pl.pallas_call(
        weight_kernel,
        in_specs=[VMEM] * 8,
        out_specs=[VMEM] * 4,
        out_shape=[
            shape((SLAB // 2, 1024)),
            shape((ROWS, 1024)),
            shape((FEAT_TILE // 2, 1024)),
            shape((FEAT_TILE // 2, 1024), jnp.float32),
        ],
        scratch_shapes=[pltpu.VMEM((FEAT_TILE, SLAB // 2), jnp.bfloat16)],
        compiler_params=params(12),
        cost_estimate=cost(700_000_000, 6_000_000),
    )(*pieces, *got_x)

    wg_got = swap(wg_send, 0)
    tile = widen(tile, tile_got)
    far_tile = swap(tile, 0)
    parts = pl.pallas_call(
        input_kernel,
        in_specs=[VMEM] * 5,
        out_specs=[VMEM] * 4,
        out_shape=[shape((FEAT_TILE + 2 * Q_COLS, ROWS))] * 4,
        scratch_shapes=[
            pltpu.VMEM((FEAT_TILE, 1024), jnp.bfloat16),
            pltpu.VMEM((4, FEAT_TILE, ROWS), jnp.bfloat16),
        ],
        compiler_params=params(12),
        cost_estimate=cost(700_000_000, 6_000_000),
    )(kv_half, tile, far_tile, dq_near, dq_got)
    parts_got = [to_shift(parts[s], s) for s in range(4)]

    def halve(axis, mask, keep, got):
        rows = keep.shape[0] // 2
        return pl.pallas_call(
            functools.partial(halve_kernel, axis, mask),
            in_specs=[VMEM] * 2,
            out_specs=[VMEM] * 2,
            out_shape=[shape((rows, 1024)), shape((rows, 1024), jnp.float32)],
            compiler_params=params(6),
            cost_estimate=cost(0, rows * 1024 * 16),
        )(keep, got)

    wg_send, wg_keep = halve("y", 1, wg_keep, wg_got)
    wg_got = lax.ppermute(wg_send, "y", [(0, 1), (1, 0)])
    for bit in (1, 2, 3, 4):
        wg_send, wg_keep = halve(*BIT_AXES[bit], wg_keep, wg_got)
        wg_got = swap(wg_send, bit)
    weight_grad = pl.pallas_call(
        add_kernel,
        in_specs=[VMEM] * 2,
        out_specs=VMEM,
        out_shape=shape((10, 1024), jnp.float32),
        compiler_params=params(2),
        cost_estimate=cost(0, 100_000),
    )(wg_keep, wg_got)

    input_grad, query_grad = pl.pallas_call(
        out_kernel,
        in_specs=[VMEM] * 4,
        out_specs=[VMEM] * 2,
        out_shape=[shape((ROWS, FEATURES)), shape((ROWS, HQ * HEAD_WIDTH))],
        compiler_params=params(8),
        cost_estimate=cost(0, 3_300_000),
    )(*parts_got)
    return (input_grad[None], query_grad[None], kv_rows[None], weight_grad)


def solution(mesh):
    axes = ("z", "yh", "core", "y", "x")
    named = jax.sharding.Mesh(mesh.devices.reshape(8, 2, 2, 2, 4), axes)
    fsdp, ctx = axes[:3], axes[3:]
    return jax.shard_map(
        body,
        mesh=named,
        in_specs=(P(fsdp, ctx, None),) * 5 + (P(fsdp, None), P(fsdp, None), P()),
        out_specs=(P(fsdp, ctx, None),) * 3 + (P(axes, None),),
        check_vma=False,
    )
```

```python
import functools
import math

import jax
import jax.numpy as jnp
from jax import lax
from jax.experimental import pallas as pl
from jax.experimental.pallas import tpu as pltpu
from jax.sharding import PartitionSpec as P

HQ = 32
KEY_VALUE_HEADS = 4
HEAD_WIDTH = 128
BLK = 32
QUERY_PER_KEY = 8

CTX = 8
FSDP = 32
ROWS = 128
SLAB = 1024
FEATURES = 2560
FEAT_TILE = FEATURES // 4
Q_COLS = 512
PACK_COLS = 2 * Q_COLS + 2 * HEAD_WIDTH
HALF = 512
SCALE = 1.0 / math.sqrt(HEAD_WIDTH)
LOG2E = math.log2(math.e)
LOWEST = -1e30
NN = (((1,), (0,)), ((), ()))
NT = (((1,), (1,)), ((), ()))
VMEM = pl.BlockSpec(memory_space=pltpu.VMEM)
HBM = pl.BlockSpec(memory_space=pltpu.HBM)
SMEM = pl.BlockSpec(memory_space=pltpu.SMEM)


def dot(a, b, dims):
    return lax.dot_general(a, b, dims, preferred_element_type=jnp.float32)


def shape(dims, kind=jnp.bfloat16):
    return jax.ShapeDtypeStruct(dims, kind)


def params(mib):
    return pltpu.CompilerParams(vmem_limit_bytes=mib * 1024 * 1024)


def cost(flops, moved):
    return pl.CostEstimate(flops=flops, bytes_accessed=moved, transcendentals=0)


def q_block(device):
    return (device % 4) * 2 + device // 4


def pack_kernel(q_ref, d_ref, k_ref, v_ref, out_ref, packed, load_sems, store_sems):
    loads, stores = [], []
    for dest in range(CTX):
        at = q_block(dest) * Q_COLS
        head = (dest % 4) * HEAD_WIDTH
        place = 0
        for ref, first, width in (
            (q_ref, at, Q_COLS),
            (d_ref, at, Q_COLS),
            (k_ref, head, HEAD_WIDTH),
            (v_ref, head, HEAD_WIDTH),
        ):
            load = pltpu.make_async_copy(
                ref.at[:, first : first + width],
                packed.at[dest, :, place : place + width],
                load_sems.at[len(loads)],
            )
            load.start()
            loads.append(load)
            place += width
    for dest in range(CTX):
        for load in loads[4 * dest : 4 * dest + 4]:
            load.wait()
        store = pltpu.make_async_copy(packed.at[dest], out_ref.at[dest], store_sems.at[dest])
        store.start()
        stores.append(store)
    for store in stores:
        store.wait()


def tile_row(z, low, y):
    return (low % 2) * 320 + (low // 2) * 160 + y * 80 + (z // 2) * 20 + (z % 2) * 10


def turn_kernel(in_ref, *refs):
    outs, turned, tile = refs[:4], refs[4], refs[5]
    for j in range(FEATURES // 128):
        block = in_ref[:, j * 128 : (j + 1) * 128].T
        turned[j * 128 : (j + 1) * 128, :] = block.astype(jnp.float32)
    for x in range(4):
        for low in range(4):
            for y in range(2):
                for z in range(8):
                    source = (z * 4 + low) * 80 + y * 40 + x * 10
                    at = tile_row(z, low, y)
                    tile[x, at : at + 10, :] = turned[source : source + 10, :]
    for s in range(4):
        outs[s][...] = tile[lax.rem(lax.axis_index("x") + s, 4)].astype(jnp.bfloat16)


def place_blocks(docs_ref, order_ref, place):
    first = lax.fori_loop(
        0, 17, lambda i, a: jnp.where(docs_ref[i] == docs_ref[i + 15], i, a), jnp.int32(0)
    )

    def place_block(st, carry):
        b = order_ref[st]
        inside = (b >= first) & (b < first + 16)
        place[st] = jnp.where(inside, b - first, jnp.where(b < first, b + 16, b))
        return carry

    lax.fori_loop(0, 32, place_block, 0)
    return first


def tile_begin(i):
    return 64 * i * (i + 1)


def attention_kernel(docs_ref, order_ref, *refs):
    in_ref, grad_ref, kt_ref, keep_ref, send_ref = refs[:5]
    q_s, d_s, k_s, v_s, dkv_s, place, begin = refs[5:]
    first = place_blocks(docs_ref, order_ref, place)

    def begin_block(t, carry):
        last_doc, last_begin = carry
        doc = docs_ref[jnp.where(t < first, t, t + 16)]
        now = jnp.where(doc == last_doc, last_begin, t)
        begin[t] = jnp.int32(0)
        begin[t + 16] = now * BLK
        return doc, now

    lax.fori_loop(0, 16, begin_block, (jnp.int32(-1), jnp.int32(0)))

    for st in range(32):
        rows = pl.ds(pl.multiple_of(place[st] * BLK, BLK), BLK)
        src, block = st // 4, slice((st % 4) * BLK, (st % 4 + 1) * BLK)
        q_s[rows, :] = in_ref[src, block, 0:Q_COLS]
        d_s[rows, :] = in_ref[src, block, Q_COLS : 2 * Q_COLS]
        k_s[rows, :] = in_ref[src, block, 2 * Q_COLS : 2 * Q_COLS + HEAD_WIDTH]
        v_s[rows, :] = in_ref[src, block, 2 * Q_COLS + HEAD_WIDTH :]
    for j in range(SLAB // 128):
        kt_ref[:, j * 128 : (j + 1) * 128] = k_s[j * 128 : (j + 1) * 128, :].T
    dkv_s[...] = jnp.zeros_like(dkv_s)

    def half(hf, carry):
        base = pl.multiple_of(hf * HALF, HALF)
        for i in range(HALF // 128):
            n = (i + 1) * 128
            rows = pl.ds(pl.multiple_of(base + i * 128, 128), 128)
            keys = pl.ds(base, n)
            key_n = k_s[keys, :]
            value_n = v_s[keys, :]
            lane = lax.broadcasted_iota(jnp.int32, (n, 128), 1)
            row = lax.broadcasted_iota(jnp.int32, (n, 128), 0)
            low = jnp.zeros((n, 128), jnp.int32)
            for kk in range(4):
                low = jnp.where(lane // BLK == kk, begin[hf * 16 + i * 4 + kk], low)
            seen = (row >= low) & (row <= lane + i * 128)
            bias = jnp.where(seen, 0.0, LOWEST)
            bias = jnp.concatenate([bias, bias], axis=1)
            for g in range(2):
                cols = [slice((2 * g + e) * 128, (2 * g + e + 1) * 128) for e in range(2)]
                qs = jnp.concatenate([q_s[rows, e] for e in cols], axis=0)
                ds = jnp.concatenate([d_s[rows, e] for e in cols], axis=0)
                scores = dot(key_n, qs, NT) * (SCALE * LOG2E) + bias
                top = jnp.max(scores, axis=0, keepdims=True)
                probs = jnp.exp2(scores - top)
                total = jnp.sum(probs, axis=0, keepdims=True)
                probs = probs * (1.0 / total)
                products = dot(value_n, ds, NT)
                delta = jnp.sum(probs * products, axis=0, keepdims=True)
                score_grad = (probs * (products - delta)).astype(jnp.bfloat16)
                probs_low = probs.astype(jnp.bfloat16)
                dkv_s[keys, 0:128] += dot(score_grad, qs, NN)
                dkv_s[keys, 128:256] += dot(probs_low, ds, NN)
                grad_ref[hf, g, tile_begin(i) : tile_begin(i) + n, :] = score_grad
        return carry

    lax.fori_loop(0, 2, half, 0)

    y = lax.axis_index("y")
    for t in range(16):
        block = slice(t * BLK, (t + 1) * BLK)
        for half_y, ref in ((y, keep_ref), (1 - y, send_ref)):
            rows = pl.ds(pl.multiple_of(place[half_y * 16 + t] * BLK, BLK), BLK)
            ref[block, 0:128] = (dkv_s[rows, 0:128] * SCALE).astype(ref.dtype)
            ref[block, 128:256] = dkv_s[rows, 128:256].astype(ref.dtype)

def query_kernel(docs_ref, order_ref, grad_ref, kt_ref, near_ref, far_ref, dq_s, place):
    place_blocks(docs_ref, order_ref, place)
    for hf in range(2):
        for i in range(HALF // 128):
            n = (i + 1) * 128
            rows = slice(hf * HALF + i * 128, hf * HALF + (i + 1) * 128)
            for g in range(2):
                part = grad_ref[hf, g, tile_begin(i) : tile_begin(i) + n, :]
                dqt = dot(kt_ref[:, hf * HALF : hf * HALF + n], part, NN) * SCALE
                for e in range(2):
                    at = (2 * g + e) * 128
                    block = dqt[:, e * 128 : (e + 1) * 128].T
                    dq_s[rows, at : at + 128] = block.astype(jnp.bfloat16)
    y = lax.axis_index("y")
    for t in range(16):
        for half_y, ref in ((y, near_ref), (1 - y, far_ref)):
            rows = pl.ds(pl.multiple_of(place[half_y * 16 + t] * BLK, BLK), BLK)
            for g in range(4):
                at = g * 128 + (t % 4) * BLK
                ref[t // 4, at : at + BLK, :] = dq_s[rows, g * 128 : (g + 1) * 128]


def pair_kernel(keep_ref, taken_ref, out_ref):
    out_ref[...] = (keep_ref[...] + taken_ref[...].astype(jnp.float32)).astype(jnp.bfloat16)


def weight_kernel(*refs):
    pieces, ins = refs[:4], refs[4:8]
    kv_ref, kv_rows_ref, send_ref, keep_ref, x_s = refs[8:]
    core, x = lax.axis_index("core"), lax.axis_index("x")
    for s in range(4):
        at = pl.multiple_of(lax.rem(x + 4 - s, 4) * 128, 128)
        kv_ref[:, pl.ds(at, 128)] = pieces[s][:, 0:128]
        kv_ref[:, pl.ds(pl.multiple_of(512 + at, 128), 128)] = pieces[s][:, 128:256]
        x_s[:, pl.ds(at, 128)] = ins[s][...]
    part = FEAT_TILE // 2
    other = pl.ds(pl.multiple_of((1 - core) * part, part), part)
    own = pl.ds(pl.multiple_of(core * part, part), part)
    for j in range(4):
        cols = slice(j * 256, (j + 1) * 256)
        send_ref[:, cols] = dot(x_s[other, :], kv_ref[:, cols], NN).astype(jnp.bfloat16)
        keep_ref[:, cols] = dot(x_s[own, :], kv_ref[:, cols], NN)
    kv_rows_ref[...] = kv_ref[pl.ds(pl.multiple_of(x * ROWS, ROWS), ROWS), :]


def split_kernel(number, count, *refs):
    count_in = len(refs) - count - 1
    ins, sends, keep_ref, parts = refs[:count_in], refs[count_in:-2], refs[-2], refs[-1]
    total = ins[0][...]
    for ref in ins[1:]:
        total = total + ref[...].astype(jnp.float32)
    rows = keep_ref.shape[0]
    for k in range(count):
        parts[k] = total[k * rows : (k + 1) * rows, :]
    own = number()
    keep_ref[...] = parts[own]
    for k in range(1, count):
        sends[k - 1][...] = parts[own ^ k].astype(jnp.bfloat16)


def add_kernel(keep_ref, got_ref, out_ref):
    out_ref[...] = keep_ref[...] + got_ref[...].astype(jnp.float32)


def holds(z, x, step):
    return z // 2 == x if step == 0 else z // 2 % 2 == x % 2


def take_kernel(step, own_ref, got_ref, out_ref):
    own = holds(lax.axis_index("z"), lax.axis_index("x"), step)
    out_ref[...] = jnp.where(own, own_ref[...], got_ref[...])


def join_kernel(near_ref, far_ref, out_ref):
    n = near_ref.shape[0]
    out_ref[0:n] = near_ref[...]
    out_ref[n:] = far_ref[...]


def input_kernel(kv_ref, w_ref, far_ref, dq_ref, dq_got_ref, *refs):
    outs, w_s, tile = refs[:4], refs[4], refs[5]
    z, yh, core = lax.axis_index("z"), lax.axis_index("yh"), lax.axis_index("core")
    x, y = lax.axis_index("x"), lax.axis_index("y")
    for at in range(8):
        shard = ((z & 1) ^ (at & 1)) * 4 + (yh ^ (at // 2 % 2)) * 2 + (core ^ (at // 4))
        rows = pl.ds(pl.multiple_of(shard * 80, 80), 80)
        w_s[rows, :] = w_ref[at] if at < 4 else far_ref[at - 4]
    for j in range(2):
        rows = slice(j * 256, (j + 1) * 256)
        block = dot(w_s[...], kv_ref[rows, :], NT).astype(jnp.bfloat16)
        tile[2 * j] = block[:, 0:128]
        tile[2 * j + 1] = block[:, 128:256]
    near = pl.multiple_of(FEAT_TILE + y * Q_COLS, 128)
    far = pl.multiple_of(FEAT_TILE + (1 - y) * Q_COLS, 128)
    for s in range(4):
        dest = lax.rem(x + s, 4)
        outs[s][0:FEAT_TILE, :] = tile[dest]
        outs[s][pl.ds(near, Q_COLS), :] = dq_ref[dest]
        outs[s][pl.ds(far, Q_COLS), :] = dq_got_ref[dest]


def out_kernel(*refs):
    parts, input_ref, query_ref = refs[:4], refs[4], refs[5]
    x = lax.axis_index("x")
    for s in range(4):
        src = lax.rem(x + 4 - s, 4)
        for j in range(FEAT_TILE // 128):
            cols = pl.ds(pl.multiple_of(src * FEAT_TILE + j * 128, 128), 128)
            input_ref[:, cols] = parts[s][j * 128 : (j + 1) * 128, :].T
        for g in range(8):
            cols = pl.ds(pl.multiple_of(src * 2 * Q_COLS + g * 128, 128), 128)
            at = FEAT_TILE + g * 128
            query_ref[:, cols] = parts[s][at : at + 128, :]


BIT_AXES = (("core", 1), ("yh", 1), ("z", 1), ("z", 2), ("z", 4))


def swap(value, bit):
    axis, mask = BIT_AXES[bit]
    return lax.ppermute(value, axis, [(i, i ^ mask) for i in range(8 if axis == "z" else 2)])


def to_shift(value, s):
    return lax.ppermute(value, "x", [(i, (i + s) % 4) for i in range(4)]) if s else value


def exchange(value, axis):
    return lax.all_to_all(value, axis, 0, 0, tiled=True)


def body(inputs, queries, keys, values, output_cotangent, key_value_weight, doc_ids, block_order):
    packed = pl.pallas_call(
        pack_kernel,
        in_specs=[HBM] * 4,
        out_specs=HBM,
        out_shape=shape((CTX, ROWS, PACK_COLS)),
        scratch_shapes=[
            pltpu.VMEM((CTX, ROWS, PACK_COLS), jnp.bfloat16),
            pltpu.SemaphoreType.DMA((4 * CTX,)),
            pltpu.SemaphoreType.DMA((CTX,)),
        ],
        compiler_params=params(56),
        cost_estimate=cost(0, 5_000_000),
    )(queries[0], output_cotangent[0], keys[0], values[0])
    got = exchange(packed, ("y", "x"))

    _, tile = lax.optimization_barrier((packed, key_value_weight))
    for step in range(2):
        mask = (4, 2)[step]
        pairs = [(z * 4 + x, (z ^ mask) * 4 + x) for z in range(8) for x in range(4) if holds(z, x, step)]
        tile = pl.pallas_call(
            functools.partial(take_kernel, step),
            in_specs=[VMEM] * 2,
            out_specs=VMEM,
            out_shape=shape((80, 1024)),
            compiler_params=params(3),
            cost_estimate=cost(0, 500_000),
        )(tile, lax.ppermute(tile, ("z", "x"), pairs))

    def widen(tile, tile_got):
        n = 2 * tile.shape[0]
        return pl.pallas_call(
            join_kernel,
            in_specs=[VMEM] * 2,
            out_specs=VMEM,
            out_shape=shape((n, 80, 1024)),
            compiler_params=params(4),
            cost_estimate=cost(0, n * 330_000),
        )(tile, tile_got)

    tile = widen(tile[None], swap(tile[None], 2))
    got, tile, inputs = lax.optimization_barrier((got, tile, inputs))

    turned = pl.pallas_call(
        turn_kernel,
        in_specs=[VMEM],
        out_specs=[VMEM] * 4,
        out_shape=[shape((FEAT_TILE, ROWS))] * 4,
        scratch_shapes=[
            pltpu.VMEM((FEATURES, ROWS), jnp.float32),
            pltpu.VMEM((4, FEAT_TILE, ROWS), jnp.float32),
        ],
        compiler_params=params(8),
        cost_estimate=cost(0, 1_300_000),
    )(inputs[0])
    got_x = [to_shift(turned[s], s) for s in range(4)]
    tile_got = swap(tile, 1)

    score_grad, keys_turned, keep, send = pl.pallas_call(
        attention_kernel,
        in_specs=[SMEM] * 2 + [VMEM],
        out_specs=[VMEM] * 4,
        out_shape=[
            shape((2, 2, tile_begin(4), 256)),
            shape((HEAD_WIDTH, SLAB)),
            shape((SLAB // 2, 2 * HEAD_WIDTH), jnp.float32),
            shape((SLAB // 2, 2 * HEAD_WIDTH)),
        ],
        scratch_shapes=[
            pltpu.VMEM((SLAB, Q_COLS), jnp.bfloat16),
            pltpu.VMEM((SLAB, Q_COLS), jnp.bfloat16),
            pltpu.VMEM((SLAB, HEAD_WIDTH), jnp.bfloat16),
            pltpu.VMEM((SLAB, HEAD_WIDTH), jnp.bfloat16),
            pltpu.VMEM((SLAB, 2 * HEAD_WIDTH), jnp.float32),
            pltpu.SMEM((32,), jnp.int32),
            pltpu.SMEM((32,), jnp.int32),
        ],
        compiler_params=params(24),
        cost_estimate=cost(10_000_000_000, 5_000_000),
    )(doc_ids[0], block_order, got)

    send, got_x, tile_got = lax.optimization_barrier((send, got_x, tile_got))
    taken = lax.ppermute(send, "y", [(0, 1), (1, 0)])
    dq_near, dq_far = pl.pallas_call(
        query_kernel,
        in_specs=[SMEM] * 2 + [VMEM] * 2,
        out_specs=[VMEM] * 2,
        out_shape=[shape((4, Q_COLS, ROWS))] * 2,
        scratch_shapes=[
            pltpu.VMEM((SLAB, Q_COLS), jnp.bfloat16),
            pltpu.SMEM((32,), jnp.int32),
        ],
        compiler_params=params(12),
        cost_estimate=cost(2_000_000_000, 4_000_000),
    )(doc_ids[0], block_order, score_grad, keys_turned)
    taken, dq_near, dq_far = lax.optimization_barrier((taken, dq_near, dq_far))
    own_cols = pl.pallas_call(
        pair_kernel,
        in_specs=[VMEM] * 2,
        out_specs=VMEM,
        out_shape=shape((SLAB // 2, 2 * HEAD_WIDTH)),
        compiler_params=params(6),
        cost_estimate=cost(0, 2_000_000),
    )(keep, taken)
    pieces = [to_shift(own_cols, s) for s in range(4)]
    _, dq_far, tile, tile_got = lax.optimization_barrier((own_cols, dq_far, tile, tile_got))
    dq_got = lax.ppermute(dq_far, "y", [(0, 1), (1, 0)])
    tile = widen(tile, tile_got)
    far_tile = swap(tile, 0)
    pieces, dq_got, far_tile = lax.optimization_barrier((pieces, dq_got, far_tile))

    kv_half, kv_rows, wg_send, wg_keep = pl.pallas_call(
        weight_kernel,
        in_specs=[VMEM] * 8,
        out_specs=[VMEM] * 4,
        out_shape=[
            shape((SLAB // 2, 1024)),
            shape((ROWS, 1024)),
            shape((FEAT_TILE // 2, 1024)),
            shape((FEAT_TILE // 2, 1024), jnp.float32),
        ],
        scratch_shapes=[pltpu.VMEM((FEAT_TILE, SLAB // 2), jnp.bfloat16)],
        compiler_params=params(12),
        cost_estimate=cost(700_000_000, 6_000_000),
    )(*pieces, *got_x)

    wg_got = swap(wg_send, 0)
    parts = pl.pallas_call(
        input_kernel,
        in_specs=[VMEM] * 5,
        out_specs=[VMEM] * 4,
        out_shape=[shape((FEAT_TILE + 2 * Q_COLS, ROWS))] * 4,
        scratch_shapes=[
            pltpu.VMEM((FEAT_TILE, 1024), jnp.bfloat16),
            pltpu.VMEM((4, FEAT_TILE, ROWS), jnp.bfloat16),
        ],
        compiler_params=params(12),
        cost_estimate=cost(700_000_000, 6_000_000),
    )(kv_half, tile, far_tile, dq_near, dq_got)
    wg_got, parts = lax.optimization_barrier((wg_got, parts))
    parts_got = [to_shift(parts[s], s) for s in range(4)]

    def split(number, count, keep, *arrived):
        rows = keep.shape[0] // count
        results = pl.pallas_call(
            functools.partial(split_kernel, number, count),
            in_specs=[VMEM] * (1 + len(arrived)),
            out_specs=[VMEM] * count,
            out_shape=[shape((rows, 1024))] * (count - 1) + [shape((rows, 1024), jnp.float32)],
            scratch_shapes=[pltpu.VMEM((count, rows, 1024), jnp.float32)],
            compiler_params=params(8),
            cost_estimate=cost(0, count * rows * 1024 * 16),
        )(keep, *arrived)
        return results[:-1], results[-1]

    sends, wg_keep = split(
        lambda: lax.axis_index("yh") * 2 + lax.axis_index("y"), 4, wg_keep, wg_got
    )
    arrived = [
        lax.ppermute(part, ("yh", "y"), [(i, i ^ (k + 1)) for i in range(4)])
        for k, part in enumerate(sends)
    ]
    sends, wg_keep = split(lambda: lax.axis_index("z") // 2, 4, wg_keep, *arrived)
    arrived = [
        lax.ppermute(part, "z", [(i, i ^ (2 * (k + 1))) for i in range(8)])
        for k, part in enumerate(sends)
    ]
    sends, wg_keep = split(lambda: lax.rem(lax.axis_index("z"), 2), 2, wg_keep, *arrived)
    wg_got = swap(sends[0], 2)
    weight_grad = pl.pallas_call(
        add_kernel,
        in_specs=[VMEM] * 2,
        out_specs=VMEM,
        out_shape=shape((10, 1024), jnp.float32),
        compiler_params=params(2),
        cost_estimate=cost(0, 100_000),
    )(wg_keep, wg_got)

    input_grad, query_grad = pl.pallas_call(
        out_kernel,
        in_specs=[VMEM] * 4,
        out_specs=[VMEM] * 2,
        out_shape=[shape((ROWS, FEATURES)), shape((ROWS, HQ * HEAD_WIDTH))],
        compiler_params=params(8),
        cost_estimate=cost(0, 3_300_000),
    )(*parts_got)
    return (input_grad[None], query_grad[None], kv_rows[None], weight_grad)


def solution(mesh):
    axes = ("z", "yh", "core", "y", "x")
    named = jax.sharding.Mesh(mesh.devices.reshape(8, 2, 2, 2, 4), axes)
    fsdp, ctx = axes[:3], axes[3:]
    return jax.shard_map(
        body,
        mesh=named,
        in_specs=(P(fsdp, ctx, None),) * 5 + (P(fsdp, None), P(fsdp, None), P()),
        out_specs=(P(fsdp, ctx, None),) * 3 + (P(axes, None),),
        check_vma=False,
    )
```

```python
import functools
import math

import jax
import jax.numpy as jnp
from jax import lax
from jax.experimental import pallas as pl
from jax.experimental.pallas import tpu as pltpu
from jax.sharding import PartitionSpec as P

HQ = 32
KEY_VALUE_HEADS = 4
HEAD_WIDTH = 128
BLK = 32
QUERY_PER_KEY = 8

CTX = 8
FSDP = 32
ROWS = 128
SLAB = 1024
FEATURES = 2560
FEAT_TILE = FEATURES // 4
Q_COLS = 512
PACK_COLS = 2 * Q_COLS + 2 * HEAD_WIDTH
HALF = 512
SCALE = 1.0 / math.sqrt(HEAD_WIDTH)
LOG2E = math.log2(math.e)
LOWEST = -1e30
NN = (((1,), (0,)), ((), ()))
NT = (((1,), (1,)), ((), ()))
VMEM = pl.BlockSpec(memory_space=pltpu.VMEM)
HBM = pl.BlockSpec(memory_space=pltpu.HBM)
SMEM = pl.BlockSpec(memory_space=pltpu.SMEM)


def dot(a, b, dims):
    return lax.dot_general(a, b, dims, preferred_element_type=jnp.float32)


def shape(dims, kind=jnp.bfloat16):
    return jax.ShapeDtypeStruct(dims, kind)


def params(mib):
    return pltpu.CompilerParams(vmem_limit_bytes=mib * 1024 * 1024)


def cost(flops, moved):
    return pl.CostEstimate(flops=flops, bytes_accessed=moved, transcendentals=0)


def q_block(device):
    return (device % 4) * 2 + device // 4


def pack_kernel(q_ref, d_ref, k_ref, v_ref, out_ref, packed, load_sems, store_sems):
    loads, stores = [], []
    for dest in range(CTX):
        at = q_block(dest) * Q_COLS
        head = (dest % 4) * HEAD_WIDTH
        place = 0
        for ref, first, width in (
            (q_ref, at, Q_COLS),
            (d_ref, at, Q_COLS),
            (k_ref, head, HEAD_WIDTH),
            (v_ref, head, HEAD_WIDTH),
        ):
            load = pltpu.make_async_copy(
                ref.at[:, first : first + width],
                packed.at[dest, :, place : place + width],
                load_sems.at[len(loads)],
            )
            load.start()
            loads.append(load)
            place += width
    for dest in range(CTX):
        for load in loads[4 * dest : 4 * dest + 4]:
            load.wait()
        store = pltpu.make_async_copy(packed.at[dest], out_ref.at[dest], store_sems.at[dest])
        store.start()
        stores.append(store)
    for store in stores:
        store.wait()


def tile_row(z, low, y):
    row = (low % 2) * 320 + y * 160 + (low // 2) * 80
    return row + (z % 2) * 40 + (z // 2 % 2) * 20 + (z // 4) * 10


def turn_kernel(in_ref, *refs):
    outs, turned, tile = refs[:4], refs[4], refs[5]
    for j in range(FEATURES // 128):
        block = in_ref[:, j * 128 : (j + 1) * 128].T
        turned[j * 128 : (j + 1) * 128, :] = block.astype(jnp.float32)
    for x in range(4):
        for low in range(4):
            for y in range(2):
                for z in range(8):
                    source = (z * 4 + low) * 80 + y * 40 + x * 10
                    at = tile_row(z, low, y)
                    tile[x, at : at + 10, :] = turned[source : source + 10, :]
    for s in range(4):
        outs[s][...] = tile[lax.rem(lax.axis_index("x") + s, 4)].astype(jnp.bfloat16)


def place_blocks(docs_ref, order_ref, place):
    first = lax.fori_loop(
        0, 17, lambda i, a: jnp.where(docs_ref[i] == docs_ref[i + 15], i, a), jnp.int32(0)
    )

    def place_block(st, carry):
        b = order_ref[st]
        inside = (b >= first) & (b < first + 16)
        place[st] = jnp.where(inside, b - first, jnp.where(b < first, b + 16, b))
        return carry

    lax.fori_loop(0, 32, place_block, 0)
    return first


def tile_begin(i):
    return 64 * i * (i + 1)


def attention_kernel(docs_ref, order_ref, *refs):
    in_ref, grad_ref, kt_ref, keep_ref, send_ref = refs[:5]
    q_s, d_s, k_s, v_s, dkv_s, place, begin = refs[5:]
    first = place_blocks(docs_ref, order_ref, place)

    def begin_block(t, carry):
        last_doc, last_begin = carry
        doc = docs_ref[jnp.where(t < first, t, t + 16)]
        now = jnp.where(doc == last_doc, last_begin, t)
        begin[t] = jnp.int32(0)
        begin[t + 16] = now * BLK
        return doc, now

    lax.fori_loop(0, 16, begin_block, (jnp.int32(-1), jnp.int32(0)))

    for st in range(32):
        rows = pl.ds(pl.multiple_of(place[st] * BLK, BLK), BLK)
        src, block = st // 4, slice((st % 4) * BLK, (st % 4 + 1) * BLK)
        q_s[rows, :] = in_ref[src, block, 0:Q_COLS]
        d_s[rows, :] = in_ref[src, block, Q_COLS : 2 * Q_COLS]
        k_s[rows, :] = in_ref[src, block, 2 * Q_COLS : 2 * Q_COLS + HEAD_WIDTH]
        v_s[rows, :] = in_ref[src, block, 2 * Q_COLS + HEAD_WIDTH :]
    for j in range(SLAB // 128):
        kt_ref[:, j * 128 : (j + 1) * 128] = k_s[j * 128 : (j + 1) * 128, :].T
    dkv_s[...] = jnp.zeros_like(dkv_s)

    def half(hf, carry):
        base = pl.multiple_of(hf * HALF, HALF)
        for i in range(HALF // 128):
            n = (i + 1) * 128
            rows = pl.ds(pl.multiple_of(base + i * 128, 128), 128)
            keys = pl.ds(base, n)
            key_n = k_s[keys, :]
            value_n = v_s[keys, :]
            lane = lax.broadcasted_iota(jnp.int32, (n, 128), 1)
            row = lax.broadcasted_iota(jnp.int32, (n, 128), 0)
            low = jnp.zeros((n, 128), jnp.int32)
            for kk in range(4):
                low = jnp.where(lane // BLK == kk, begin[hf * 16 + i * 4 + kk], low)
            seen = (row >= low) & (row <= lane + i * 128)
            bias = jnp.where(seen, 0.0, LOWEST)
            bias = jnp.concatenate([bias, bias], axis=1)
            q_rows = [q_s[rows, e * 128 : (e + 1) * 128] for e in range(4)]
            d_rows = [d_s[rows, e * 128 : (e + 1) * 128] for e in range(4)]
            grads, lows = [], []
            for g in range(2):
                qs = jnp.concatenate(q_rows[2 * g : 2 * g + 2], axis=0)
                ds = jnp.concatenate(d_rows[2 * g : 2 * g + 2], axis=0)
                scores = dot(key_n, qs, NT) * (SCALE * LOG2E) + bias
                top = jnp.max(scores, axis=0, keepdims=True)
                weights = jnp.exp2(scores - top)
                share = 1.0 / jnp.sum(weights, axis=0, keepdims=True)
                products = dot(value_n, ds, NT)
                delta = jnp.sum(weights * products, axis=0, keepdims=True) * share
                probs = weights * share
                grads.append((probs * (products - delta)).astype(jnp.bfloat16))
                lows.append(probs.astype(jnp.bfloat16))
                grad_ref[hf, g, tile_begin(i) : tile_begin(i) + n, :] = grads[g]
            dkv_s[keys, 0:128] += dot(
                jnp.concatenate(grads, axis=1), jnp.concatenate(q_rows, axis=0), NN
            )
            dkv_s[keys, 128:256] += dot(
                jnp.concatenate(lows, axis=1), jnp.concatenate(d_rows, axis=0), NN
            )
        return carry

    lax.fori_loop(0, 2, half, 0)

    y = lax.axis_index("y")
    for t in range(16):
        block = slice(t * BLK, (t + 1) * BLK)
        for half_y, ref in ((y, keep_ref), (1 - y, send_ref)):
            rows = pl.ds(pl.multiple_of(place[half_y * 16 + t] * BLK, BLK), BLK)
            ref[block, 0:128] = (dkv_s[rows, 0:128] * SCALE).astype(ref.dtype)
            ref[block, 128:256] = dkv_s[rows, 128:256].astype(ref.dtype)

def query_kernel(docs_ref, order_ref, grad_ref, kt_ref, near_ref, far_ref, dq_s, place):
    place_blocks(docs_ref, order_ref, place)
    for hf in range(2):
        for i in range(HALF // 128):
            n = (i + 1) * 128
            rows = slice(hf * HALF + i * 128, hf * HALF + (i + 1) * 128)
            for g in range(2):
                part = grad_ref[hf, g, tile_begin(i) : tile_begin(i) + n, :]
                dqt = dot(kt_ref[:, hf * HALF : hf * HALF + n], part, NN) * SCALE
                for e in range(2):
                    at = (2 * g + e) * 128
                    block = dqt[:, e * 128 : (e + 1) * 128].T
                    dq_s[rows, at : at + 128] = block.astype(jnp.bfloat16)
    y = lax.axis_index("y")
    for t in range(16):
        for half_y, ref in ((y, near_ref), (1 - y, far_ref)):
            rows = pl.ds(pl.multiple_of(place[half_y * 16 + t] * BLK, BLK), BLK)
            for g in range(4):
                at = g * 128 + (t % 4) * BLK
                ref[t // 4, at : at + BLK, :] = dq_s[rows, g * 128 : (g + 1) * 128]


def pair_kernel(keep_ref, taken_ref, out_ref):
    out_ref[...] = (keep_ref[...] + taken_ref[...].astype(jnp.float32)).astype(jnp.bfloat16)


def weight_kernel(*refs):
    pieces, ins = refs[:4], refs[4:8]
    kv_ref, kv_rows_ref, send_ref, keep_ref, x_s = refs[8:]
    core, x = lax.axis_index("core"), lax.axis_index("x")
    for s in range(4):
        at = pl.multiple_of(lax.rem(x + 4 - s, 4) * 128, 128)
        kv_ref[:, pl.ds(at, 128)] = pieces[s][:, 0:128]
        kv_ref[:, pl.ds(pl.multiple_of(512 + at, 128), 128)] = pieces[s][:, 128:256]
        x_s[:, pl.ds(at, 128)] = ins[s][...]
    part = FEAT_TILE // 2
    other = pl.ds(pl.multiple_of((1 - core) * part, part), part)
    own = pl.ds(pl.multiple_of(core * part, part), part)
    for j in range(4):
        cols = slice(j * 256, (j + 1) * 256)
        send_ref[:, cols] = dot(x_s[other, :], kv_ref[:, cols], NN).astype(jnp.bfloat16)
        keep_ref[:, cols] = dot(x_s[own, :], kv_ref[:, cols], NN)
    kv_rows_ref[...] = kv_ref[pl.ds(pl.multiple_of(x * ROWS, ROWS), ROWS), :]


def split_kernel(number, count, *refs):
    count_in = len(refs) - count - 1
    ins, sends, keep_ref, parts = refs[:count_in], refs[count_in:-2], refs[-2], refs[-1]
    total = ins[0][...]
    for ref in ins[1:]:
        total = total + ref[...].astype(jnp.float32)
    rows = keep_ref.shape[0]
    for k in range(count):
        parts[k] = total[k * rows : (k + 1) * rows, :]
    own = number()
    keep_ref[...] = parts[own]
    for k in range(1, count):
        sends[k - 1][...] = parts[own ^ k].astype(jnp.bfloat16)


def add_kernel(keep_ref, got_ref, out_ref):
    out_ref[...] = keep_ref[...] + got_ref[...].astype(jnp.float32)


def holds(z, x, step):
    return z // 2 == x if step == 0 else z // 2 % 2 == x % 2


def take_kernel(step, own_ref, got_ref, out_ref):
    own = holds(lax.axis_index("z"), lax.axis_index("x"), step)
    out_ref[...] = jnp.where(own, own_ref[...], got_ref[...])


def join_kernel(near_ref, far_ref, out_ref):
    n = near_ref.shape[0]
    out_ref[0:n] = near_ref[...]
    out_ref[n:] = far_ref[...]


def input_kernel(kv_ref, w_ref, far_ref, dq_ref, dq_got_ref, *refs):
    outs, w_s, tile = refs[:4], refs[4], refs[5]
    z, yh, core = lax.axis_index("z"), lax.axis_index("yh"), lax.axis_index("core")
    x, y = lax.axis_index("x"), lax.axis_index("y")
    for at in range(8):
        shard = ((z & 1) ^ (at & 1)) * 4 + (yh ^ (at // 2 % 2)) * 2 + (core ^ (at // 4))
        rows = pl.ds(pl.multiple_of(shard * 80, 80), 80)
        w_s[rows, :] = w_ref[at] if at < 4 else far_ref[at - 4]
    for j in range(2):
        rows = slice(j * 256, (j + 1) * 256)
        block = dot(w_s[...], kv_ref[rows, :], NT).astype(jnp.bfloat16)
        tile[2 * j] = block[:, 0:128]
        tile[2 * j + 1] = block[:, 128:256]
    near = pl.multiple_of(FEAT_TILE + y * Q_COLS, 128)
    far = pl.multiple_of(FEAT_TILE + (1 - y) * Q_COLS, 128)
    for s in range(4):
        dest = lax.rem(x + s, 4)
        outs[s][0:FEAT_TILE, :] = tile[dest]
        outs[s][pl.ds(near, Q_COLS), :] = dq_ref[dest]
        outs[s][pl.ds(far, Q_COLS), :] = dq_got_ref[dest]


def out_kernel(*refs):
    parts, input_ref, query_ref = refs[:4], refs[4], refs[5]
    x = lax.axis_index("x")
    for s in range(4):
        src = lax.rem(x + 4 - s, 4)
        for j in range(FEAT_TILE // 128):
            cols = pl.ds(pl.multiple_of(src * FEAT_TILE + j * 128, 128), 128)
            input_ref[:, cols] = parts[s][j * 128 : (j + 1) * 128, :].T
        for g in range(8):
            cols = pl.ds(pl.multiple_of(src * 2 * Q_COLS + g * 128, 128), 128)
            at = FEAT_TILE + g * 128
            query_ref[:, cols] = parts[s][at : at + 128, :]


BIT_AXES = (("core", 1), ("yh", 1), ("z", 1), ("z", 2), ("z", 4))


def swap(value, bit):
    axis, mask = BIT_AXES[bit]
    return lax.ppermute(value, axis, [(i, i ^ mask) for i in range(8 if axis == "z" else 2)])


def to_shift(value, s):
    return lax.ppermute(value, "x", [(i, (i + s) % 4) for i in range(4)]) if s else value


def exchange(value, axis):
    return lax.all_to_all(value, axis, 0, 0, tiled=True)


def body(inputs, queries, keys, values, output_cotangent, key_value_weight, doc_ids, block_order):
    packed = pl.pallas_call(
        pack_kernel,
        in_specs=[HBM] * 4,
        out_specs=HBM,
        out_shape=shape((CTX, ROWS, PACK_COLS)),
        scratch_shapes=[
            pltpu.VMEM((CTX, ROWS, PACK_COLS), jnp.bfloat16),
            pltpu.SemaphoreType.DMA((4 * CTX,)),
            pltpu.SemaphoreType.DMA((CTX,)),
        ],
        compiler_params=params(56),
        cost_estimate=cost(0, 5_000_000),
    )(queries[0], output_cotangent[0], keys[0], values[0])
    got = exchange(packed, ("y", "x"))

    _, tile = lax.optimization_barrier((packed, key_value_weight))
    for step in range(2):
        mask = (4, 2)[step]
        pairs = [(z * 4 + x, (z ^ mask) * 4 + x) for z in range(8) for x in range(4) if holds(z, x, step)]
        tile = pl.pallas_call(
            functools.partial(take_kernel, step),
            in_specs=[VMEM] * 2,
            out_specs=VMEM,
            out_shape=shape((80, 1024)),
            compiler_params=params(3),
            cost_estimate=cost(0, 500_000),
        )(tile, lax.ppermute(tile, ("z", "x"), pairs))

    def widen(tile, tile_got):
        n = 2 * tile.shape[0]
        return pl.pallas_call(
            join_kernel,
            in_specs=[VMEM] * 2,
            out_specs=VMEM,
            out_shape=shape((n, 80, 1024)),
            compiler_params=params(4),
            cost_estimate=cost(0, n * 330_000),
        )(tile, tile_got)

    tile = widen(tile[None], swap(tile[None], 2))
    got, tile, inputs = lax.optimization_barrier((got, tile, inputs))

    turned = pl.pallas_call(
        turn_kernel,
        in_specs=[VMEM],
        out_specs=[VMEM] * 4,
        out_shape=[shape((FEAT_TILE, ROWS))] * 4,
        scratch_shapes=[
            pltpu.VMEM((FEATURES, ROWS), jnp.float32),
            pltpu.VMEM((4, FEAT_TILE, ROWS), jnp.float32),
        ],
        compiler_params=params(8),
        cost_estimate=cost(0, 1_300_000),
    )(inputs[0])
    got_x = [to_shift(turned[s], s) for s in range(4)]
    tile_got = swap(tile, 1)

    score_grad, keys_turned, keep, send = pl.pallas_call(
        attention_kernel,
        in_specs=[SMEM] * 2 + [VMEM],
        out_specs=[VMEM] * 4,
        out_shape=[
            shape((2, 2, tile_begin(4), 256)),
            shape((HEAD_WIDTH, SLAB)),
            shape((SLAB // 2, 2 * HEAD_WIDTH), jnp.float32),
            shape((SLAB // 2, 2 * HEAD_WIDTH)),
        ],
        scratch_shapes=[
            pltpu.VMEM((SLAB, Q_COLS), jnp.bfloat16),
            pltpu.VMEM((SLAB, Q_COLS), jnp.bfloat16),
            pltpu.VMEM((SLAB, HEAD_WIDTH), jnp.bfloat16),
            pltpu.VMEM((SLAB, HEAD_WIDTH), jnp.bfloat16),
            pltpu.VMEM((SLAB, 2 * HEAD_WIDTH), jnp.float32),
            pltpu.SMEM((32,), jnp.int32),
            pltpu.SMEM((32,), jnp.int32),
        ],
        compiler_params=params(24),
        cost_estimate=cost(10_000_000_000, 5_000_000),
    )(doc_ids[0], block_order, got)

    send, got_x, tile_got = lax.optimization_barrier((send, got_x, tile_got))
    taken = lax.ppermute(send, "y", [(0, 1), (1, 0)])
    dq_near, dq_far = pl.pallas_call(
        query_kernel,
        in_specs=[SMEM] * 2 + [VMEM] * 2,
        out_specs=[VMEM] * 2,
        out_shape=[shape((4, Q_COLS, ROWS))] * 2,
        scratch_shapes=[
            pltpu.VMEM((SLAB, Q_COLS), jnp.bfloat16),
            pltpu.SMEM((32,), jnp.int32),
        ],
        compiler_params=params(12),
        cost_estimate=cost(2_000_000_000, 4_000_000),
    )(doc_ids[0], block_order, score_grad, keys_turned)
    dq_far, tile, tile_got = lax.optimization_barrier((dq_far, tile, tile_got))
    tile = widen(tile, tile_got)
    far_tile = swap(tile, 0)
    taken, dq_near, dq_far, tile = lax.optimization_barrier((taken, dq_near, dq_far, tile))
    own_cols = pl.pallas_call(
        pair_kernel,
        in_specs=[VMEM] * 2,
        out_specs=VMEM,
        out_shape=shape((SLAB // 2, 2 * HEAD_WIDTH)),
        compiler_params=params(6),
        cost_estimate=cost(0, 2_000_000),
    )(keep, taken)
    pieces = [to_shift(own_cols, s) for s in range(4)]
    _, dq_far = lax.optimization_barrier((own_cols, dq_far))
    dq_got = lax.ppermute(dq_far, "y", [(0, 1), (1, 0)])
    pieces, dq_got, far_tile = lax.optimization_barrier((pieces, dq_got, far_tile))

    kv_half, kv_rows, wg_send, wg_keep = pl.pallas_call(
        weight_kernel,
        in_specs=[VMEM] * 8,
        out_specs=[VMEM] * 4,
        out_shape=[
            shape((SLAB // 2, 1024)),
            shape((ROWS, 1024)),
            shape((FEAT_TILE // 2, 1024)),
            shape((FEAT_TILE // 2, 1024), jnp.float32),
        ],
        scratch_shapes=[pltpu.VMEM((FEAT_TILE, SLAB // 2), jnp.bfloat16)],
        compiler_params=params(12),
        cost_estimate=cost(700_000_000, 6_000_000),
    )(*pieces, *got_x)

    wg_got = swap(wg_send, 0)
    parts = pl.pallas_call(
        input_kernel,
        in_specs=[VMEM] * 5,
        out_specs=[VMEM] * 4,
        out_shape=[shape((FEAT_TILE + 2 * Q_COLS, ROWS))] * 4,
        scratch_shapes=[
            pltpu.VMEM((FEAT_TILE, 1024), jnp.bfloat16),
            pltpu.VMEM((4, FEAT_TILE, ROWS), jnp.bfloat16),
        ],
        compiler_params=params(12),
        cost_estimate=cost(700_000_000, 6_000_000),
    )(kv_half, tile, far_tile, dq_near, dq_got)
    wg_got, parts = lax.optimization_barrier((wg_got, parts))
    parts_got = [to_shift(parts[s], s) for s in range(4)]

    def split(number, count, keep, *arrived):
        rows = keep.shape[0] // count
        results = pl.pallas_call(
            functools.partial(split_kernel, number, count),
            in_specs=[VMEM] * (1 + len(arrived)),
            out_specs=[VMEM] * count,
            out_shape=[shape((rows, 1024))] * (count - 1) + [shape((rows, 1024), jnp.float32)],
            scratch_shapes=[pltpu.VMEM((count, rows, 1024), jnp.float32)],
            compiler_params=params(8),
            cost_estimate=cost(0, count * rows * 1024 * 16),
        )(keep, *arrived)
        return results[:-1], results[-1]

    def bit_of(axis, mask):
        return lambda: (lax.axis_index(axis) & mask) // mask

    for axis, mask in (("y", 1), ("yh", 1), ("z", 1), ("z", 2), ("z", 4)):
        sends, wg_keep = split(bit_of(axis, mask), 2, wg_keep, wg_got)
        size = 8 if axis == "z" else 2
        wg_got = lax.ppermute(sends[0], axis, [(i, i ^ mask) for i in range(size)])
    weight_grad = pl.pallas_call(
        add_kernel,
        in_specs=[VMEM] * 2,
        out_specs=VMEM,
        out_shape=shape((10, 1024), jnp.float32),
        compiler_params=params(2),
        cost_estimate=cost(0, 100_000),
    )(wg_keep, wg_got)

    input_grad, query_grad = pl.pallas_call(
        out_kernel,
        in_specs=[VMEM] * 4,
        out_specs=[VMEM] * 2,
        out_shape=[shape((ROWS, FEATURES)), shape((ROWS, HQ * HEAD_WIDTH))],
        compiler_params=params(8),
        cost_estimate=cost(0, 3_300_000),
    )(*parts_got)
    return (input_grad[None], query_grad[None], kv_rows[None], weight_grad)


def solution(mesh):
    axes = ("z", "yh", "core", "y", "x")
    named = jax.sharding.Mesh(mesh.devices.reshape(8, 2, 2, 2, 4), axes)
    fsdp, ctx = axes[:3], axes[3:]
    return jax.shard_map(
        body,
        mesh=named,
        in_specs=(P(fsdp, ctx, None),) * 5 + (P(fsdp, None), P(fsdp, None), P()),
        out_specs=(P(fsdp, ctx, None),) * 3 + (P(axes, None),),
        check_vma=False,
    )
```

```python
import functools
import math

import jax
import jax.numpy as jnp
from jax import lax
from jax.experimental import pallas as pl
from jax.experimental.pallas import tpu as pltpu
from jax.sharding import PartitionSpec as P

HQ = 32
KEY_VALUE_HEADS = 4
HEAD_WIDTH = 128
BLK = 32
QUERY_PER_KEY = 8

CTX = 8
FSDP = 32
ROWS = 128
SLAB = 1024
FEATURES = 2560
FEAT_TILE = FEATURES // 4
Q_COLS = 512
PACK_COLS = 2 * Q_COLS + 2 * HEAD_WIDTH
HALF = 512
SCALE = 1.0 / math.sqrt(HEAD_WIDTH)
LOG2E = math.log2(math.e)
LOWEST = -1e30
NN = (((1,), (0,)), ((), ()))
NT = (((1,), (1,)), ((), ()))
VMEM = pl.BlockSpec(memory_space=pltpu.VMEM)
HBM = pl.BlockSpec(memory_space=pltpu.HBM)
SMEM = pl.BlockSpec(memory_space=pltpu.SMEM)


def dot(a, b, dims):
    return lax.dot_general(a, b, dims, preferred_element_type=jnp.float32)


def shape(dims, kind=jnp.bfloat16):
    return jax.ShapeDtypeStruct(dims, kind)


def params(mib):
    return pltpu.CompilerParams(vmem_limit_bytes=mib * 1024 * 1024)


def cost(flops, moved):
    return pl.CostEstimate(flops=flops, bytes_accessed=moved, transcendentals=0)


def q_block(device):
    return (device % 4) * 2 + device // 4


def pack_kernel(q_ref, d_ref, k_ref, v_ref, out_ref, packed, load_sems, store_sems):
    loads, stores = [], []
    for dest in range(CTX):
        at = q_block(dest) * Q_COLS
        head = (dest % 4) * HEAD_WIDTH
        place = 0
        for ref, first, width in (
            (q_ref, at, Q_COLS),
            (d_ref, at, Q_COLS),
            (k_ref, head, HEAD_WIDTH),
            (v_ref, head, HEAD_WIDTH),
        ):
            load = pltpu.make_async_copy(
                ref.at[:, first : first + width],
                packed.at[dest, :, place : place + width],
                load_sems.at[len(loads)],
            )
            load.start()
            loads.append(load)
            place += width
    for dest in range(CTX):
        for load in loads[4 * dest : 4 * dest + 4]:
            load.wait()
        store = pltpu.make_async_copy(packed.at[dest], out_ref.at[dest], store_sems.at[dest])
        store.start()
        stores.append(store)
    for store in stores:
        store.wait()


def tile_row(z, low, y):
    row = (low % 2) * 320 + y * 160 + (low // 2) * 80
    return row + (z % 2) * 40 + (z // 2 % 2) * 20 + (z // 4) * 10


def turn_kernel(in_ref, *refs):
    outs, turned, tile = refs[:4], refs[4], refs[5]
    for j in range(FEATURES // 128):
        block = in_ref[:, j * 128 : (j + 1) * 128].T
        turned[j * 128 : (j + 1) * 128, :] = block.astype(jnp.float32)
    for x in range(4):
        for low in range(4):
            for y in range(2):
                for z in range(8):
                    source = (z * 4 + low) * 80 + y * 40 + x * 10
                    at = tile_row(z, low, y)
                    tile[x, at : at + 10, :] = turned[source : source + 10, :]
    for s in range(4):
        outs[s][...] = tile[lax.rem(lax.axis_index("x") + s, 4)].astype(jnp.bfloat16)


def place_blocks(docs_ref, order_ref, place):
    first = lax.fori_loop(
        0, 17, lambda i, a: jnp.where(docs_ref[i] == docs_ref[i + 15], i, a), jnp.int32(0)
    )

    def place_block(st, carry):
        b = order_ref[st]
        inside = (b >= first) & (b < first + 16)
        place[st] = jnp.where(inside, b - first, jnp.where(b < first, b + 16, b))
        return carry

    lax.fori_loop(0, 32, place_block, 0)
    return first


def tile_begin(i):
    return 64 * i * (i + 1)


def attention_kernel(docs_ref, order_ref, *refs):
    in_ref, grad_ref, kt_ref, keep_ref, send_ref = refs[:5]
    q_s, d_s, k_s, v_s, dkv_s, place, begin = refs[5:]
    first = place_blocks(docs_ref, order_ref, place)

    def begin_block(t, carry):
        last_doc, last_begin = carry
        doc = docs_ref[jnp.where(t < first, t, t + 16)]
        now = jnp.where(doc == last_doc, last_begin, t)
        begin[t] = jnp.int32(0)
        begin[t + 16] = now * BLK
        return doc, now

    lax.fori_loop(0, 16, begin_block, (jnp.int32(-1), jnp.int32(0)))

    for st in range(32):
        rows = pl.ds(pl.multiple_of(place[st] * BLK, BLK), BLK)
        src, block = st // 4, slice((st % 4) * BLK, (st % 4 + 1) * BLK)
        q_s[rows, :] = in_ref[src, block, 0:Q_COLS]
        d_s[rows, :] = in_ref[src, block, Q_COLS : 2 * Q_COLS]
        k_s[rows, :] = in_ref[src, block, 2 * Q_COLS : 2 * Q_COLS + HEAD_WIDTH]
        v_s[rows, :] = in_ref[src, block, 2 * Q_COLS + HEAD_WIDTH :]
    for j in range(SLAB // 128):
        kt_ref[:, j * 128 : (j + 1) * 128] = k_s[j * 128 : (j + 1) * 128, :].T
    dkv_s[...] = jnp.zeros_like(dkv_s)

    def half(hf, carry):
        base = pl.multiple_of(hf * HALF, HALF)
        for i in range(HALF // 128):
            n = (i + 1) * 128
            rows = pl.ds(pl.multiple_of(base + i * 128, 128), 128)
            keys = pl.ds(base, n)
            key_n = k_s[keys, :]
            value_n = v_s[keys, :]
            lane = lax.broadcasted_iota(jnp.int32, (n, 128), 1)
            row = lax.broadcasted_iota(jnp.int32, (n, 128), 0)
            low = jnp.zeros((n, 128), jnp.int32)
            for kk in range(4):
                low = jnp.where(lane // BLK == kk, begin[hf * 16 + i * 4 + kk], low)
            seen = (row >= low) & (row <= lane + i * 128)
            bias = jnp.where(seen, 0.0, LOWEST)
            bias = jnp.concatenate([bias, bias], axis=1)
            q_rows = [q_s[rows, e * 128 : (e + 1) * 128] for e in range(4)]
            d_rows = [d_s[rows, e * 128 : (e + 1) * 128] for e in range(4)]
            grads, lows = [], []
            for g in range(2):
                qs = jnp.concatenate(q_rows[2 * g : 2 * g + 2], axis=0)
                ds = jnp.concatenate(d_rows[2 * g : 2 * g + 2], axis=0)
                scores = dot(key_n, qs, NT) * (SCALE * LOG2E) + bias
                top = jnp.max(scores, axis=0, keepdims=True)
                weights = jnp.exp2(scores - top)
                share = 1.0 / jnp.sum(weights, axis=0, keepdims=True)
                products = dot(value_n, ds, NT)
                delta = jnp.sum(weights * products, axis=0, keepdims=True) * share
                probs = weights * share
                grads.append((probs * (products - delta)).astype(jnp.bfloat16))
                lows.append(probs.astype(jnp.bfloat16))
                grad_ref[hf, g, tile_begin(i) : tile_begin(i) + n, :] = grads[g]
            dkv_s[keys, 0:128] += dot(
                jnp.concatenate(grads, axis=1), jnp.concatenate(q_rows, axis=0), NN
            )
            dkv_s[keys, 128:256] += dot(
                jnp.concatenate(lows, axis=1), jnp.concatenate(d_rows, axis=0), NN
            )
        return carry

    lax.fori_loop(0, 2, half, 0)

    y = lax.axis_index("y")
    for t in range(16):
        block = slice(t * BLK, (t + 1) * BLK)
        for half_y, ref in ((y, keep_ref), (1 - y, send_ref)):
            rows = pl.ds(pl.multiple_of(place[half_y * 16 + t] * BLK, BLK), BLK)
            ref[block, 0:128] = (dkv_s[rows, 0:128] * SCALE).astype(ref.dtype)
            ref[block, 128:256] = dkv_s[rows, 128:256].astype(ref.dtype)

def query_kernel(docs_ref, order_ref, grad_ref, kt_ref, near_ref, far_ref, dq_s, place):
    place_blocks(docs_ref, order_ref, place)
    for hf in range(2):
        for i in range(HALF // 128):
            n = (i + 1) * 128
            rows = slice(hf * HALF + i * 128, hf * HALF + (i + 1) * 128)
            for g in range(2):
                part = grad_ref[hf, g, tile_begin(i) : tile_begin(i) + n, :]
                dqt = dot(kt_ref[:, hf * HALF : hf * HALF + n], part, NN) * SCALE
                for e in range(2):
                    at = (2 * g + e) * 128
                    block = dqt[:, e * 128 : (e + 1) * 128].T
                    dq_s[rows, at : at + 128] = block.astype(jnp.bfloat16)
    y = lax.axis_index("y")
    for t in range(16):
        for half_y, ref in ((y, near_ref), (1 - y, far_ref)):
            rows = pl.ds(pl.multiple_of(place[half_y * 16 + t] * BLK, BLK), BLK)
            for g in range(4):
                at = g * 128 + (t % 4) * BLK
                ref[t // 4, at : at + BLK, :] = dq_s[rows, g * 128 : (g + 1) * 128]


def pair_kernel(keep_ref, taken_ref, out_ref):
    out_ref[...] = (keep_ref[...] + taken_ref[...].astype(jnp.float32)).astype(jnp.bfloat16)


def weight_kernel(*refs):
    pieces, ins = refs[:4], refs[4:8]
    kv_ref, kv_rows_ref, send_ref, keep_ref, x_s = refs[8:]
    core, x = lax.axis_index("core"), lax.axis_index("x")
    for s in range(4):
        at = pl.multiple_of(lax.rem(x + 4 - s, 4) * 128, 128)
        kv_ref[:, pl.ds(at, 128)] = pieces[s][:, 0:128]
        kv_ref[:, pl.ds(pl.multiple_of(512 + at, 128), 128)] = pieces[s][:, 128:256]
        x_s[:, pl.ds(at, 128)] = ins[s][...]
    part = FEAT_TILE // 2
    other = pl.ds(pl.multiple_of((1 - core) * part, part), part)
    own = pl.ds(pl.multiple_of(core * part, part), part)
    for j in range(4):
        cols = slice(j * 256, (j + 1) * 256)
        send_ref[:, cols] = dot(x_s[other, :], kv_ref[:, cols], NN).astype(jnp.bfloat16)
        keep_ref[:, cols] = dot(x_s[own, :], kv_ref[:, cols], NN)
    kv_rows_ref[...] = kv_ref[pl.ds(pl.multiple_of(x * ROWS, ROWS), ROWS), :]


def split_kernel(number, count, *refs):
    count_in = len(refs) - count - 1
    ins, sends, keep_ref, parts = refs[:count_in], refs[count_in:-2], refs[-2], refs[-1]
    total = ins[0][...]
    for ref in ins[1:]:
        total = total + ref[...].astype(jnp.float32)
    rows = keep_ref.shape[0]
    for k in range(count):
        parts[k] = total[k * rows : (k + 1) * rows, :]
    own = number()
    keep_ref[...] = parts[own]
    for k in range(1, count):
        sends[k - 1][...] = parts[own ^ k].astype(jnp.bfloat16)


def add_kernel(keep_ref, got_ref, out_ref):
    out_ref[...] = keep_ref[...] + got_ref[...].astype(jnp.float32)


def holds(z, x, step):
    return z // 2 == x if step == 0 else z // 2 % 2 == x % 2


def take_kernel(step, own_ref, got_ref, out_ref):
    own = holds(lax.axis_index("z"), lax.axis_index("x"), step)
    out_ref[...] = jnp.where(own, own_ref[...], got_ref[...])


def join_kernel(near_ref, far_ref, out_ref):
    n = near_ref.shape[0]
    out_ref[0:n] = near_ref[...]
    out_ref[n:] = far_ref[...]


def input_kernel(kv_ref, w_ref, far_ref, dq_ref, dq_got_ref, *refs):
    outs, w_s, tile = refs[:4], refs[4], refs[5]
    z, yh, core = lax.axis_index("z"), lax.axis_index("yh"), lax.axis_index("core")
    x, y = lax.axis_index("x"), lax.axis_index("y")
    for at in range(8):
        shard = ((z & 1) ^ (at & 1)) * 4 + (yh ^ (at // 2 % 2)) * 2 + (core ^ (at // 4))
        rows = pl.ds(pl.multiple_of(shard * 80, 80), 80)
        w_s[rows, :] = w_ref[at] if at < 4 else far_ref[at - 4]
    for j in range(2):
        rows = slice(j * 256, (j + 1) * 256)
        block = dot(w_s[...], kv_ref[rows, :], NT).astype(jnp.bfloat16)
        tile[2 * j] = block[:, 0:128]
        tile[2 * j + 1] = block[:, 128:256]
    near = pl.multiple_of(FEAT_TILE + y * Q_COLS, 128)
    far = pl.multiple_of(FEAT_TILE + (1 - y) * Q_COLS, 128)
    for s in range(4):
        dest = lax.rem(x + s, 4)
        outs[s][0:FEAT_TILE, :] = tile[dest]
        outs[s][pl.ds(near, Q_COLS), :] = dq_ref[dest]
        outs[s][pl.ds(far, Q_COLS), :] = dq_got_ref[dest]


def out_kernel(*refs):
    parts, input_ref, query_ref = refs[:4], refs[4], refs[5]
    x = lax.axis_index("x")
    for s in range(4):
        src = lax.rem(x + 4 - s, 4)
        for j in range(FEAT_TILE // 128):
            cols = pl.ds(pl.multiple_of(src * FEAT_TILE + j * 128, 128), 128)
            input_ref[:, cols] = parts[s][j * 128 : (j + 1) * 128, :].T
        for g in range(8):
            cols = pl.ds(pl.multiple_of(src * 2 * Q_COLS + g * 128, 128), 128)
            at = FEAT_TILE + g * 128
            query_ref[:, cols] = parts[s][at : at + 128, :]


BIT_AXES = (("core", 1), ("yh", 1), ("z", 1), ("z", 2), ("z", 4))


def swap(value, bit):
    axis, mask = BIT_AXES[bit]
    return lax.ppermute(value, axis, [(i, i ^ mask) for i in range(8 if axis == "z" else 2)])


def to_shift(value, s):
    return lax.ppermute(value, "x", [(i, (i + s) % 4) for i in range(4)]) if s else value


def exchange(value, axis):
    return lax.all_to_all(value, axis, 0, 0, tiled=True)


def body(inputs, queries, keys, values, output_cotangent, key_value_weight, doc_ids, block_order):
    packed = pl.pallas_call(
        pack_kernel,
        in_specs=[HBM] * 4,
        out_specs=HBM,
        out_shape=shape((CTX, ROWS, PACK_COLS)),
        scratch_shapes=[
            pltpu.VMEM((CTX, ROWS, PACK_COLS), jnp.bfloat16),
            pltpu.SemaphoreType.DMA((4 * CTX,)),
            pltpu.SemaphoreType.DMA((CTX,)),
        ],
        compiler_params=params(56),
        cost_estimate=cost(0, 5_000_000),
    )(queries[0], output_cotangent[0], keys[0], values[0])
    got = exchange(packed, ("y", "x"))

    _, tile = lax.optimization_barrier((packed, key_value_weight))
    for step in range(2):
        mask = (4, 2)[step]
        pairs = [(z * 4 + x, (z ^ mask) * 4 + x) for z in range(8) for x in range(4) if holds(z, x, step)]
        tile = pl.pallas_call(
            functools.partial(take_kernel, step),
            in_specs=[VMEM] * 2,
            out_specs=VMEM,
            out_shape=shape((80, 1024)),
            compiler_params=params(3),
            cost_estimate=cost(0, 500_000),
        )(tile, lax.ppermute(tile, ("z", "x"), pairs))

    def widen(tile, tile_got):
        n = 2 * tile.shape[0]
        return pl.pallas_call(
            join_kernel,
            in_specs=[VMEM] * 2,
            out_specs=VMEM,
            out_shape=shape((n, 80, 1024)),
            compiler_params=params(4),
            cost_estimate=cost(0, n * 330_000),
        )(tile, tile_got)

    tile = widen(tile[None], swap(tile[None], 2))
    turned = pl.pallas_call(
        turn_kernel,
        in_specs=[VMEM],
        out_specs=[VMEM] * 4,
        out_shape=[shape((FEAT_TILE, ROWS))] * 4,
        scratch_shapes=[
            pltpu.VMEM((FEATURES, ROWS), jnp.float32),
            pltpu.VMEM((4, FEAT_TILE, ROWS), jnp.float32),
        ],
        compiler_params=params(8),
        cost_estimate=cost(0, 1_300_000),
    )(inputs[0])
    got_x = [to_shift(turned[s], s) for s in range(4)]
    tile_got = swap(tile, 1)

    score_grad, keys_turned, keep, send = pl.pallas_call(
        attention_kernel,
        in_specs=[SMEM] * 2 + [VMEM],
        out_specs=[VMEM] * 4,
        out_shape=[
            shape((2, 2, tile_begin(4), 256)),
            shape((HEAD_WIDTH, SLAB)),
            shape((SLAB // 2, 2 * HEAD_WIDTH), jnp.float32),
            shape((SLAB // 2, 2 * HEAD_WIDTH)),
        ],
        scratch_shapes=[
            pltpu.VMEM((SLAB, Q_COLS), jnp.bfloat16),
            pltpu.VMEM((SLAB, Q_COLS), jnp.bfloat16),
            pltpu.VMEM((SLAB, HEAD_WIDTH), jnp.bfloat16),
            pltpu.VMEM((SLAB, HEAD_WIDTH), jnp.bfloat16),
            pltpu.VMEM((SLAB, 2 * HEAD_WIDTH), jnp.float32),
            pltpu.SMEM((32,), jnp.int32),
            pltpu.SMEM((32,), jnp.int32),
        ],
        compiler_params=params(24),
        cost_estimate=cost(0, 5_000),
    )(doc_ids[0], block_order, got)

    send, got_x, tile_got = lax.optimization_barrier((send, got_x, tile_got))
    taken = lax.ppermute(send, "y", [(0, 1), (1, 0)])
    dq_near, dq_far = pl.pallas_call(
        query_kernel,
        in_specs=[SMEM] * 2 + [VMEM] * 2,
        out_specs=[VMEM] * 2,
        out_shape=[shape((4, Q_COLS, ROWS))] * 2,
        scratch_shapes=[
            pltpu.VMEM((SLAB, Q_COLS), jnp.bfloat16),
            pltpu.SMEM((32,), jnp.int32),
        ],
        compiler_params=params(12),
        cost_estimate=cost(2_000_000_000, 4_000_000),
    )(doc_ids[0], block_order, score_grad, keys_turned)
    dq_far, tile, tile_got = lax.optimization_barrier((dq_far, tile, tile_got))
    tile = widen(tile, tile_got)
    far_tile = swap(tile, 0)
    taken, dq_near, dq_far, tile = lax.optimization_barrier((taken, dq_near, dq_far, tile))
    own_cols = pl.pallas_call(
        pair_kernel,
        in_specs=[VMEM] * 2,
        out_specs=VMEM,
        out_shape=shape((SLAB // 2, 2 * HEAD_WIDTH)),
        compiler_params=params(6),
        cost_estimate=cost(0, 2_000_000),
    )(keep, taken)
    pieces = [to_shift(own_cols, s) for s in range(4)]
    _, dq_far = lax.optimization_barrier((own_cols, dq_far))
    dq_got = lax.ppermute(dq_far, "y", [(0, 1), (1, 0)])
    pieces, dq_got, far_tile = lax.optimization_barrier((pieces, dq_got, far_tile))

    kv_half, kv_rows, wg_send, wg_keep = pl.pallas_call(
        weight_kernel,
        in_specs=[VMEM] * 8,
        out_specs=[VMEM] * 4,
        out_shape=[
            shape((SLAB // 2, 1024)),
            shape((ROWS, 1024)),
            shape((FEAT_TILE // 2, 1024)),
            shape((FEAT_TILE // 2, 1024), jnp.float32),
        ],
        scratch_shapes=[pltpu.VMEM((FEAT_TILE, SLAB // 2), jnp.bfloat16)],
        compiler_params=params(12),
        cost_estimate=cost(700_000_000, 6_000_000),
    )(*pieces, *got_x)

    wg_got = swap(wg_send, 0)
    parts = pl.pallas_call(
        input_kernel,
        in_specs=[VMEM] * 5,
        out_specs=[VMEM] * 4,
        out_shape=[shape((FEAT_TILE + 2 * Q_COLS, ROWS))] * 4,
        scratch_shapes=[
            pltpu.VMEM((FEAT_TILE, 1024), jnp.bfloat16),
            pltpu.VMEM((4, FEAT_TILE, ROWS), jnp.bfloat16),
        ],
        compiler_params=params(12),
        cost_estimate=cost(700_000_000, 6_000_000),
    )(kv_half, tile, far_tile, dq_near, dq_got)
    wg_got, parts = lax.optimization_barrier((wg_got, parts))
    parts_got = [to_shift(parts[s], s) for s in range(4)]

    def split(number, count, keep, *arrived):
        rows = keep.shape[0] // count
        results = pl.pallas_call(
            functools.partial(split_kernel, number, count),
            in_specs=[VMEM] * (1 + len(arrived)),
            out_specs=[VMEM] * count,
            out_shape=[shape((rows, 1024))] * (count - 1) + [shape((rows, 1024), jnp.float32)],
            scratch_shapes=[pltpu.VMEM((count, rows, 1024), jnp.float32)],
            compiler_params=params(8),
            cost_estimate=cost(0, count * rows * 1024 * 16),
        )(keep, *arrived)
        return results[:-1], results[-1]

    def bit_of(axis, mask):
        return lambda: (lax.axis_index(axis) & mask) // mask

    for axis, mask in (("y", 1), ("yh", 1), ("z", 1), ("z", 2), ("z", 4)):
        sends, wg_keep = split(bit_of(axis, mask), 2, wg_keep, wg_got)
        size = 8 if axis == "z" else 2
        wg_got = lax.ppermute(sends[0], axis, [(i, i ^ mask) for i in range(size)])
    weight_grad = pl.pallas_call(
        add_kernel,
        in_specs=[VMEM] * 2,
        out_specs=VMEM,
        out_shape=shape((10, 1024), jnp.float32),
        compiler_params=params(2),
        cost_estimate=cost(0, 100_000),
    )(wg_keep, wg_got)

    input_grad, query_grad = pl.pallas_call(
        out_kernel,
        in_specs=[VMEM] * 4,
        out_specs=[VMEM] * 2,
        out_shape=[shape((ROWS, FEATURES)), shape((ROWS, HQ * HEAD_WIDTH))],
        compiler_params=params(8),
        cost_estimate=cost(0, 3_300_000),
    )(*parts_got)
    return (input_grad[None], query_grad[None], kv_rows[None], weight_grad)


def solution(mesh):
    axes = ("z", "yh", "core", "y", "x")
    named = jax.sharding.Mesh(mesh.devices.reshape(8, 2, 2, 2, 4), axes)
    fsdp, ctx = axes[:3], axes[3:]
    return jax.shard_map(
        body,
        mesh=named,
        in_specs=(P(fsdp, ctx, None),) * 5 + (P(fsdp, None), P(fsdp, None), P()),
        out_specs=(P(fsdp, ctx, None),) * 3 + (P(axes, None),),
        check_vma=False,
    )
```

```python
import functools
import math

import jax
import jax.numpy as jnp
from jax import lax
from jax.experimental import pallas as pl
from jax.experimental.pallas import tpu as pltpu
from jax.sharding import PartitionSpec as P

HQ = 32
KEY_VALUE_HEADS = 4
HEAD_WIDTH = 128
BLK = 32
QUERY_PER_KEY = 8

CTX = 8
FSDP = 32
ROWS = 128
SLAB = 1024
FEATURES = 2560
FEAT_TILE = FEATURES // 4
Q_COLS = 512
PACK_COLS = 2 * Q_COLS + 2 * HEAD_WIDTH
HALF = 512
SCALE = 1.0 / math.sqrt(HEAD_WIDTH)
LOG2E = math.log2(math.e)
LOWEST = -1e30
NN = (((1,), (0,)), ((), ()))
NT = (((1,), (1,)), ((), ()))
VMEM = pl.BlockSpec(memory_space=pltpu.VMEM)
HBM = pl.BlockSpec(memory_space=pltpu.HBM)
SMEM = pl.BlockSpec(memory_space=pltpu.SMEM)


def dot(a, b, dims):
    return lax.dot_general(a, b, dims, preferred_element_type=jnp.float32)


def shape(dims, kind=jnp.bfloat16):
    return jax.ShapeDtypeStruct(dims, kind)


def params(mib):
    return pltpu.CompilerParams(vmem_limit_bytes=mib * 1024 * 1024)


def cost(flops, moved):
    return pl.CostEstimate(flops=flops, bytes_accessed=moved, transcendentals=0)


def q_block(device):
    return (device % 4) * 2 + device // 4


def pack_kernel(q_ref, d_ref, k_ref, v_ref, out_ref, packed, load_sems, store_sems):
    loads, stores = [], []
    for dest in range(CTX):
        at = q_block(dest) * Q_COLS
        head = (dest % 4) * HEAD_WIDTH
        place = 0
        for ref, first, width in (
            (q_ref, at, Q_COLS),
            (d_ref, at, Q_COLS),
            (k_ref, head, HEAD_WIDTH),
            (v_ref, head, HEAD_WIDTH),
        ):
            load = pltpu.make_async_copy(
                ref.at[:, first : first + width],
                packed.at[dest, :, place : place + width],
                load_sems.at[len(loads)],
            )
            load.start()
            loads.append(load)
            place += width
    for dest in range(CTX):
        for load in loads[4 * dest : 4 * dest + 4]:
            load.wait()
        store = pltpu.make_async_copy(packed.at[dest], out_ref.at[dest], store_sems.at[dest])
        store.start()
        stores.append(store)
    for store in stores:
        store.wait()


def tile_row(z, low, y):
    row = (low % 2) * 320 + y * 160 + (z % 2) * 80
    return row + (low // 2) * 40 + (z // 2 % 2) * 20 + (z // 4) * 10


def turn_kernel(in_ref, *refs):
    outs, turned, tile = refs[:4], refs[4], refs[5]
    for j in range(FEATURES // 128):
        block = in_ref[:, j * 128 : (j + 1) * 128].T
        turned[j * 128 : (j + 1) * 128, :] = block.astype(jnp.float32)
    for x in range(4):
        for low in range(4):
            for y in range(2):
                for z in range(8):
                    source = (z * 4 + low) * 80 + y * 40 + x * 10
                    at = tile_row(z, low, y)
                    tile[x, at : at + 10, :] = turned[source : source + 10, :]
    for s in range(4):
        outs[s][...] = tile[lax.rem(lax.axis_index("x") + s, 4)].astype(jnp.bfloat16)


def place_blocks(docs_ref, order_ref, place):
    first = lax.fori_loop(
        0, 17, lambda i, a: jnp.where(docs_ref[i] == docs_ref[i + 15], i, a), jnp.int32(0)
    )

    def place_block(st, carry):
        b = order_ref[st]
        inside = (b >= first) & (b < first + 16)
        place[st] = jnp.where(inside, b - first, jnp.where(b < first, b + 16, b))
        return carry

    lax.fori_loop(0, 32, place_block, 0)
    return first


def tile_begin(i):
    return 64 * i * (i + 1)


def attention_kernel(docs_ref, order_ref, *refs):
    in_ref, grad_ref, kt_ref, keep_ref, send_ref = refs[:5]
    q_s, d_s, k_s, v_s, dkv_s, place, begin = refs[5:]
    first = place_blocks(docs_ref, order_ref, place)

    def begin_block(t, carry):
        last_doc, last_begin = carry
        doc = docs_ref[jnp.where(t < first, t, t + 16)]
        now = jnp.where(doc == last_doc, last_begin, t)
        begin[t] = jnp.int32(0)
        begin[t + 16] = now * BLK
        return doc, now

    lax.fori_loop(0, 16, begin_block, (jnp.int32(-1), jnp.int32(0)))

    for st in range(32):
        rows = pl.ds(pl.multiple_of(place[st] * BLK, BLK), BLK)
        src, block = st // 4, slice((st % 4) * BLK, (st % 4 + 1) * BLK)
        q_s[rows, :] = in_ref[src, block, 0:Q_COLS]
        d_s[rows, :] = in_ref[src, block, Q_COLS : 2 * Q_COLS]
        k_s[rows, :] = in_ref[src, block, 2 * Q_COLS : 2 * Q_COLS + HEAD_WIDTH]
        v_s[rows, :] = in_ref[src, block, 2 * Q_COLS + HEAD_WIDTH :]
    for j in range(SLAB // 128):
        kt_ref[:, j * 128 : (j + 1) * 128] = k_s[j * 128 : (j + 1) * 128, :].T
    dkv_s[...] = jnp.zeros_like(dkv_s)

    def half(hf, carry):
        base = pl.multiple_of(hf * HALF, HALF)
        for i in range(HALF // 128):
            n = (i + 1) * 128
            rows = pl.ds(pl.multiple_of(base + i * 128, 128), 128)
            keys = pl.ds(base, n)
            key_n = k_s[keys, :]
            value_n = v_s[keys, :]
            lane = lax.broadcasted_iota(jnp.int32, (n, 128), 1)
            row = lax.broadcasted_iota(jnp.int32, (n, 128), 0)
            low = jnp.zeros((n, 128), jnp.int32)
            for kk in range(4):
                low = jnp.where(lane // BLK == kk, begin[hf * 16 + i * 4 + kk], low)
            seen = (row >= low) & (row <= lane + i * 128)
            bias = jnp.where(seen, 0.0, LOWEST)
            bias = jnp.concatenate([bias, bias], axis=1)
            q_rows = [q_s[rows, e * 128 : (e + 1) * 128] for e in range(4)]
            d_rows = [d_s[rows, e * 128 : (e + 1) * 128] for e in range(4)]
            grads, lows = [], []
            for g in range(2):
                qs = jnp.concatenate(q_rows[2 * g : 2 * g + 2], axis=0)
                ds = jnp.concatenate(d_rows[2 * g : 2 * g + 2], axis=0)
                scores = dot(key_n, qs, NT) * (SCALE * LOG2E) + bias
                top = jnp.max(scores, axis=0, keepdims=True)
                weights = jnp.exp2(scores - top)
                share = 1.0 / jnp.sum(weights, axis=0, keepdims=True)
                products = dot(value_n, ds, NT)
                delta = jnp.sum(weights * products, axis=0, keepdims=True) * share
                probs = weights * share
                grads.append((probs * (products - delta)).astype(jnp.bfloat16))
                lows.append(probs.astype(jnp.bfloat16))
                grad_ref[hf, g, tile_begin(i) : tile_begin(i) + n, :] = grads[g]
            dkv_s[keys, 0:128] += dot(
                jnp.concatenate(grads, axis=1), jnp.concatenate(q_rows, axis=0), NN
            )
            dkv_s[keys, 128:256] += dot(
                jnp.concatenate(lows, axis=1), jnp.concatenate(d_rows, axis=0), NN
            )
        return carry

    lax.fori_loop(0, 2, half, 0)

    y = lax.axis_index("y")
    for t in range(16):
        block = slice(t * BLK, (t + 1) * BLK)
        for half_y, ref in ((y, keep_ref), (1 - y, send_ref)):
            rows = pl.ds(pl.multiple_of(place[half_y * 16 + t] * BLK, BLK), BLK)
            ref[block, 0:128] = (dkv_s[rows, 0:128] * SCALE).astype(ref.dtype)
            ref[block, 128:256] = dkv_s[rows, 128:256].astype(ref.dtype)

def query_kernel(docs_ref, order_ref, grad_ref, kt_ref, near_ref, far_ref, dq_s, place):
    place_blocks(docs_ref, order_ref, place)
    for hf in range(2):
        for i in range(HALF // 128):
            n = (i + 1) * 128
            rows = slice(hf * HALF + i * 128, hf * HALF + (i + 1) * 128)
            for g in range(2):
                part = grad_ref[hf, g, tile_begin(i) : tile_begin(i) + n, :]
                dqt = dot(kt_ref[:, hf * HALF : hf * HALF + n], part, NN) * SCALE
                for e in range(2):
                    at = (2 * g + e) * 128
                    block = dqt[:, e * 128 : (e + 1) * 128].T
                    dq_s[rows, at : at + 128] = block.astype(jnp.bfloat16)
    y = lax.axis_index("y")
    for t in range(16):
        for half_y, ref in ((y, near_ref), (1 - y, far_ref)):
            rows = pl.ds(pl.multiple_of(place[half_y * 16 + t] * BLK, BLK), BLK)
            for g in range(4):
                at = g * 128 + (t % 4) * BLK
                ref[t // 4, at : at + BLK, :] = dq_s[rows, g * 128 : (g + 1) * 128]


def pair_kernel(keep_ref, taken_ref, out_ref):
    out_ref[...] = (keep_ref[...] + taken_ref[...].astype(jnp.float32)).astype(jnp.bfloat16)


def rows_kernel(*refs):
    ins, out_ref = refs[:4], refs[4]
    for s in range(4):
        at = pl.multiple_of(lax.rem(lax.axis_index("x") + 4 - s, 4) * 128, 128)
        out_ref[:, pl.ds(at, 128)] = ins[s][...]


def weight_kernel(*refs):
    pieces, x_s = refs[:4], refs[4]
    kv_ref, kv_rows_ref, send_ref, keep_ref = refs[5:]
    core, x = lax.axis_index("core"), lax.axis_index("x")
    for s in range(4):
        at = pl.multiple_of(lax.rem(x + 4 - s, 4) * 128, 128)
        kv_ref[:, pl.ds(at, 128)] = pieces[s][:, 0:128]
        kv_ref[:, pl.ds(pl.multiple_of(512 + at, 128), 128)] = pieces[s][:, 128:256]
    part = FEAT_TILE // 2
    other = pl.ds(pl.multiple_of((1 - core) * part, part), part)
    own = pl.ds(pl.multiple_of(core * part, part), part)
    for j in range(4):
        cols = slice(j * 256, (j + 1) * 256)
        send_ref[:, cols] = dot(x_s[other, :], kv_ref[:, cols], NN).astype(jnp.bfloat16)
        keep_ref[:, cols] = dot(x_s[own, :], kv_ref[:, cols], NN)
    kv_rows_ref[...] = kv_ref[pl.ds(pl.multiple_of(x * ROWS, ROWS), ROWS), :]


def split_kernel(number, count, *refs):
    count_in = len(refs) - count - 1
    ins, sends, keep_ref, parts = refs[:count_in], refs[count_in:-2], refs[-2], refs[-1]
    total = ins[0][...]
    for ref in ins[1:]:
        total = total + ref[...].astype(jnp.float32)
    rows = keep_ref.shape[0]
    for k in range(count):
        parts[k] = total[k * rows : (k + 1) * rows, :]
    own = number()
    keep_ref[...] = parts[own]
    for k in range(1, count):
        sends[k - 1][...] = parts[own ^ k].astype(jnp.bfloat16)


def add_kernel(keep_ref, got_ref, out_ref):
    out_ref[...] = keep_ref[...] + got_ref[...].astype(jnp.float32)


def holds(z, x, step):
    return z // 2 == x if step == 0 else z // 2 % 2 == x % 2


def take_kernel(step, own_ref, got_ref, out_ref):
    own = holds(lax.axis_index("z"), lax.axis_index("x"), step)
    out_ref[...] = jnp.where(own, own_ref[...], got_ref[...])


def join_kernel(near_ref, far_ref, out_ref):
    n = near_ref.shape[0]
    out_ref[0:n] = near_ref[...]
    out_ref[n:] = far_ref[...]


def input_kernel(kv_ref, w_ref, far_ref, dq_ref, dq_got_ref, *refs):
    outs, w_s, tile = refs[:4], refs[4], refs[5]
    z, yh, core = lax.axis_index("z"), lax.axis_index("yh"), lax.axis_index("core")
    x, y = lax.axis_index("x"), lax.axis_index("y")
    for at in range(8):
        shard = ((z & 1) ^ (at & 1)) * 4 + (yh ^ (at // 2 % 2)) * 2 + (core ^ (at // 4))
        rows = pl.ds(pl.multiple_of(shard * 80, 80), 80)
        w_s[rows, :] = w_ref[at] if at < 4 else far_ref[at - 4]
    for j in range(2):
        rows = slice(j * 256, (j + 1) * 256)
        block = dot(w_s[...], kv_ref[rows, :], NT).astype(jnp.bfloat16)
        tile[2 * j] = block[:, 0:128]
        tile[2 * j + 1] = block[:, 128:256]
    near = pl.multiple_of(FEAT_TILE + y * Q_COLS, 128)
    far = pl.multiple_of(FEAT_TILE + (1 - y) * Q_COLS, 128)
    for s in range(4):
        dest = lax.rem(x + s, 4)
        outs[s][0:FEAT_TILE, :] = tile[dest]
        outs[s][pl.ds(near, Q_COLS), :] = dq_ref[dest]
        outs[s][pl.ds(far, Q_COLS), :] = dq_got_ref[dest]


def out_kernel(*refs):
    parts, input_ref, query_ref = refs[:4], refs[4], refs[5]
    x = lax.axis_index("x")
    for s in range(4):
        src = lax.rem(x + 4 - s, 4)
        for j in range(FEAT_TILE // 128):
            cols = pl.ds(pl.multiple_of(src * FEAT_TILE + j * 128, 128), 128)
            input_ref[:, cols] = parts[s][j * 128 : (j + 1) * 128, :].T
        for g in range(8):
            cols = pl.ds(pl.multiple_of(src * 2 * Q_COLS + g * 128, 128), 128)
            at = FEAT_TILE + g * 128
            query_ref[:, cols] = parts[s][at : at + 128, :]


BIT_AXES = (("core", 1), ("yh", 1), ("z", 1), ("z", 2), ("z", 4))


def swap(value, bit):
    axis, mask = BIT_AXES[bit]
    return lax.ppermute(value, axis, [(i, i ^ mask) for i in range(8 if axis == "z" else 2)])


def to_shift(value, s):
    return lax.ppermute(value, "x", [(i, (i + s) % 4) for i in range(4)]) if s else value


def exchange(value, axis):
    return lax.all_to_all(value, axis, 0, 0, tiled=True)


def body(inputs, queries, keys, values, output_cotangent, key_value_weight, doc_ids, block_order):
    packed = pl.pallas_call(
        pack_kernel,
        in_specs=[HBM] * 4,
        out_specs=HBM,
        out_shape=shape((CTX, ROWS, PACK_COLS)),
        scratch_shapes=[
            pltpu.VMEM((CTX, ROWS, PACK_COLS), jnp.bfloat16),
            pltpu.SemaphoreType.DMA((4 * CTX,)),
            pltpu.SemaphoreType.DMA((CTX,)),
        ],
        compiler_params=params(56),
        cost_estimate=cost(0, 5_000_000),
    )(queries[0], output_cotangent[0], keys[0], values[0])
    got = exchange(packed, ("y", "x"))

    _, tile = lax.optimization_barrier((packed, key_value_weight))
    for step in range(2):
        mask = (4, 2)[step]
        pairs = [(z * 4 + x, (z ^ mask) * 4 + x) for z in range(8) for x in range(4) if holds(z, x, step)]
        tile = pl.pallas_call(
            functools.partial(take_kernel, step),
            in_specs=[VMEM] * 2,
            out_specs=VMEM,
            out_shape=shape((80, 1024)),
            compiler_params=params(3),
            cost_estimate=cost(0, 500_000),
        )(tile, lax.ppermute(tile, ("z", "x"), pairs))

    def widen(tile, tile_got):
        n = 2 * tile.shape[0]
        return pl.pallas_call(
            join_kernel,
            in_specs=[VMEM] * 2,
            out_specs=VMEM,
            out_shape=shape((n, 80, 1024)),
            compiler_params=params(4),
            cost_estimate=cost(0, n * 330_000),
        )(tile, tile_got)

    tile = widen(tile[None], swap(tile[None], 2))
    turned = pl.pallas_call(
        turn_kernel,
        in_specs=[VMEM],
        out_specs=[VMEM] * 4,
        out_shape=[shape((FEAT_TILE, ROWS))] * 4,
        scratch_shapes=[
            pltpu.VMEM((FEATURES, ROWS), jnp.float32),
            pltpu.VMEM((4, FEAT_TILE, ROWS), jnp.float32),
        ],
        compiler_params=params(8),
        cost_estimate=cost(0, 1_300_000),
    )(inputs[0])
    got_x = [to_shift(turned[s], s) for s in range(4)]
    tile_got = swap(tile, 1)

    score_grad, keys_turned, keep, send = pl.pallas_call(
        attention_kernel,
        in_specs=[SMEM] * 2 + [VMEM],
        out_specs=[VMEM] * 4,
        out_shape=[
            shape((2, 2, tile_begin(4), 256)),
            shape((HEAD_WIDTH, SLAB)),
            shape((SLAB // 2, 2 * HEAD_WIDTH), jnp.float32),
            shape((SLAB // 2, 2 * HEAD_WIDTH)),
        ],
        scratch_shapes=[
            pltpu.VMEM((SLAB, Q_COLS), jnp.bfloat16),
            pltpu.VMEM((SLAB, Q_COLS), jnp.bfloat16),
            pltpu.VMEM((SLAB, HEAD_WIDTH), jnp.bfloat16),
            pltpu.VMEM((SLAB, HEAD_WIDTH), jnp.bfloat16),
            pltpu.VMEM((SLAB, 2 * HEAD_WIDTH), jnp.float32),
            pltpu.SMEM((32,), jnp.int32),
            pltpu.SMEM((32,), jnp.int32),
        ],
        compiler_params=params(24),
        cost_estimate=cost(0, 5_000),
    )(doc_ids[0], block_order, got)

    send, got_x, tile_got = lax.optimization_barrier((send, got_x, tile_got))
    taken = lax.ppermute(send, "y", [(0, 1), (1, 0)])
    dq_near, dq_far = pl.pallas_call(
        query_kernel,
        in_specs=[SMEM] * 2 + [VMEM] * 2,
        out_specs=[VMEM] * 2,
        out_shape=[shape((4, Q_COLS, ROWS))] * 2,
        scratch_shapes=[
            pltpu.VMEM((SLAB, Q_COLS), jnp.bfloat16),
            pltpu.SMEM((32,), jnp.int32),
        ],
        compiler_params=params(12),
        cost_estimate=cost(2_000_000_000, 4_000_000),
    )(doc_ids[0], block_order, score_grad, keys_turned)
    dq_far, tile, tile_got = lax.optimization_barrier((dq_far, tile, tile_got))
    tile = widen(tile, tile_got)
    far_tile = swap(tile, 0)
    rows_x = pl.pallas_call(
        rows_kernel,
        in_specs=[VMEM] * 4,
        out_specs=VMEM,
        out_shape=shape((FEAT_TILE, SLAB // 2)),
        compiler_params=params(4),
        cost_estimate=cost(0, 1_300_000),
    )(*got_x)
    taken, dq_near, dq_far, tile, rows_x = lax.optimization_barrier(
        (taken, dq_near, dq_far, tile, rows_x)
    )
    own_cols = pl.pallas_call(
        pair_kernel,
        in_specs=[VMEM] * 2,
        out_specs=VMEM,
        out_shape=shape((SLAB // 2, 2 * HEAD_WIDTH)),
        compiler_params=params(6),
        cost_estimate=cost(0, 2_000_000),
    )(keep, taken)
    pieces = [to_shift(own_cols, s) for s in range(4)]
    _, dq_far = lax.optimization_barrier((own_cols, dq_far))
    dq_got = lax.ppermute(dq_far, "y", [(0, 1), (1, 0)])
    pieces, dq_got, far_tile = lax.optimization_barrier((pieces, dq_got, far_tile))

    kv_half, kv_rows, wg_send, wg_keep = pl.pallas_call(
        weight_kernel,
        in_specs=[VMEM] * 5,
        out_specs=[VMEM] * 4,
        out_shape=[
            shape((SLAB // 2, 1024)),
            shape((ROWS, 1024)),
            shape((FEAT_TILE // 2, 1024)),
            shape((FEAT_TILE // 2, 1024), jnp.float32),
        ],
        compiler_params=params(12),
        cost_estimate=cost(700_000_000, 6_000_000),
    )(*pieces, rows_x)

    wg_got = swap(wg_send, 0)
    parts = pl.pallas_call(
        input_kernel,
        in_specs=[VMEM] * 5,
        out_specs=[VMEM] * 4,
        out_shape=[shape((FEAT_TILE + 2 * Q_COLS, ROWS))] * 4,
        scratch_shapes=[
            pltpu.VMEM((FEAT_TILE, 1024), jnp.bfloat16),
            pltpu.VMEM((4, FEAT_TILE, ROWS), jnp.bfloat16),
        ],
        compiler_params=params(12),
        cost_estimate=cost(700_000_000, 6_000_000),
    )(kv_half, tile, far_tile, dq_near, dq_got)
    wg_got, parts = lax.optimization_barrier((wg_got, parts))
    parts_got = [to_shift(parts[s], s) for s in range(4)]

    def split(number, count, keep, *arrived):
        rows = keep.shape[0] // count
        results = pl.pallas_call(
            functools.partial(split_kernel, number, count),
            in_specs=[VMEM] * (1 + len(arrived)),
            out_specs=[VMEM] * count,
            out_shape=[shape((rows, 1024))] * (count - 1) + [shape((rows, 1024), jnp.float32)],
            scratch_shapes=[pltpu.VMEM((count, rows, 1024), jnp.float32)],
            compiler_params=params(8),
            cost_estimate=cost(0, count * rows * 1024 * 16),
        )(keep, *arrived)
        return results[:-1], results[-1]

    def bit_of(axis, mask):
        return lambda: (lax.axis_index(axis) & mask) // mask

    for axis, mask in (("y", 1), ("z", 1), ("yh", 1), ("z", 2), ("z", 4)):
        sends, wg_keep = split(bit_of(axis, mask), 2, wg_keep, wg_got)
        size = 8 if axis == "z" else 2
        wg_got = lax.ppermute(sends[0], axis, [(i, i ^ mask) for i in range(size)])
    weight_grad = pl.pallas_call(
        add_kernel,
        in_specs=[VMEM] * 2,
        out_specs=VMEM,
        out_shape=shape((10, 1024), jnp.float32),
        compiler_params=params(2),
        cost_estimate=cost(0, 100_000),
    )(wg_keep, wg_got)

    input_grad, query_grad = pl.pallas_call(
        out_kernel,
        in_specs=[VMEM] * 4,
        out_specs=[VMEM] * 2,
        out_shape=[shape((ROWS, FEATURES)), shape((ROWS, HQ * HEAD_WIDTH))],
        compiler_params=params(8),
        cost_estimate=cost(0, 3_300_000),
    )(*parts_got)
    return (input_grad[None], query_grad[None], kv_rows[None], weight_grad)


def solution(mesh):
    axes = ("z", "yh", "core", "y", "x")
    named = jax.sharding.Mesh(mesh.devices.reshape(8, 2, 2, 2, 4), axes)
    fsdp, ctx = axes[:3], axes[3:]
    return jax.shard_map(
        body,
        mesh=named,
        in_specs=(P(fsdp, ctx, None),) * 5 + (P(fsdp, None), P(fsdp, None), P()),
        out_specs=(P(fsdp, ctx, None),) * 3 + (P(axes, None),),
        check_vma=False,
    )
```

```python
import functools
import math

import jax
import jax.numpy as jnp
from jax import lax
from jax.experimental import pallas as pl
from jax.experimental.pallas import tpu as pltpu
from jax.sharding import PartitionSpec as P

HQ = 32
KEY_VALUE_HEADS = 4
HEAD_WIDTH = 128
BLK = 32
QUERY_PER_KEY = 8

CTX = 8
FSDP = 32
ROWS = 128
SLAB = 1024
FEATURES = 2560
FEAT_TILE = FEATURES // 4
Q_COLS = 512
PACK_COLS = 2 * Q_COLS + 2 * HEAD_WIDTH
HALF = 512
SCALE = 1.0 / math.sqrt(HEAD_WIDTH)
LOG2E = math.log2(math.e)
LOWEST = -1e30
NN = (((1,), (0,)), ((), ()))
NT = (((1,), (1,)), ((), ()))
VMEM = pl.BlockSpec(memory_space=pltpu.VMEM)
HBM = pl.BlockSpec(memory_space=pltpu.HBM)
SMEM = pl.BlockSpec(memory_space=pltpu.SMEM)


def dot(a, b, dims):
    return lax.dot_general(a, b, dims, preferred_element_type=jnp.float32)


def shape(dims, kind=jnp.bfloat16):
    return jax.ShapeDtypeStruct(dims, kind)


def params(mib):
    return pltpu.CompilerParams(vmem_limit_bytes=mib * 1024 * 1024)


def cost(flops, moved):
    return pl.CostEstimate(flops=flops, bytes_accessed=moved, transcendentals=0)


def q_block(device):
    return (device % 4) * 2 + device // 4


def pack_kernel(q_ref, d_ref, k_ref, v_ref, out_ref, packed, load_sems, store_sems):
    loads, stores = [], []
    for dest in range(CTX):
        at = q_block(dest) * Q_COLS
        head = (dest % 4) * HEAD_WIDTH
        place = 0
        for ref, first, width in (
            (q_ref, at, Q_COLS),
            (d_ref, at, Q_COLS),
            (k_ref, head, HEAD_WIDTH),
            (v_ref, head, HEAD_WIDTH),
        ):
            load = pltpu.make_async_copy(
                ref.at[:, first : first + width],
                packed.at[dest, :, place : place + width],
                load_sems.at[len(loads)],
            )
            load.start()
            loads.append(load)
            place += width
    for dest in range(CTX):
        for load in loads[4 * dest : 4 * dest + 4]:
            load.wait()
        store = pltpu.make_async_copy(packed.at[dest], out_ref.at[dest], store_sems.at[dest])
        store.start()
        stores.append(store)
    for store in stores:
        store.wait()


def tile_row(z, low, y):
    row = (low % 2) * 320 + y * 160 + (z % 2) * 80
    return row + (low // 2) * 40 + (z // 2 % 2) * 20 + (z // 4) * 10


def turn_kernel(in_ref, *refs):
    outs, turned, tile = refs[:4], refs[4], refs[5]
    for j in range(FEATURES // 128):
        block = in_ref[:, j * 128 : (j + 1) * 128].T
        turned[j * 128 : (j + 1) * 128, :] = block.astype(jnp.float32)
    for x in range(4):
        for low in range(4):
            for y in range(2):
                for z in range(8):
                    source = (z * 4 + low) * 80 + y * 40 + x * 10
                    at = tile_row(z, low, y)
                    tile[x, at : at + 10, :] = turned[source : source + 10, :]
    for s in range(4):
        outs[s][...] = tile[lax.rem(lax.axis_index("x") + s, 4)].astype(jnp.bfloat16)


def place_blocks(docs_ref, order_ref, place):
    first = lax.fori_loop(
        0, 17, lambda i, a: jnp.where(docs_ref[i] == docs_ref[i + 15], i, a), jnp.int32(0)
    )

    def place_block(st, carry):
        b = order_ref[st]
        inside = (b >= first) & (b < first + 16)
        place[st] = jnp.where(inside, b - first, jnp.where(b < first, b + 16, b))
        return carry

    lax.fori_loop(0, 32, place_block, 0)
    return first


def tile_begin(i):
    return 64 * i * (i + 1)


def attention_kernel(docs_ref, order_ref, *refs):
    in_ref, grad_ref, kt_ref, keep_ref, send_ref = refs[:5]
    q_s, d_s, k_s, v_s, dkv_s, place, begin = refs[5:]
    first = place_blocks(docs_ref, order_ref, place)

    def begin_block(t, carry):
        last_doc, last_begin = carry
        doc = docs_ref[jnp.where(t < first, t, t + 16)]
        now = jnp.where(doc == last_doc, last_begin, t)
        begin[t] = jnp.int32(0)
        begin[t + 16] = now * BLK
        return doc, now

    lax.fori_loop(0, 16, begin_block, (jnp.int32(-1), jnp.int32(0)))

    for st in range(32):
        rows = pl.ds(pl.multiple_of(place[st] * BLK, BLK), BLK)
        src, block = st // 4, slice((st % 4) * BLK, (st % 4 + 1) * BLK)
        q_s[rows, :] = in_ref[src, block, 0:Q_COLS]
        d_s[rows, :] = in_ref[src, block, Q_COLS : 2 * Q_COLS]
        k_s[rows, :] = in_ref[src, block, 2 * Q_COLS : 2 * Q_COLS + HEAD_WIDTH]
        v_s[rows, :] = in_ref[src, block, 2 * Q_COLS + HEAD_WIDTH :]
    for j in range(SLAB // 128):
        kt_ref[:, j * 128 : (j + 1) * 128] = k_s[j * 128 : (j + 1) * 128, :].T
    dkv_s[...] = jnp.zeros_like(dkv_s)

    for hf in range(2):
        base = hf * HALF
        for i in range(HALF // 128):
            n = (i + 1) * 128
            rows = pl.ds(base + i * 128, 128)
            keys = pl.ds(base, n)
            key_n = k_s[keys, :]
            value_n = v_s[keys, :]
            masked = 128 if hf == 0 else n
            lane = lax.broadcasted_iota(jnp.int32, (masked, 128), 1)
            row = lax.broadcasted_iota(jnp.int32, (masked, 128), 0) + (n - masked)
            seen = row <= lane + i * 128
            if hf == 1:
                low = jnp.zeros((masked, 128), jnp.int32)
                for kk in range(4):
                    low = jnp.where(lane // BLK == kk, begin[16 + i * 4 + kk], low)
                seen = seen & (row >= low)
            bias = jnp.where(seen, 0.0, LOWEST)
            bias = jnp.concatenate([bias, bias], axis=1)
            q_rows = [q_s[rows, e * 128 : (e + 1) * 128] for e in range(4)]
            d_rows = [d_s[rows, e * 128 : (e + 1) * 128] for e in range(4)]
            grads, lows = [], []
            for g in range(2):
                qs = jnp.concatenate(q_rows[2 * g : 2 * g + 2], axis=0)
                ds = jnp.concatenate(d_rows[2 * g : 2 * g + 2], axis=0)
                scores = dot(key_n, qs, NT) * (SCALE * LOG2E)
                if masked < n:
                    scores = jnp.concatenate(
                        [scores[: n - masked], scores[n - masked :] + bias], axis=0
                    )
                else:
                    scores = scores + bias
                top = jnp.max(scores, axis=0, keepdims=True)
                weights = jnp.exp2(scores - top)
                share = 1.0 / jnp.sum(weights, axis=0, keepdims=True)
                products = dot(value_n, ds, NT)
                delta = jnp.sum(weights * products, axis=0, keepdims=True) * share
                probs = weights * share
                grads.append((probs * (products - delta)).astype(jnp.bfloat16))
                lows.append(probs.astype(jnp.bfloat16))
                grad_ref[hf, g, tile_begin(i) : tile_begin(i) + n, :] = grads[g]
            dkv_s[keys, 0:128] += dot(
                jnp.concatenate(grads, axis=1), jnp.concatenate(q_rows, axis=0), NN
            )
            dkv_s[keys, 128:256] += dot(
                jnp.concatenate(lows, axis=1), jnp.concatenate(d_rows, axis=0), NN
            )

    y = lax.axis_index("y")
    for t in range(16):
        block = slice(t * BLK, (t + 1) * BLK)
        for half_y, ref in ((y, keep_ref), (1 - y, send_ref)):
            rows = pl.ds(pl.multiple_of(place[half_y * 16 + t] * BLK, BLK), BLK)
            ref[block, 0:128] = (dkv_s[rows, 0:128] * SCALE).astype(ref.dtype)
            ref[block, 128:256] = dkv_s[rows, 128:256].astype(ref.dtype)

def query_kernel(docs_ref, order_ref, grad_ref, kt_ref, near_ref, far_ref, dq_s, place):
    place_blocks(docs_ref, order_ref, place)
    for hf in range(2):
        for i in range(HALF // 128):
            n = (i + 1) * 128
            rows = slice(hf * HALF + i * 128, hf * HALF + (i + 1) * 128)
            for g in range(2):
                part = grad_ref[hf, g, tile_begin(i) : tile_begin(i) + n, :]
                dqt = dot(kt_ref[:, hf * HALF : hf * HALF + n], part, NN) * SCALE
                for e in range(2):
                    at = (2 * g + e) * 128
                    block = dqt[:, e * 128 : (e + 1) * 128].T
                    dq_s[rows, at : at + 128] = block.astype(jnp.bfloat16)
    y = lax.axis_index("y")
    for t in range(16):
        for half_y, ref in ((y, near_ref), (1 - y, far_ref)):
            rows = pl.ds(pl.multiple_of(place[half_y * 16 + t] * BLK, BLK), BLK)
            for g in range(4):
                at = g * 128 + (t % 4) * BLK
                ref[t // 4, at : at + BLK, :] = dq_s[rows, g * 128 : (g + 1) * 128]


def pair_kernel(keep_ref, taken_ref, out_ref):
    out_ref[...] = (keep_ref[...] + taken_ref[...].astype(jnp.float32)).astype(jnp.bfloat16)


def rows_kernel(*refs):
    ins, out_ref = refs[:4], refs[4]
    for s in range(4):
        at = pl.multiple_of(lax.rem(lax.axis_index("x") + 4 - s, 4) * 128, 128)
        out_ref[:, pl.ds(at, 128)] = ins[s][...]


KV_SHIFTS = (0, 1, 3, 2)
PART_SHIFTS = (0, 2, 1, 3)


def weight_kernel(*refs):
    pieces, x_s, kv_ref, send_ref = refs[:4], refs[4], refs[5], refs[6]
    for s, piece in zip(KV_SHIFTS, pieces):
        at = pl.multiple_of(lax.rem(lax.axis_index("x") + 4 - s, 4) * 128, 128)
        kv_ref[:, pl.ds(at, 128)] = piece[:, 0:128]
        kv_ref[:, pl.ds(pl.multiple_of(512 + at, 128), 128)] = piece[:, 128:256]
    part = FEAT_TILE // 2
    other = pl.ds(pl.multiple_of((1 - lax.axis_index("core")) * part, part), part)
    for j in range(4):
        cols = slice(j * 256, (j + 1) * 256)
        send_ref[:, cols] = dot(x_s[other, :], kv_ref[:, cols], NN).astype(jnp.bfloat16)


def weight_keep_kernel(x_s, kv_ref, kv_rows_ref, keep_ref):
    part = FEAT_TILE // 2
    own = pl.ds(pl.multiple_of(lax.axis_index("core") * part, part), part)
    for j in range(4):
        cols = slice(j * 256, (j + 1) * 256)
        keep_ref[:, cols] = dot(x_s[own, :], kv_ref[:, cols], NN)
    kv_rows_ref[...] = kv_ref[pl.ds(pl.multiple_of(lax.axis_index("x") * ROWS, ROWS), ROWS), :]


def split_kernel(number, count, *refs):
    count_in = len(refs) - count - 1
    ins, sends, keep_ref, parts = refs[:count_in], refs[count_in:-2], refs[-2], refs[-1]
    total = ins[0][...]
    for ref in ins[1:]:
        total = total + ref[...].astype(jnp.float32)
    rows = keep_ref.shape[0]
    for k in range(count):
        parts[k] = total[k * rows : (k + 1) * rows, :]
    own = number()
    keep_ref[...] = parts[own]
    for k in range(1, count):
        sends[k - 1][...] = parts[own ^ k].astype(jnp.bfloat16)


def add_kernel(keep_ref, got_ref, out_ref):
    out_ref[...] = keep_ref[...] + got_ref[...].astype(jnp.float32)


def holds(z, x, step):
    return z // 2 == x if step == 0 else z // 2 % 2 == x % 2


def take_kernel(step, own_ref, got_ref, out_ref):
    own = holds(lax.axis_index("z"), lax.axis_index("x"), step)
    out_ref[...] = jnp.where(own, own_ref[...], got_ref[...])


def join_kernel(near_ref, far_ref, out_ref):
    n = near_ref.shape[0]
    out_ref[0:n] = near_ref[...]
    out_ref[n:] = far_ref[...]


def input_kernel(kv_ref, w_ref, far_ref, dq_ref, dq_got_ref, *refs):
    outs, w_s, tile = refs[:4], refs[4], refs[5]
    z, yh, core = lax.axis_index("z"), lax.axis_index("yh"), lax.axis_index("core")
    x, y = lax.axis_index("x"), lax.axis_index("y")
    for at in range(8):
        shard = ((z & 1) ^ (at & 1)) * 4 + (yh ^ (at // 2 % 2)) * 2 + (core ^ (at // 4))
        rows = pl.ds(pl.multiple_of(shard * 80, 80), 80)
        w_s[rows, :] = w_ref[at] if at < 4 else far_ref[at - 4]
    for j in range(2):
        rows = slice(j * 256, (j + 1) * 256)
        block = dot(w_s[...], kv_ref[rows, :], NT).astype(jnp.bfloat16)
        tile[2 * j] = block[:, 0:128]
        tile[2 * j + 1] = block[:, 128:256]
    near = pl.multiple_of(FEAT_TILE + y * Q_COLS, 128)
    far = pl.multiple_of(FEAT_TILE + (1 - y) * Q_COLS, 128)
    for s in range(4):
        dest = lax.rem(x + s, 4)
        outs[s][0:FEAT_TILE, :] = tile[dest]
        outs[s][pl.ds(near, Q_COLS), :] = dq_ref[dest]
        outs[s][pl.ds(far, Q_COLS), :] = dq_got_ref[dest]


def out_kernel(*refs):
    parts, input_ref, query_ref = refs[:4], refs[4], refs[5]
    x = lax.axis_index("x")
    for s, part in zip(PART_SHIFTS, parts):
        src = lax.rem(x + 4 - s, 4)
        for j in range(FEAT_TILE // 128):
            cols = pl.ds(pl.multiple_of(src * FEAT_TILE + j * 128, 128), 128)
            input_ref[:, cols] = part[j * 128 : (j + 1) * 128, :].T
        for g in range(8):
            cols = pl.ds(pl.multiple_of(src * 2 * Q_COLS + g * 128, 128), 128)
            at = FEAT_TILE + g * 128
            query_ref[:, cols] = part[at : at + 128, :]


BIT_AXES = (("core", 1), ("yh", 1), ("z", 1), ("z", 2), ("z", 4))


def swap(value, bit):
    axis, mask = BIT_AXES[bit]
    return lax.ppermute(value, axis, [(i, i ^ mask) for i in range(8 if axis == "z" else 2)])


def to_shift(value, s):
    return lax.ppermute(value, "x", [(i, (i + s) % 4) for i in range(4)]) if s else value


def exchange(value, axis):
    return lax.all_to_all(value, axis, 0, 0, tiled=True)


def body(inputs, queries, keys, values, output_cotangent, key_value_weight, doc_ids, block_order):
    packed = pl.pallas_call(
        pack_kernel,
        in_specs=[HBM] * 4,
        out_specs=HBM,
        out_shape=shape((CTX, ROWS, PACK_COLS)),
        scratch_shapes=[
            pltpu.VMEM((CTX, ROWS, PACK_COLS), jnp.bfloat16),
            pltpu.SemaphoreType.DMA((4 * CTX,)),
            pltpu.SemaphoreType.DMA((CTX,)),
        ],
        compiler_params=params(56),
        cost_estimate=cost(0, 5_000_000),
    )(queries[0], output_cotangent[0], keys[0], values[0])
    got = exchange(packed, ("y", "x"))

    _, tile = lax.optimization_barrier((packed, key_value_weight))
    for step in range(2):
        mask = (4, 2)[step]
        pairs = [(z * 4 + x, (z ^ mask) * 4 + x) for z in range(8) for x in range(4) if holds(z, x, step)]
        tile = pl.pallas_call(
            functools.partial(take_kernel, step),
            in_specs=[VMEM] * 2,
            out_specs=VMEM,
            out_shape=shape((80, 1024)),
            compiler_params=params(3),
            cost_estimate=cost(0, 500_000),
        )(tile, lax.ppermute(tile, ("z", "x"), pairs))

    def widen(tile, tile_got):
        n = 2 * tile.shape[0]
        return pl.pallas_call(
            join_kernel,
            in_specs=[VMEM] * 2,
            out_specs=VMEM,
            out_shape=shape((n, 80, 1024)),
            compiler_params=params(4),
            cost_estimate=cost(0, n * 330_000),
        )(tile, tile_got)

    tile = widen(tile[None], swap(tile[None], 2))
    turned = pl.pallas_call(
        turn_kernel,
        in_specs=[VMEM],
        out_specs=[VMEM] * 4,
        out_shape=[shape((FEAT_TILE, ROWS))] * 4,
        scratch_shapes=[
            pltpu.VMEM((FEATURES, ROWS), jnp.float32),
            pltpu.VMEM((4, FEAT_TILE, ROWS), jnp.float32),
        ],
        compiler_params=params(8),
        cost_estimate=cost(0, 1_300_000),
    )(inputs[0])
    got_x = [to_shift(turned[s], s) for s in range(4)]
    tile_got = swap(tile, 1)

    score_grad, keys_turned, keep, send = pl.pallas_call(
        attention_kernel,
        in_specs=[SMEM] * 2 + [VMEM],
        out_specs=[VMEM] * 4,
        out_shape=[
            shape((2, 2, tile_begin(4), 256)),
            shape((HEAD_WIDTH, SLAB)),
            shape((SLAB // 2, 2 * HEAD_WIDTH), jnp.float32),
            shape((SLAB // 2, 2 * HEAD_WIDTH)),
        ],
        scratch_shapes=[
            pltpu.VMEM((SLAB, Q_COLS), jnp.bfloat16),
            pltpu.VMEM((SLAB, Q_COLS), jnp.bfloat16),
            pltpu.VMEM((SLAB, HEAD_WIDTH), jnp.bfloat16),
            pltpu.VMEM((SLAB, HEAD_WIDTH), jnp.bfloat16),
            pltpu.VMEM((SLAB, 2 * HEAD_WIDTH), jnp.float32),
            pltpu.SMEM((32,), jnp.int32),
            pltpu.SMEM((32,), jnp.int32),
        ],
        compiler_params=params(24),
        cost_estimate=cost(0, 5_000),
    )(doc_ids[0], block_order, got)

    send, got_x, tile_got = lax.optimization_barrier((send, got_x, tile_got))
    taken = lax.ppermute(send, "y", [(0, 1), (1, 0)])
    dq_near, dq_far = pl.pallas_call(
        query_kernel,
        in_specs=[SMEM] * 2 + [VMEM] * 2,
        out_specs=[VMEM] * 2,
        out_shape=[shape((4, Q_COLS, ROWS))] * 2,
        scratch_shapes=[
            pltpu.VMEM((SLAB, Q_COLS), jnp.bfloat16),
            pltpu.SMEM((32,), jnp.int32),
        ],
        compiler_params=params(12),
        cost_estimate=cost(2_000_000_000, 4_000_000),
    )(doc_ids[0], block_order, score_grad, keys_turned)
    dq_far, tile, tile_got = lax.optimization_barrier((dq_far, tile, tile_got))
    tile = widen(tile, tile_got)
    far_tile = swap(tile, 0)
    rows_x = pl.pallas_call(
        rows_kernel,
        in_specs=[VMEM] * 4,
        out_specs=VMEM,
        out_shape=shape((FEAT_TILE, SLAB // 2)),
        compiler_params=params(4),
        cost_estimate=cost(0, 1_300_000),
    )(*got_x)
    taken, dq_near, dq_far, tile, rows_x = lax.optimization_barrier(
        (taken, dq_near, dq_far, tile, rows_x)
    )
    own_cols = pl.pallas_call(
        pair_kernel,
        in_specs=[VMEM] * 2,
        out_specs=VMEM,
        out_shape=shape((SLAB // 2, 2 * HEAD_WIDTH)),
        compiler_params=params(6),
        cost_estimate=cost(0, 2_000_000),
    )(keep, taken)
    pieces = [to_shift(own_cols, s) for s in KV_SHIFTS]
    _, dq_far = lax.optimization_barrier((own_cols, dq_far))
    dq_got = lax.ppermute(dq_far, "y", [(0, 1), (1, 0)])
    pieces, dq_got, far_tile = lax.optimization_barrier((pieces, dq_got, far_tile))

    kv_half, wg_send = pl.pallas_call(
        weight_kernel,
        in_specs=[VMEM] * 5,
        out_specs=[VMEM] * 2,
        out_shape=[shape((SLAB // 2, 1024)), shape((FEAT_TILE // 2, 1024))],
        compiler_params=params(12),
        cost_estimate=cost(350_000_000, 4_000_000),
    )(*pieces, rows_x)
    wg_got = swap(wg_send, 0)
    kv_rows, wg_keep = pl.pallas_call(
        weight_keep_kernel,
        in_specs=[VMEM] * 2,
        out_specs=[VMEM] * 2,
        out_shape=[shape((ROWS, 1024)), shape((FEAT_TILE // 2, 1024), jnp.float32)],
        compiler_params=params(12),
        cost_estimate=cost(350_000_000, 4_000_000),
    )(rows_x, kv_half)
    parts = pl.pallas_call(
        input_kernel,
        in_specs=[VMEM] * 5,
        out_specs=[VMEM] * 4,
        out_shape=[shape((FEAT_TILE + 2 * Q_COLS, ROWS))] * 4,
        scratch_shapes=[
            pltpu.VMEM((FEAT_TILE, 1024), jnp.bfloat16),
            pltpu.VMEM((4, FEAT_TILE, ROWS), jnp.bfloat16),
        ],
        compiler_params=params(12),
        cost_estimate=cost(700_000_000, 6_000_000),
    )(kv_half, tile, far_tile, dq_near, dq_got)
    wg_got, parts = lax.optimization_barrier((wg_got, parts))
    parts_got = [to_shift(parts[s], s) for s in PART_SHIFTS]

    def split(number, count, keep, *arrived):
        rows = keep.shape[0] // count
        results = pl.pallas_call(
            functools.partial(split_kernel, number, count),
            in_specs=[VMEM] * (1 + len(arrived)),
            out_specs=[VMEM] * count,
            out_shape=[shape((rows, 1024))] * (count - 1) + [shape((rows, 1024), jnp.float32)],
            scratch_shapes=[pltpu.VMEM((count, rows, 1024), jnp.float32)],
            compiler_params=params(8),
            cost_estimate=cost(0, count * rows * 1024 * 16),
        )(keep, *arrived)
        return results[:-1], results[-1]

    def bit_of(axis, mask):
        return lambda: (lax.axis_index(axis) & mask) // mask

    for axis, mask in (("y", 1), ("z", 1), ("yh", 1), ("z", 2), ("z", 4)):
        sends, wg_keep = split(bit_of(axis, mask), 2, wg_keep, wg_got)
        size = 8 if axis == "z" else 2
        wg_got = lax.ppermute(sends[0], axis, [(i, i ^ mask) for i in range(size)])
    weight_grad = pl.pallas_call(
        add_kernel,
        in_specs=[VMEM] * 2,
        out_specs=VMEM,
        out_shape=shape((10, 1024), jnp.float32),
        compiler_params=params(2),
        cost_estimate=cost(0, 100_000),
    )(wg_keep, wg_got)

    input_grad, query_grad = pl.pallas_call(
        out_kernel,
        in_specs=[VMEM] * 4,
        out_specs=[VMEM] * 2,
        out_shape=[shape((ROWS, FEATURES)), shape((ROWS, HQ * HEAD_WIDTH))],
        compiler_params=params(8),
        cost_estimate=cost(0, 3_300_000),
    )(*parts_got)
    return (input_grad[None], query_grad[None], kv_rows[None], weight_grad)


def solution(mesh):
    axes = ("z", "yh", "core", "y", "x")
    named = jax.sharding.Mesh(mesh.devices.reshape(8, 2, 2, 2, 4), axes)
    fsdp, ctx = axes[:3], axes[3:]
    return jax.shard_map(
        body,
        mesh=named,
        in_specs=(P(fsdp, ctx, None),) * 5 + (P(fsdp, None), P(fsdp, None), P()),
        out_specs=(P(fsdp, ctx, None),) * 3 + (P(axes, None),),
        check_vma=False,
    )
```

```python
import functools
import math

import jax
import jax.numpy as jnp
from jax import lax
from jax.experimental import pallas as pl
from jax.experimental.pallas import tpu as pltpu
from jax.sharding import PartitionSpec as P

HQ = 32
KEY_VALUE_HEADS = 4
HEAD_WIDTH = 128
BLK = 32
QUERY_PER_KEY = 8

CTX = 8
FSDP = 32
ROWS = 128
SLAB = 1024
FEATURES = 2560
FEAT_TILE = FEATURES // 4
Q_COLS = 512
PACK_COLS = 2 * Q_COLS + 2 * HEAD_WIDTH
HALF = 512
SCALE = 1.0 / math.sqrt(HEAD_WIDTH)
LOG2E = math.log2(math.e)
LOWEST = -3e38
NN = (((1,), (0,)), ((), ()))
NT = (((1,), (1,)), ((), ()))
VMEM = pl.BlockSpec(memory_space=pltpu.VMEM)
HBM = pl.BlockSpec(memory_space=pltpu.HBM)
SMEM = pl.BlockSpec(memory_space=pltpu.SMEM)


def dot(a, b, dims):
    return lax.dot_general(a, b, dims, preferred_element_type=jnp.float32)


def shape(dims, kind=jnp.bfloat16):
    return jax.ShapeDtypeStruct(dims, kind)


def params(mib):
    return pltpu.CompilerParams(vmem_limit_bytes=mib * 1024 * 1024)


def cost(flops, moved):
    return pl.CostEstimate(flops=flops, bytes_accessed=moved, transcendentals=0)


def q_block(device):
    return (device % 4) * 2 + device // 4


def pack_kernel(q_ref, d_ref, k_ref, v_ref, out_ref, packed, load_sems, store_sems):
    loads, stores = [], []
    for dest in range(CTX):
        at = q_block(dest) * Q_COLS
        head = (dest % 4) * HEAD_WIDTH
        place = 0
        for ref, first, width in (
            (q_ref, at, Q_COLS),
            (d_ref, at, Q_COLS),
            (k_ref, head, HEAD_WIDTH),
            (v_ref, head, HEAD_WIDTH),
        ):
            load = pltpu.make_async_copy(
                ref.at[:, first : first + width],
                packed.at[dest, :, place : place + width],
                load_sems.at[len(loads)],
            )
            load.start()
            loads.append(load)
            place += width
    for dest in range(CTX):
        for load in loads[4 * dest : 4 * dest + 4]:
            load.wait()
        store = pltpu.make_async_copy(packed.at[dest], out_ref.at[dest], store_sems.at[dest])
        store.start()
        stores.append(store)
    for store in stores:
        store.wait()


def tile_row(z, low, y):
    row = (low % 2) * 320 + y * 160 + (z % 2) * 80
    return row + (low // 2) * 40 + (z // 2 % 2) * 20 + (z // 4) * 10


def turn_kernel(in_ref, *refs):
    outs, turned, tile = refs[:4], refs[4], refs[5]
    for j in range(FEATURES // 128):
        block = in_ref[:, j * 128 : (j + 1) * 128].T
        turned[j * 128 : (j + 1) * 128, :] = block.astype(jnp.float32)
    for x in range(4):
        for low in range(4):
            for y in range(2):
                for z in range(8):
                    source = (z * 4 + low) * 80 + y * 40 + x * 10
                    at = tile_row(z, low, y)
                    tile[x, at : at + 10, :] = turned[source : source + 10, :]
    for s in range(4):
        outs[s][...] = tile[lax.rem(lax.axis_index("x") + s, 4)].astype(jnp.bfloat16)


def place_blocks(docs_ref, order_ref, place):
    first = lax.fori_loop(
        0, 17, lambda i, a: jnp.where(docs_ref[i] == docs_ref[i + 15], i, a), jnp.int32(0)
    )

    def place_block(st, carry):
        b = order_ref[st]
        inside = (b >= first) & (b < first + 16)
        place[st] = jnp.where(inside, b - first, jnp.where(b < first, b + 16, b))
        return carry

    lax.fori_loop(0, 32, place_block, 0)
    return first


def tile_begin(i):
    return 64 * i * (i + 1)


def attention_kernel(docs_ref, order_ref, *refs):
    in_ref, grad_ref, kt_ref, keep_ref, send_ref = refs[:5]
    q_s, d_s, k_s, v_s, dkv_s, place, begin = refs[5:]
    first = place_blocks(docs_ref, order_ref, place)

    def begin_block(t, carry):
        last_doc, last_begin = carry
        doc = docs_ref[jnp.where(t < first, t, t + 16)]
        now = jnp.where(doc == last_doc, last_begin, t)
        begin[t] = jnp.int32(0)
        begin[t + 16] = now * BLK
        return doc, now

    lax.fori_loop(0, 16, begin_block, (jnp.int32(-1), jnp.int32(0)))

    for st in range(32):
        rows = pl.ds(pl.multiple_of(place[st] * BLK, BLK), BLK)
        src, block = st // 4, slice((st % 4) * BLK, (st % 4 + 1) * BLK)
        q_s[rows, :] = in_ref[src, block, 0:Q_COLS]
        d_s[rows, :] = in_ref[src, block, Q_COLS : 2 * Q_COLS]
        k_s[rows, :] = in_ref[src, block, 2 * Q_COLS : 2 * Q_COLS + HEAD_WIDTH]
        v_s[rows, :] = in_ref[src, block, 2 * Q_COLS + HEAD_WIDTH :]
    for j in range(SLAB // 128):
        kt_ref[:, j * 128 : (j + 1) * 128] = k_s[j * 128 : (j + 1) * 128, :].T
    dkv_s[...] = jnp.zeros_like(dkv_s)

    for hf in range(2):
        base = hf * HALF
        for i in range(HALF // 128):
            n = (i + 1) * 128
            rows = pl.ds(base + i * 128, 128)
            keys = pl.ds(base, n)
            key_n = k_s[keys, :]
            value_n = v_s[keys, :]
            masked = 128 if hf == 0 else n
            lane = lax.broadcasted_iota(jnp.int32, (masked, 128), 1)
            row = lax.broadcasted_iota(jnp.int32, (masked, 128), 0) + (n - masked)
            seen = row <= lane + i * 128
            if hf == 1:
                low = jnp.zeros((masked, 128), jnp.int32)
                for kk in range(4):
                    low = jnp.where(lane // BLK == kk, begin[16 + i * 4 + kk], low)
                seen = seen & (row >= low)
            bias = jnp.where(seen, 0.0, LOWEST)
            bias = jnp.concatenate([bias, bias], axis=1)
            q_rows = [q_s[rows, e * 128 : (e + 1) * 128] for e in range(4)]
            d_rows = [d_s[rows, e * 128 : (e + 1) * 128] for e in range(4)]
            grads, lows = [], []
            for g in range(2):
                qs = jnp.concatenate(q_rows[2 * g : 2 * g + 2], axis=0)
                ds = jnp.concatenate(d_rows[2 * g : 2 * g + 2], axis=0)
                scores = dot(key_n, qs, NT) * (SCALE * LOG2E)
                if masked < n:
                    scores = jnp.concatenate(
                        [scores[: n - masked], scores[n - masked :] + bias], axis=0
                    )
                else:
                    scores = scores + bias
                top = jnp.max(scores, axis=0, keepdims=True)
                weights = jnp.exp2(scores - top)
                share = 1.0 / jnp.sum(weights, axis=0, keepdims=True)
                products = dot(value_n, ds, NT)
                delta = jnp.sum(weights * products, axis=0, keepdims=True) * share
                probs = weights * share
                grads.append((probs * (products - delta)).astype(jnp.bfloat16))
                lows.append(probs.astype(jnp.bfloat16))
                grad_ref[hf, g, tile_begin(i) : tile_begin(i) + n, :] = grads[g]
            dkv_s[keys, 0:128] += dot(
                jnp.concatenate(grads, axis=1), jnp.concatenate(q_rows, axis=0), NN
            )
            dkv_s[keys, 128:256] += dot(
                jnp.concatenate(lows, axis=1), jnp.concatenate(d_rows, axis=0), NN
            )

    y = lax.axis_index("y")
    for t in range(16):
        block = slice(t * BLK, (t + 1) * BLK)
        for half_y, ref in ((y, keep_ref), (1 - y, send_ref)):
            rows = pl.ds(pl.multiple_of(place[half_y * 16 + t] * BLK, BLK), BLK)
            ref[block, 0:128] = (dkv_s[rows, 0:128] * SCALE).astype(ref.dtype)
            ref[block, 128:256] = dkv_s[rows, 128:256].astype(ref.dtype)

def query_kernel(docs_ref, order_ref, grad_ref, kt_ref, near_ref, far_ref, dq_s, place):
    place_blocks(docs_ref, order_ref, place)
    for hf in range(2):
        for i in range(HALF // 128):
            n = (i + 1) * 128
            rows = slice(hf * HALF + i * 128, hf * HALF + (i + 1) * 128)
            for g in range(2):
                part = grad_ref[hf, g, tile_begin(i) : tile_begin(i) + n, :]
                dqt = dot(kt_ref[:, hf * HALF : hf * HALF + n], part, NN) * SCALE
                for e in range(2):
                    at = (2 * g + e) * 128
                    block = dqt[:, e * 128 : (e + 1) * 128].T
                    dq_s[rows, at : at + 128] = block.astype(jnp.bfloat16)
    y = lax.axis_index("y")
    for t in range(16):
        for half_y, ref in ((y, near_ref), (1 - y, far_ref)):
            rows = pl.ds(pl.multiple_of(place[half_y * 16 + t] * BLK, BLK), BLK)
            for g in range(4):
                at = g * 128 + (t % 4) * BLK
                ref[t // 4, at : at + BLK, :] = dq_s[rows, g * 128 : (g + 1) * 128]


def pair_kernel(keep_ref, taken_ref, out_ref):
    out_ref[...] = (keep_ref[...] + taken_ref[...].astype(jnp.float32)).astype(jnp.bfloat16)


def rows_kernel(*refs):
    ins, out_ref = refs[:4], refs[4]
    for s in range(4):
        at = pl.multiple_of(lax.rem(lax.axis_index("x") + 4 - s, 4) * 128, 128)
        out_ref[:, pl.ds(at, 128)] = ins[s][...]


KV_SHIFTS = (0, 1, 3, 2)
PART_SHIFTS = (0, 2, 1, 3)


def weight_kernel(*refs):
    pieces, x_s, kv_ref, send_ref = refs[:4], refs[4], refs[5], refs[6]
    for s, piece in zip(KV_SHIFTS, pieces):
        at = pl.multiple_of(lax.rem(lax.axis_index("x") + 4 - s, 4) * 128, 128)
        kv_ref[:, pl.ds(at, 128)] = piece[:, 0:128]
        kv_ref[:, pl.ds(pl.multiple_of(512 + at, 128), 128)] = piece[:, 128:256]
    part = FEAT_TILE // 2
    other = pl.ds(pl.multiple_of((1 - lax.axis_index("core")) * part, part), part)
    for j in range(4):
        cols = slice(j * 256, (j + 1) * 256)
        send_ref[:, cols] = dot(x_s[other, :], kv_ref[:, cols], NN).astype(jnp.bfloat16)


def weight_keep_kernel(x_s, kv_ref, kv_rows_ref, keep_ref):
    part = FEAT_TILE // 2
    own = pl.ds(pl.multiple_of(lax.axis_index("core") * part, part), part)
    for j in range(4):
        cols = slice(j * 256, (j + 1) * 256)
        keep_ref[:, cols] = dot(x_s[own, :], kv_ref[:, cols], NN)
    kv_rows_ref[...] = kv_ref[pl.ds(pl.multiple_of(lax.axis_index("x") * ROWS, ROWS), ROWS), :]


def split_kernel(number, count, *refs):
    count_in = len(refs) - count - 1
    ins, sends, keep_ref, parts = refs[:count_in], refs[count_in:-2], refs[-2], refs[-1]
    total = ins[0][...]
    for ref in ins[1:]:
        total = total + ref[...].astype(jnp.float32)
    rows = keep_ref.shape[0]
    for k in range(count):
        parts[k] = total[k * rows : (k + 1) * rows, :]
    own = number()
    keep_ref[...] = parts[own]
    for k in range(1, count):
        sends[k - 1][...] = parts[own ^ k].astype(jnp.bfloat16)


def add_kernel(keep_ref, got_ref, out_ref):
    out_ref[...] = keep_ref[...] + got_ref[...].astype(jnp.float32)


def holds(z, x, step):
    return z // 2 == x if step == 0 else z // 2 % 2 == x % 2


def take_kernel(step, own_ref, got_ref, out_ref):
    own = holds(lax.axis_index("z"), lax.axis_index("x"), step)
    out_ref[...] = jnp.where(own, own_ref[...], got_ref[...])


def join_kernel(near_ref, far_ref, out_ref):
    n = near_ref.shape[0]
    out_ref[0:n] = near_ref[...]
    out_ref[n:] = far_ref[...]


def input_kernel(kv_ref, w_ref, far_ref, dq_ref, dq_got_ref, *refs):
    outs, w_s, tile = refs[:4], refs[4], refs[5]
    z, yh, core = lax.axis_index("z"), lax.axis_index("yh"), lax.axis_index("core")
    x, y = lax.axis_index("x"), lax.axis_index("y")
    for at in range(8):
        shard = ((z & 1) ^ (at & 1)) * 4 + (yh ^ (at // 2 % 2)) * 2 + (core ^ (at // 4))
        rows = pl.ds(pl.multiple_of(shard * 80, 80), 80)
        w_s[rows, :] = w_ref[at] if at < 4 else far_ref[at - 4]
    for j in range(2):
        rows = slice(j * 256, (j + 1) * 256)
        block = dot(w_s[...], kv_ref[rows, :], NT).astype(jnp.bfloat16)
        tile[2 * j] = block[:, 0:128]
        tile[2 * j + 1] = block[:, 128:256]
    near = pl.multiple_of(FEAT_TILE + y * Q_COLS, 128)
    far = pl.multiple_of(FEAT_TILE + (1 - y) * Q_COLS, 128)
    for s in range(4):
        dest = lax.rem(x + s, 4)
        outs[s][0:FEAT_TILE, :] = tile[dest]
        outs[s][pl.ds(near, Q_COLS), :] = dq_ref[dest]
        outs[s][pl.ds(far, Q_COLS), :] = dq_got_ref[dest]


def out_kernel(*refs):
    parts, input_ref, query_ref = refs[:4], refs[4], refs[5]
    x = lax.axis_index("x")
    for s, part in zip(PART_SHIFTS, parts):
        src = lax.rem(x + 4 - s, 4)
        for j in range(FEAT_TILE // 128):
            cols = pl.ds(pl.multiple_of(src * FEAT_TILE + j * 128, 128), 128)
            input_ref[:, cols] = part[j * 128 : (j + 1) * 128, :].T
        for g in range(8):
            cols = pl.ds(pl.multiple_of(src * 2 * Q_COLS + g * 128, 128), 128)
            at = FEAT_TILE + g * 128
            query_ref[:, cols] = part[at : at + 128, :]


BIT_AXES = (("core", 1), ("yh", 1), ("z", 1), ("z", 2), ("z", 4))


def swap(value, bit):
    axis, mask = BIT_AXES[bit]
    return lax.ppermute(value, axis, [(i, i ^ mask) for i in range(8 if axis == "z" else 2)])


def to_shift(value, s):
    return lax.ppermute(value, "x", [(i, (i + s) % 4) for i in range(4)]) if s else value


def exchange(value, axis):
    return lax.all_to_all(value, axis, 0, 0, tiled=True)


def body(inputs, queries, keys, values, output_cotangent, key_value_weight, doc_ids, block_order):
    packed = pl.pallas_call(
        pack_kernel,
        in_specs=[HBM] * 4,
        out_specs=HBM,
        out_shape=shape((CTX, ROWS, PACK_COLS)),
        scratch_shapes=[
            pltpu.VMEM((CTX, ROWS, PACK_COLS), jnp.bfloat16),
            pltpu.SemaphoreType.DMA((4 * CTX,)),
            pltpu.SemaphoreType.DMA((CTX,)),
        ],
        compiler_params=params(56),
        cost_estimate=cost(0, 5_000_000),
    )(queries[0], output_cotangent[0], keys[0], values[0])
    got = exchange(packed, ("y", "x"))

    _, tile = lax.optimization_barrier((packed, key_value_weight))
    for step in range(2):
        mask = (4, 2)[step]
        pairs = [(z * 4 + x, (z ^ mask) * 4 + x) for z in range(8) for x in range(4) if holds(z, x, step)]
        tile = pl.pallas_call(
            functools.partial(take_kernel, step),
            in_specs=[VMEM] * 2,
            out_specs=VMEM,
            out_shape=shape((80, 1024)),
            compiler_params=params(3),
            cost_estimate=cost(0, 500_000),
        )(tile, lax.ppermute(tile, ("z", "x"), pairs))

    def widen(tile, tile_got):
        n = 2 * tile.shape[0]
        return pl.pallas_call(
            join_kernel,
            in_specs=[VMEM] * 2,
            out_specs=VMEM,
            out_shape=shape((n, 80, 1024)),
            compiler_params=params(4),
            cost_estimate=cost(0, n * 330_000),
        )(tile, tile_got)

    tile = widen(tile[None], swap(tile[None], 2))
    turned = pl.pallas_call(
        turn_kernel,
        in_specs=[VMEM],
        out_specs=[VMEM] * 4,
        out_shape=[shape((FEAT_TILE, ROWS))] * 4,
        scratch_shapes=[
            pltpu.VMEM((FEATURES, ROWS), jnp.float32),
            pltpu.VMEM((4, FEAT_TILE, ROWS), jnp.float32),
        ],
        compiler_params=params(8),
        cost_estimate=cost(0, 1_300_000),
    )(inputs[0])
    got_x = [to_shift(turned[s], s) for s in range(4)]
    tile_got = swap(tile, 1)

    score_grad, keys_turned, keep, send = pl.pallas_call(
        attention_kernel,
        in_specs=[SMEM] * 2 + [VMEM],
        out_specs=[VMEM] * 4,
        out_shape=[
            shape((2, 2, tile_begin(4), 256)),
            shape((HEAD_WIDTH, SLAB)),
            shape((SLAB // 2, 2 * HEAD_WIDTH), jnp.float32),
            shape((SLAB // 2, 2 * HEAD_WIDTH)),
        ],
        scratch_shapes=[
            pltpu.VMEM((SLAB, Q_COLS), jnp.bfloat16),
            pltpu.VMEM((SLAB, Q_COLS), jnp.bfloat16),
            pltpu.VMEM((SLAB, HEAD_WIDTH), jnp.bfloat16),
            pltpu.VMEM((SLAB, HEAD_WIDTH), jnp.bfloat16),
            pltpu.VMEM((SLAB, 2 * HEAD_WIDTH), jnp.float32),
            pltpu.SMEM((32,), jnp.int32),
            pltpu.SMEM((32,), jnp.int32),
        ],
        compiler_params=params(24),
        cost_estimate=cost(0, 5_000),
    )(doc_ids[0], block_order, got)

    send, got_x, tile_got = lax.optimization_barrier((send, got_x, tile_got))
    taken = lax.ppermute(send, "y", [(0, 1), (1, 0)])
    dq_near, dq_far = pl.pallas_call(
        query_kernel,
        in_specs=[SMEM] * 2 + [VMEM] * 2,
        out_specs=[VMEM] * 2,
        out_shape=[shape((4, Q_COLS, ROWS))] * 2,
        scratch_shapes=[
            pltpu.VMEM((SLAB, Q_COLS), jnp.bfloat16),
            pltpu.SMEM((32,), jnp.int32),
        ],
        compiler_params=params(12),
        cost_estimate=cost(2_000_000_000, 4_000_000),
    )(doc_ids[0], block_order, score_grad, keys_turned)
    dq_far, tile, tile_got = lax.optimization_barrier((dq_far, tile, tile_got))
    tile = widen(tile, tile_got)
    far_tile = swap(tile, 0)
    rows_x = pl.pallas_call(
        rows_kernel,
        in_specs=[VMEM] * 4,
        out_specs=VMEM,
        out_shape=shape((FEAT_TILE, SLAB // 2)),
        compiler_params=params(4),
        cost_estimate=cost(0, 1_300_000),
    )(*got_x)
    taken, dq_near, dq_far, tile, rows_x = lax.optimization_barrier(
        (taken, dq_near, dq_far, tile, rows_x)
    )
    own_cols = pl.pallas_call(
        pair_kernel,
        in_specs=[VMEM] * 2,
        out_specs=VMEM,
        out_shape=shape((SLAB // 2, 2 * HEAD_WIDTH)),
        compiler_params=params(6),
        cost_estimate=cost(0, 2_000_000),
    )(keep, taken)
    pieces = [to_shift(own_cols, s) for s in KV_SHIFTS]
    _, dq_far = lax.optimization_barrier((own_cols, dq_far))
    dq_got = lax.ppermute(dq_far, "y", [(0, 1), (1, 0)])
    pieces, dq_got, far_tile = lax.optimization_barrier((pieces, dq_got, far_tile))

    kv_half, wg_send = pl.pallas_call(
        weight_kernel,
        in_specs=[VMEM] * 5,
        out_specs=[VMEM] * 2,
        out_shape=[shape((SLAB // 2, 1024)), shape((FEAT_TILE // 2, 1024))],
        compiler_params=params(12),
        cost_estimate=cost(350_000_000, 4_000_000),
    )(*pieces, rows_x)
    wg_got = swap(wg_send, 0)
    kv_rows, wg_keep = pl.pallas_call(
        weight_keep_kernel,
        in_specs=[VMEM] * 2,
        out_specs=[VMEM] * 2,
        out_shape=[shape((ROWS, 1024)), shape((FEAT_TILE // 2, 1024), jnp.float32)],
        compiler_params=params(12),
        cost_estimate=cost(350_000_000, 4_000_000),
    )(rows_x, kv_half)
    parts = pl.pallas_call(
        input_kernel,
        in_specs=[VMEM] * 5,
        out_specs=[VMEM] * 4,
        out_shape=[shape((FEAT_TILE + 2 * Q_COLS, ROWS))] * 4,
        scratch_shapes=[
            pltpu.VMEM((FEAT_TILE, 1024), jnp.bfloat16),
            pltpu.VMEM((4, FEAT_TILE, ROWS), jnp.bfloat16),
        ],
        compiler_params=params(12),
        cost_estimate=cost(700_000_000, 6_000_000),
    )(kv_half, tile, far_tile, dq_near, dq_got)
    wg_got, parts = lax.optimization_barrier((wg_got, parts))
    parts_got = [to_shift(parts[s], s) for s in PART_SHIFTS]

    def split(number, count, keep, *arrived):
        rows = keep.shape[0] // count
        results = pl.pallas_call(
            functools.partial(split_kernel, number, count),
            in_specs=[VMEM] * (1 + len(arrived)),
            out_specs=[VMEM] * count,
            out_shape=[shape((rows, 1024))] * (count - 1) + [shape((rows, 1024), jnp.float32)],
            scratch_shapes=[pltpu.VMEM((count, rows, 1024), jnp.float32)],
            compiler_params=params(8),
            cost_estimate=cost(0, count * rows * 1024 * 16),
        )(keep, *arrived)
        return results[:-1], results[-1]

    def bit_of(axis, mask):
        return lambda: (lax.axis_index(axis) & mask) // mask

    for axis, mask in (("y", 1), ("z", 1), ("yh", 1), ("z", 2), ("z", 4)):
        sends, wg_keep = split(bit_of(axis, mask), 2, wg_keep, wg_got)
        size = 8 if axis == "z" else 2
        wg_got = lax.ppermute(sends[0], axis, [(i, i ^ mask) for i in range(size)])
    weight_grad = pl.pallas_call(
        add_kernel,
        in_specs=[VMEM] * 2,
        out_specs=VMEM,
        out_shape=shape((10, 1024), jnp.float32),
        compiler_params=params(2),
        cost_estimate=cost(0, 100_000),
    )(wg_keep, wg_got)

    input_grad, query_grad = pl.pallas_call(
        out_kernel,
        in_specs=[VMEM] * 4,
        out_specs=[VMEM] * 2,
        out_shape=[shape((ROWS, FEATURES)), shape((ROWS, HQ * HEAD_WIDTH))],
        compiler_params=params(8),
        cost_estimate=cost(0, 3_300_000),
    )(*parts_got)
    return (input_grad[None], query_grad[None], kv_rows[None], weight_grad)


def solution(mesh):
    axes = ("z", "yh", "core", "y", "x")
    named = jax.sharding.Mesh(mesh.devices.reshape(8, 2, 2, 2, 4), axes)
    fsdp, ctx = axes[:3], axes[3:]
    return jax.shard_map(
        body,
        mesh=named,
        in_specs=(P(fsdp, ctx, None),) * 5 + (P(fsdp, None), P(fsdp, None), P()),
        out_specs=(P(fsdp, ctx, None),) * 3 + (P(axes, None),),
        check_vma=False,
    )
```
